32 devices in a mesh: blk: 16 (over z, y, core), grp: 2 (over x).
Axes of the slice: x: 2, y: 2, z: 4, core: 2. Of those that a mesh axis runs over, the one named last changes fastest.
Arguments:
- dual_rhs: float32 [2, 16, 16384], P('grp', None, 'blk'), may hold values from -32 to 32
- dual_ops: bfloat16 [2, 16384, 1024], P('grp', 'blk'), may hold values from -1 to 6, as said below
- prec_ops: bfloat16 [2, 16384, 1024], P('grp', 'blk'), may hold values from -1 to 4, as said below
- corner_coupling: bfloat16 [2, 384, 512], P('grp', 'blk'), may hold values from -0.25 to 0.25
- corner_map: int32 [2, 384], P('grp', 'blk'), may hold values from 0 to 767
- signs: int32 [2, 16384], P('grp', 'blk'), may hold values from -1 to 1, as said below
- coarse_inverse: float32 [768, 768], replicated, may hold values from -1 to 5, as said below
Outputs:
- multipliers: float32 [2, 16, 16384], P('grp', None, 'blk')
- residual: float32 [2, 16, 16384], P('grp', None, 'blk')
The draws below stay inside these ranges and needn't reach their ends.
Inputs may be any that keep to these rules, and one draw needn't show every extreme that they name: `dual_ops`: each subdomain's 1024 x 1024 block is symmetric positive definite. `prec_ops`: each subdomain's 1024 x 1024 block is symmetric positive definite. `signs`: every entry is 1 or -1; the lower face of each subdomain after the first of a group carries the negated signs of the upper face of the subdomain before it. `coarse_inverse`: symmetric positive definite.
All inputs are finite; a program needn't handle non-finite values.
Results may differ from the reference program's by a relative error of at most 0.003.
Values sent between devices are 32-bit elements; how exact they have to be, the bound alone decides.
No kernel may reach another device: no remote copies, remote signals or barrier semaphores. Data moves between devices by JAX's collectives and lax.ppermute only.
A program may use at most 64 MiB of HBM per device.

```python
import math
import jax
import jax.numpy as jnp
from jax import lax

M = 1024
HALF = 512
NRHS = 16
NCG = 768
NC = 12
ITERS = 2
N_BLK = 16
N_GRP = 2


def symmetric_blocks(key, spread, low_diag, high_diag):

    def single(index):
        subkey = jax.random.fold_in(key, index)
        noise_key, diag_key = jax.random.split(subkey)
        noise = jax.random.truncated_normal(noise_key, -6.0, 6.0, (M, M), jnp.float32)
        mixed = (noise + noise.T) * (spread / math.sqrt(2.0 * M))
        diagonal = jnp.exp(jax.random.uniform(diag_key, (M,), jnp.float32, math.log(low_diag), math.log(high_diag)))
        return (mixed + jnp.diag(diagonal)).astype(jnp.bfloat16)
    blocks = lax.map(single, jnp.arange(N_GRP * N_BLK, dtype=jnp.int32))
    return blocks.reshape(N_GRP, N_BLK * M, M)


def draw_dual_ops(key, part):
    own_key = jax.random.fold_in(key, 11)
    return symmetric_blocks(own_key, 0.5, 1.5, 4.0)


def draw_prec_ops(key, part):
    own_key = jax.random.fold_in(key, 23)
    return symmetric_blocks(own_key, 0.3, 0.8, 2.5)


def draw_dual_rhs(key, part):
    own_key = jax.random.fold_in(key, 37)
    base_key = jax.random.fold_in(own_key, 0)
    columns = N_BLK * M
    position = jnp.arange(columns, dtype=jnp.float32) / (columns - 1)
    base = jax.random.truncated_normal(base_key, -4.0, 4.0, (N_GRP, NRHS, columns), jnp.float32)
    rising = jnp.exp(math.log(3.0) * position)
    return base * rising[None, None, :]


def draw_signs(key, part):
    own_key = jax.random.fold_in(key, 41)
    faces = 2 * N_BLK
    base = jax.random.randint(own_key, (N_GRP, faces, HALF), 0, 2, dtype=jnp.int32) * 2 - 1
    previous = jnp.roll(base, 1, axis=1)
    face_index = jnp.arange(faces, dtype=jnp.int32)[None, :, None]
    take_previous = (face_index % 2 == 0) & (face_index > 0)
    joined = jnp.where(take_previous, -previous, base)
    return joined.reshape(N_GRP, N_BLK * M).astype(jnp.int32)


def draw_coarse_inverse(key, part):
    own_key = jax.random.fold_in(key, 53)
    noise_key, diag_key = jax.random.split(own_key)
    noise = jax.random.truncated_normal(noise_key, -6.0, 6.0, (NCG, NCG), jnp.float32)
    mixed = (noise + noise.T) * (0.4 / math.sqrt(2.0 * NCG))
    diagonal = jnp.exp(jax.random.uniform(diag_key, (NCG,), jnp.float32, 0.0, math.log(3.0)))
    return mixed + jnp.diag(diagonal)


def touch_ends(array, key, least, high):
    longest = array.shape.index(max(array.shape))
    spots = []
    for shift in (0, 1):
        where = [jax.random.randint(jax.random.fold_in(key, axis), (), 0, length) for axis, length in enumerate(array.shape)]
        where[longest] = (where[longest] + shift) % array.shape[longest]
        spots.append(tuple(where))
    return array.at[spots[0]].set(least).at[spots[1]].set(high)


def levels(rng, extent, cuts, least, high):
    def one(axis_at, parts):
        steps = jax.random.uniform(jax.random.fold_in(jax.random.fold_in(rng, 6), axis_at), (parts,), jnp.float32, least / len(cuts), high / len(cuts))
        return jnp.repeat(jnp.exp(steps), extent[axis_at] // parts).reshape((-1,) + (1,) * (len(extent) - axis_at - 1))

    gain = one(*cuts[0])
    for cut in cuts[1:]:
        gain = gain * one(*cut)
    return gain


def gaussian(key, dims, scale, limit, shards=(), kind=jnp.bfloat16):
    array = jax.random.normal(key, dims, jnp.float32) * scale
    if len(shards) > 0:
        array = levels(key, dims, shards, -0.22, 0.18) * array
    return jnp.clip(array, min=-limit, max=limit).astype(kind)


def setup_inputs(seed: int = 0) -> dict:
    streams_of = jax.random.split(jax.random.key(seed), 8)
    return {
        "dual_rhs": draw_dual_rhs(jax.random.fold_in(streams_of[7], 71), 0),
        "dual_ops": draw_dual_ops(jax.random.fold_in(streams_of[7], 71), 0),
        "prec_ops": draw_prec_ops(jax.random.fold_in(streams_of[7], 71), 0),
        "corner_coupling": gaussian(streams_of[3], (N_GRP, N_BLK * 2 * NC, HALF), HALF ** -0.5, 0.25, ((0, 2), (1, 16))),
        "corner_map": touch_ends(jax.random.randint(streams_of[4], (N_GRP, N_BLK * 2 * NC), 0, NCG), jax.random.fold_in(streams_of[4], 1), 0, NCG - 1).astype(jnp.int32),
        "signs": draw_signs(jax.random.fold_in(streams_of[7], 71), 0),
        "coarse_inverse": draw_coarse_inverse(jax.random.fold_in(streams_of[7], 71), 0),
    }


def gram_solve(matrix, target):
    balanced = 0.5 * (matrix + matrix.T)
    factor = jnp.linalg.cholesky(balanced)
    middle = lax.linalg.triangular_solve(factor, target, left_side=True, lower=True)
    return lax.linalg.triangular_solve(factor, middle, left_side=True, lower=True, transpose_a=True)

def per_subdomain(operands):
    vector, block = operands
    return jnp.dot(vector.astype(jnp.float32), block.T.astype(jnp.float32), preferred_element_type=jnp.float32)

def reference(dual_rhs, dual_ops, prec_ops, corner_coupling, corner_map, signs, coarse_inverse):
    highest = lax.Precision.HIGHEST
    faces = 2 * N_BLK
    face_index = jnp.arange(faces, dtype=jnp.int32)
    live_face = ((face_index > 0) & (face_index < faces - 1)).astype(jnp.float32)
    even_face = face_index % 2 == 0
    face_sign = signs.reshape(N_GRP, faces, HALF).astype(jnp.float32) * live_face[None, :, None]
    couple = corner_coupling.reshape(N_GRP, faces, NC, HALF).astype(jnp.float32)
    corner_index = corner_map.reshape(N_GRP, faces, NC)
    dual_blocks = dual_ops.reshape(N_GRP * N_BLK, M, M)
    prec_blocks = prec_ops.reshape(N_GRP * N_BLK, M, M)

    def operate(values, blocks, coarse):
        signed_in = face_sign[:, None] * values
        rounded = signed_in.astype(jnp.bfloat16).reshape(N_GRP, NRHS, N_BLK, M)
        ordered = jnp.transpose(rounded, (0, 2, 1, 3)).reshape(N_GRP * N_BLK, NRHS, M)
        products = lax.map(per_subdomain, (ordered, blocks))
        local_out = jnp.transpose(products.reshape(N_GRP, N_BLK, NRHS, M), (0, 2, 1, 3)).reshape(N_GRP, NRHS, faces, HALF)
        if coarse:
            partial_value = jnp.einsum('grbh,gbch->gbcr', signed_in, couple, precision=highest)
            corner_sum = jax.ops.segment_sum(partial_value.reshape(-1, NRHS), corner_index.reshape(-1), num_segments=NCG)
            solved = jnp.dot(coarse_inverse, corner_sum, precision=highest)
            picked = solved[corner_index]
            local_out = local_out + jnp.einsum('gbcr,gbch->grbh', picked, couple, precision=highest)
        signed_out = face_sign[:, None] * local_out
        padding = jnp.zeros_like(signed_out[:, :, :1])
        from_left = jnp.concatenate([padding, signed_out[:, :, :-1]], axis=2)
        from_right = jnp.concatenate([signed_out[:, :, 1:], padding], axis=2)
        partner = jnp.where(even_face[None, None, :, None], from_left, from_right)
        return live_face[None, None, :, None] * (signed_out + partner)

    def inner(first, second):
        return jnp.einsum('grbh,gsbh->rs', first, second, precision=highest)

    def combine(weights, values):
        return jnp.einsum('rs,grbh->gsbh', weights, values, precision=highest)
    residual = live_face[None, None, :, None] * dual_rhs.reshape(N_GRP, NRHS, faces, HALF)
    multipliers = jnp.zeros_like(residual)
    precond = operate(residual, prec_blocks, False)
    gram_old = inner(residual, precond)
    direction = precond
    for iteration in range(ITERS):
        image_dir = operate(direction, dual_blocks, True)
        step_alpha = gram_solve(inner(direction, image_dir), gram_old)
        multipliers = multipliers + combine(step_alpha, direction)
        residual = residual - combine(step_alpha, image_dir)
        if iteration + 1 < ITERS:
            precond = operate(residual, prec_blocks, False)
            gram_new = inner(residual, precond)
            step_beta = gram_solve(gram_old, gram_new)
            direction = precond + combine(step_beta, direction)
            gram_old = gram_new
    return (multipliers.reshape(N_GRP, NRHS, N_BLK * M), residual.reshape(N_GRP, NRHS, N_BLK * M))
```

```python
import functools
import jax
import jax.numpy as jnp
from jax import lax
from jax.sharding import PartitionSpec as P

ITERS = 2
AXES = ("blk", "grp")
HIGHEST = lax.Precision.HIGHEST
NT = (((1,), (1,)), ((), ()))
TN = (((0,), (0,)), ((), ()))


def radices(count):
    found = []
    factor = 2
    while count > 1:
        while count % factor == 0:
            found.append(factor)
            count //= factor
        factor += 1
    return found


def swap(count, groups, partner):
    pairs = []
    for blk in range(count):
        for grp in range(groups):
            other = partner(blk)
            if 0 <= other < count:
                target = other * groups + grp
            elif grp ^ 1 < groups:
                target = blk * groups + (grp ^ 1)
            else:
                target = blk * groups + grp
            pairs.append((blk * groups + grp, target))
    return pairs


def inner_pairs(count, groups):
    return swap(count, groups, lambda blk: blk ^ 1)


def outer_pairs(count, groups):
    return swap(count, groups, lambda blk: blk + 1 if blk % 2 == 1 else blk - 1)


def rotations(count, groups):
    core = 2 if count % 2 == 0 else 1
    steps = []

    def flipped(blk, turn):
        return (blk ^ 1) if (core == 2 and turn) else blk

    def add_axis(step_target, factor):
        steps.append(
            [
                [
                    (blk * groups + grp, step_target(blk, grp, turn))
                    for blk in range(count)
                    for grp in range(groups)
                ]
                for turn in range(1, factor)
            ]
        )

    stride = 1
    blk_steps = []
    for factor in radices(count // core):
        blk_steps.append((stride, factor))
        stride *= factor
    grp_steps = []
    stride = 1
    for factor in radices(groups):
        grp_steps.append((stride, factor))
        stride *= factor

    def blk_target(stride, factor):
        def target(blk, grp, turn):
            chip = blk // core
            digit = (chip // stride) % factor
            moved = chip + ((digit + turn) % factor - digit) * stride
            return flipped(moved * core + blk % core, turn) * groups + grp

        return target

    def grp_target(stride, factor):
        def target(blk, grp, turn):
            digit = (grp // stride) % factor
            moved = grp + ((digit + turn) % factor - digit) * stride
            return flipped(blk, turn) * groups + moved

        return target

    for stride, factor in blk_steps[:1]:
        add_axis(blk_target(stride, factor), factor)
    for stride, factor in grp_steps:
        add_axis(grp_target(stride, factor), factor)
    for stride, factor in blk_steps[1:]:
        add_axis(blk_target(stride, factor), factor)
    return steps


def gram_solve(matrix, target):
    balanced = 0.5 * (matrix + matrix.T)
    factor = jnp.linalg.cholesky(balanced)
    middle = lax.linalg.triangular_solve(factor, target, left_side=True, lower=True)
    return lax.linalg.triangular_solve(factor, middle, left_side=True, lower=True, transpose_a=True)


def local(count, groups, dual_rhs, dual_ops, prec_ops, corner_coupling, corner_map, signs, coarse_inverse):
    nrhs, width = dual_rhs.shape[1:]
    half = width // 2
    corners = coarse_inverse.shape[0]
    blk = lax.axis_index("blk")
    even = blk % 2 == 0
    lower_live = jnp.where(blk > 0, 1.0, 0.0).astype(jnp.float32)
    upper_live = jnp.where(blk < count - 1, 1.0, 0.0).astype(jnp.float32)
    live = jnp.concatenate(
        [
            jnp.full((1, half), 1.0, jnp.float32) * lower_live,
            jnp.full((1, half), 1.0, jnp.float32) * upper_live,
        ],
        axis=1,
    )
    sign = signs.astype(jnp.float32) * live
    slots = corner_coupling.shape[1] // 2
    faces = corner_coupling[0].astype(jnp.float32).reshape(2, slots, half)
    maps = corner_map.astype(jnp.float32).reshape(2, slots)
    inner, outer = inner_pairs(count, groups), outer_pairs(count, groups)
    steps = rotations(count, groups)

    def split(low, up):
        return jnp.where(even, up, low), jnp.where(even, low, up)

    def joined(from_inner, from_outer):
        return jnp.where(even, from_outer, from_inner), jnp.where(even, from_inner, from_outer)

    def permute(values, pairs):
        return lax.ppermute(values, AXES, pairs)

    def region(values, low, up):
        to_inner, to_outer = split(low, up)
        from_outer = permute(to_outer, outer)
        lanes = values.shape[1]
        got = permute(jnp.concatenate([values, to_inner], axis=1), inner)
        values, from_inner = values + got[:, :lanes], got[:, lanes:]
        for turns in steps:
            values = values + sum(permute(values, pairs) for pairs in turns)
        return values, *joined(from_inner, from_outer)

    def beside(values):
        to_inner, to_outer = split(values[:, :half], values[:, half:])
        from_outer = permute(to_outer, outer)
        return jnp.concatenate(joined(permute(to_inner, inner), from_outer), axis=1)

    def block_product(values, blocks):
        return lax.dot_general(
            values.astype(jnp.bfloat16), blocks[0], NT, preferred_element_type=jnp.float32
        )

    def dots(first, second):
        return lax.dot_general(first, second, NT, precision=HIGHEST)

    def combine(weights, values):
        return lax.dot_general(weights, values, TN, precision=HIGHEST)

    def onehot_of(rows):
        index = jnp.arange(corners, dtype=jnp.int32)[None, :].astype(jnp.float32)
        return (rows.reshape(-1)[:, None] == index).astype(jnp.float32)

    onehot = onehot_of(maps)

    def corner_part(values):
        low = dots(values[:, :half], faces[0])
        up = dots(values[:, half:], faces[1])
        return jnp.dot(jnp.concatenate([low, up], axis=1), onehot, precision=HIGHEST)

    def spread(solved, chosen, blocks):
        picked = dots(solved, chosen)
        return jnp.concatenate(
            [
                jnp.dot(picked[:, :slots], blocks[0], precision=HIGHEST),
                jnp.dot(picked[:, slots:], blocks[1], precision=HIGHEST),
            ],
            axis=1,
        )

    def extras(face):
        map_row = jnp.pad(maps[face][None], ((0, 0), (0, half - slots)))
        fill = jnp.zeros((nrhs - slots - 1, half), jnp.float32)
        return jnp.concatenate([faces[face], map_row, fill], axis=0)

    residual = sign * dual_rhs[0]
    product = block_product(residual, prec_ops)
    precond = live * (product - beside(product))
    image_local = block_product(precond, dual_ops)
    grams = jnp.concatenate([dots(residual, precond), dots(precond, image_local)], axis=1)
    payload = jnp.concatenate([corner_part(precond), grams], axis=1)
    payload = jnp.pad(payload, ((0, 0), (0, -payload.shape[1] % 128)))
    summed, low, up = region(
        payload,
        jnp.concatenate([image_local[:, :half], extras(0)], axis=1),
        jnp.concatenate([image_local[:, half:], extras(1)], axis=1),
    )
    image_beside = jnp.concatenate([low[:, :half], up[:, :half]], axis=1)
    faces_beside = (low[:slots, half:], up[:slots, half:])
    onehot_beside = onehot_of(jnp.stack([low[slots, half : half + slots], up[slots, half : half + slots]]))
    corner_sum = summed[:, :corners]
    gram_old = summed[:, corners : corners + nrhs]
    solved = dots(corner_sum, coarse_inverse)
    energy = 2.0 * (summed[:, corners + nrhs : corners + 2 * nrhs] + dots(corner_sum, solved))
    alpha = gram_solve(energy, gram_old)
    image_part = live * (image_local - image_beside)
    image = image_part + live * (
        spread(solved, onehot, faces) - spread(solved, onehot_beside, faces_beside)
    )
    multipliers = combine(alpha, precond)
    residual = residual - combine(alpha, image)
    direction, image_dir_part = precond, image_part
    energy_local = summed[:, corners + nrhs : corners + 2 * nrhs]

    product = block_product(residual, prec_ops)
    precond = live * (product - beside(product))
    new_local = block_product(precond, dual_ops)
    grams = jnp.concatenate(
        [
            dots(residual, precond),
            dots(precond, new_local),
            dots(direction, new_local) + dots(image_local, precond),
        ],
        axis=1,
    )
    payload = jnp.concatenate([corner_part(precond), grams], axis=1)
    payload = jnp.pad(payload, ((0, 0), (0, -payload.shape[1] % 128)))
    summed, low, up = region(payload, new_local[:, :half], new_local[:, half:])
    gram_new = summed[:, corners : corners + nrhs]
    new_new = summed[:, corners + nrhs : corners + 2 * nrhs]
    old_new = summed[:, corners + 2 * nrhs : corners + 3 * nrhs]
    beta = gram_solve(gram_old, gram_new)
    corner_sum = summed[:, :corners] + combine(beta, corner_sum)
    solved = dots(corner_sum, coarse_inverse)
    energy = 2.0 * (
        new_new
        + combine(beta, old_new)
        + combine(beta, jnp.dot(energy_local, beta, precision=HIGHEST))
        + dots(corner_sum, solved)
    )
    alpha = gram_solve(energy, gram_new)
    direction = precond + combine(beta, direction)
    image = (
        live * (new_local - jnp.concatenate([low, up], axis=1))
        + combine(beta, image_dir_part)
        + live * (spread(solved, onehot, faces) - spread(solved, onehot_beside, faces_beside))
    )
    multipliers = multipliers + combine(alpha, direction)
    residual = residual - combine(alpha, image)
    return (sign * multipliers)[None], (sign * residual)[None]


def solution(mesh):
    in_specs = (
        P("grp", None, "blk"),
        P("grp", "blk", None),
        P("grp", "blk", None),
        P("grp", "blk", None),
        P("grp", "blk"),
        P("grp", "blk"),
        P(),
    )
    out_specs = (P("grp", None, "blk"), P("grp", None, "blk"))
    return jax.shard_map(
        functools.partial(local, mesh.shape["blk"], mesh.shape["grp"]),
        mesh=mesh,
        in_specs=in_specs,
        out_specs=out_specs,
        check_vma=False,
    )
```

```python
import functools

import jax
import jax.numpy as jnp
from jax import lax
from jax.experimental import pallas as pl
from jax.experimental.pallas import tpu as pltpu
from jax.sharding import PartitionSpec as P

AXES = ("blk", "grp")
NN = (((1,), (0,)), ((), ()))
NT = (((1,), (1,)), ((), ()))
TN = (((0,), (0,)), ((), ()))
F32 = jnp.float32
BF16 = jnp.bfloat16


def radices(count):
    found = []
    factor = 2
    while count > 1:
        while count % factor == 0:
            found.append(factor)
            count //= factor
        factor += 1
    return found


def swap(count, groups, partner):
    pairs = []
    for blk in range(count):
        for grp in range(groups):
            other = partner(blk)
            if 0 <= other < count:
                target = other * groups + grp
            elif grp ^ 1 < groups:
                target = blk * groups + (grp ^ 1)
            else:
                target = blk * groups + grp
            pairs.append((blk * groups + grp, target))
    return pairs


def inner_pairs(count, groups):
    return swap(count, groups, lambda blk: blk ^ 1)


def outer_pairs(count, groups):
    return swap(count, groups, lambda blk: blk + 1 if blk % 2 == 1 else blk - 1)


def rotations(count, groups):
    core = 2 if count % 2 == 0 else 1
    steps = []

    def flipped(blk, turn):
        return (blk ^ 1) if (core == 2 and turn) else blk

    def add_axis(step_target, factor):
        steps.append(
            [
                [
                    (blk * groups + grp, step_target(blk, grp, turn))
                    for blk in range(count)
                    for grp in range(groups)
                ]
                for turn in range(1, factor)
            ]
        )

    stride = 1
    blk_steps = []
    for factor in radices(count // core):
        blk_steps.append((stride, factor))
        stride *= factor
    grp_steps = []
    stride = 1
    for factor in radices(groups):
        grp_steps.append((stride, factor))
        stride *= factor

    def blk_target(stride, factor):
        def target(blk, grp, turn):
            chip = blk // core
            digit = (chip // stride) % factor
            moved = chip + ((digit + turn) % factor - digit) * stride
            return flipped(moved * core + blk % core, turn) * groups + grp

        return target

    def grp_target(stride, factor):
        def target(blk, grp, turn):
            digit = (grp // stride) % factor
            moved = grp + ((digit + turn) % factor - digit) * stride
            return flipped(blk, turn) * groups + moved

        return target

    for stride, factor in blk_steps[:1]:
        add_axis(blk_target(stride, factor), factor)
    for stride, factor in grp_steps:
        add_axis(grp_target(stride, factor), factor)
    for stride, factor in blk_steps[1:]:
        add_axis(blk_target(stride, factor), factor)
    return steps


def mm(first, second, dims):
    return lax.dot_general(first, second, dims, preferred_element_type=F32)


def halves(values):
    high = values.astype(BF16)
    return high, (values - high.astype(F32)).astype(BF16)


def stacked(values):
    return jnp.concatenate(halves(values), axis=0)


def folded(rows):
    count = rows.shape[0] // 2
    return rows[:count] + rows[count:]


def dots(first, second):
    product = folded(mm(stacked(first), stacked(second), NT))
    count = second.shape[0]
    return product[:, :count] + product[:, count:]


def combine(weights, values):
    weight_high, weight_low = halves(weights)
    high, low = halves(values)
    left = jnp.concatenate([weight_high, weight_high, weight_low, weight_low], axis=0)
    right = jnp.concatenate([high, low, high, low], axis=0)
    return mm(left, right, TN)


def against(values, exact):
    return folded(mm(stacked(values), exact, NN))


def lanes_of(shape):
    return lax.broadcasted_iota(jnp.int32, shape, len(shape) - 1)


def chosen(row, corners):
    shape = (corners, row.shape[1])
    return (lax.broadcasted_iota(jnp.int32, shape, 0) == row).astype(BF16)


def live_mask(blk, count, width):
    lane = lanes_of((1, width))
    low = (blk > 0).astype(F32)
    up = (blk < count - 1).astype(F32)
    return jnp.where(lane < width // 2, low, up)


def split(even, low, up):
    return jnp.where(even, up, low), jnp.where(even, low, up)


def joined(even, from_inner, from_outer):
    low = jnp.where(even, from_outer, from_inner)
    up = jnp.where(even, from_inner, from_outer)
    return jnp.concatenate([low, up], axis=1)


def transposed(matrix):
    return matrix.T


def eliminate(matrix, target):
    count = matrix.shape[0]
    work = jnp.concatenate([matrix, target], axis=1)
    row_index = lax.broadcasted_iota(jnp.int32, (count, 1), 0)
    for step in range(count):
        row = work[step : step + 1, :]
        scaled = row * (1.0 / work[step : step + 1, step : step + 1])
        column = work[:, step : step + 1]
        work = jnp.where(row_index == step, scaled, work - column * scaled)
    return work[:, count:]


def symmetric(matrix):
    return 0.5 * (matrix + transposed(matrix))


def corner_values(values, couple, own_choice):
    half = values.shape[1] // 2
    both = stacked(values)
    low = folded(mm(both[:, :half], couple, NT))
    up = folded(mm(both[:, half:], couple, NT))
    mine = jnp.where(lanes_of(low.shape) < couple.shape[0] // 2, low, up)
    return folded(mm(stacked(mine), own_choice, NT))


def coarse_spread(solved, couple, own_row, beside):
    corners = solved.shape[1]
    slots = couple.shape[0] // 2
    half = couple.shape[1]
    both = stacked(solved)
    picked = folded(mm(both, chosen(own_row, corners), NN))
    lane = lanes_of(picked.shape)
    low = jnp.where(lane < slots, picked, 0.0)
    up = jnp.where(lane < slots, 0.0, picked)
    own_low = against(low, couple)
    own_up = against(up, couple)
    others = []
    for face in (beside[:, :half], beside[:, half:]):
        row = face[slots : slots + 1, : face.shape[0]]
        valid = lanes_of(row.shape) < slots
        choice = chosen(jnp.where(valid, row, -1.0).astype(jnp.int32), corners)
        others.append(against(folded(mm(both, choice, NN)), face.astype(BF16)))
    return jnp.concatenate([own_low - others[0], own_up - others[1]], axis=1)


def coarse_solve(corner_sum, parts):
    high, low = parts
    first = folded(mm(stacked(corner_sum), high, NN))
    return first + mm(corner_sum.astype(BF16), low, NN)


def start_kernel(count, rhs, signs, blocks, product, to_inner, to_outer, held, sems):
    rows = held.shape[1]
    copies = [
        pltpu.make_async_copy(blocks.at[0, pl.ds(part * rows, rows)], held.at[part], sems.at[part])
        for part in range(held.shape[0])
    ]
    for copy in copies:
        copy.start()
    blk = lax.axis_index("blk")
    width = rhs.shape[2]
    sign = signs[...].astype(F32) * live_mask(blk, count, width)
    rounded = (sign * rhs[0]).astype(BF16)
    total = jnp.zeros((rhs.shape[1], width), F32)
    for part, copy in enumerate(copies):
        copy.wait()
        total = total + mm(rounded[:, part * rows : (part + 1) * rows], held[part], NN)
    product[...] = total
    inner, outer = split(blk % 2 == 0, total[:, : width // 2], total[:, width // 2 :])
    to_inner[...] = inner
    to_outer[...] = outer


def first_kernel(
    count, corners, product, from_inner, from_outer, rhs, signs, blocks, coupling, corner_map,
    precond_out, image_out, to_inner, to_outer,
):
    blk = lax.axis_index("blk")
    even = blk % 2 == 0
    nrhs, width = product.shape
    half = width // 2
    live = live_mask(blk, count, width)
    residual = signs[...].astype(F32) * live * rhs[0]
    precond = live * (product[...] - joined(even, from_inner[...], from_outer[...]))
    image = mm(precond.astype(BF16), blocks[0], NN)
    precond_out[...] = precond
    image_out[...] = image
    couple = coupling[0]
    slots = couple.shape[0] // 2
    lanes = to_inner.shape[1] - width
    to_inner[:, :corners] = corner_values(precond, couple, chosen(corner_map[...], corners))
    grams = dots(jnp.concatenate([residual, precond], axis=0), jnp.concatenate([precond, image], axis=0))
    to_inner[:, corners:lanes] = jnp.concatenate(
        [grams[:nrhs, :nrhs], grams[nrhs:, nrhs:], jnp.zeros((nrhs, lanes - corners - 2 * nrhs), F32)], axis=1
    )
    inner, outer = split(even, image[:, :half], image[:, half:])
    to_inner[:, lanes : lanes + half] = inner
    to_outer[:, :half] = outer
    wide = couple.astype(F32)
    row = jnp.concatenate([corner_map[...].astype(F32), jnp.zeros((1, half - 2 * slots), F32)], axis=1)
    low, up = wide[:slots], wide[slots:]
    low_row, up_row = row, pltpu.roll(row, half - slots, 1)
    fill = jnp.zeros((nrhs - slots - 1, half), F32)
    inner, outer = split(
        even,
        jnp.concatenate([low, low_row, fill], axis=0),
        jnp.concatenate([up, up_row, fill], axis=0),
    )
    to_inner[:, lanes + half :] = inner
    to_outer[:, half:] = outer


def prepare_kernel(coarse, high, low):
    top, rest = halves(coarse[...])
    high[...] = top
    low[...] = rest


def middle_kernel(
    count, corners, summed_a, summed_b, got, from_outer, precond, image, rhs, signs, blocks, coupling, corner_map,
    coarse_high, coarse_low,
    sums_out, solved_out, residual_out, image_out, product_out, small_out, beside_out, to_inner, to_outer,
):
    blk = lax.axis_index("blk")
    even = blk % 2 == 0
    nrhs, width = precond.shape
    half = width // 2
    live = live_mask(blk, count, width)
    lanes = summed_a.shape[1]
    summed = summed_a[...] + summed_b[...]
    corner_sum = summed[:, :corners]
    gram = summed[:, corners : corners + nrhs]
    local_energy = summed[:, corners + nrhs : corners + 2 * nrhs]
    solved = coarse_solve(corner_sum, (coarse_high[...], coarse_low[...]))
    energy = local_energy + dots(corner_sum, solved)
    alpha = eliminate(symmetric(2.0 * energy), gram)
    inner_got = got[:, lanes:]
    outer_got = from_outer[...]
    image_beside = joined(even, inner_got[:, :half], outer_got[:, :half])
    beside = joined(even, inner_got[:, half:], outer_got[:, half:])
    whole = live * (
        image[...] - image_beside + coarse_spread(solved, coupling[0], corner_map[...], beside)
    )
    residual = signs[...].astype(F32) * live * rhs[0] - combine(alpha, whole)
    product = mm(residual.astype(BF16), blocks[0], NN)
    inner, outer = split(even, product[:, :half], product[:, half:])
    to_inner[...] = inner
    to_outer[...] = outer
    sums_out[...] = corner_sum
    solved_out[...] = solved
    residual_out[...] = residual
    image_out[...] = whole
    product_out[...] = product
    small_out[...] = jnp.concatenate([gram, energy, alpha, jnp.zeros((nrhs, 128 - 3 * nrhs), F32)], axis=1)
    beside_out[...] = beside


def invert_kernel(small, inverse):
    nrhs = small.shape[0]
    row = lax.broadcasted_iota(jnp.int32, (nrhs, nrhs), 0)
    unit = (row == lanes_of((nrhs, nrhs))).astype(F32)
    inverse[...] = eliminate(symmetric(small[:, :nrhs]), unit)


def second_kernel(
    count, corners, product, from_inner, from_outer, residual, old_precond, old_image, blocks, coupling, corner_map,
    precond_out, image_out, to_inner, to_outer,
):
    blk = lax.axis_index("blk")
    even = blk % 2 == 0
    nrhs, width = product.shape
    half = width // 2
    live = live_mask(blk, count, width)
    precond = live * (product[...] - joined(even, from_inner[...], from_outer[...]))
    image = mm(precond.astype(BF16), blocks[0], NN)
    precond_out[...] = precond
    image_out[...] = image
    inner, outer = split(even, image[:, :half], image[:, half:])
    lanes = to_inner.shape[1] - half
    to_inner[:, lanes:] = inner
    to_outer[...] = outer
    to_inner[:, :corners] = corner_values(precond, coupling[0], chosen(corner_map[...], corners))
    left = jnp.concatenate([residual[...], precond, old_precond[...], old_image[...]], axis=0)
    grams = dots(left, jnp.concatenate([precond, image], axis=0))
    to_inner[:, corners:lanes] = jnp.concatenate(
        [
            grams[:nrhs, :nrhs],
            grams[nrhs : 2 * nrhs, nrhs:],
            grams[2 * nrhs : 3 * nrhs, nrhs:] + grams[3 * nrhs :, :nrhs],
            jnp.zeros((nrhs, lanes - corners - 3 * nrhs), F32),
        ],
        axis=1,
    )


def final_kernel(
    count, corners, summed_a, summed_b, got, from_outer, precond, image, residual, old_precond, old_image, old_sums,
    old_solved, small, inverse, beside, signs, coupling, corner_map, coarse_high, coarse_low,
    multipliers_out, residual_out,
):
    blk = lax.axis_index("blk")
    even = blk % 2 == 0
    nrhs, width = precond.shape
    live = live_mask(blk, count, width)
    lanes = summed_a.shape[1]
    summed = summed_a[...] + summed_b[...]
    corner_sum = summed[:, :corners]
    gram = summed[:, corners : corners + nrhs]
    new_new = summed[:, corners + nrhs : corners + 2 * nrhs]
    old_new = summed[:, corners + 2 * nrhs : corners + 3 * nrhs]
    beta = combine(inverse[...], gram)
    solved = coarse_solve(corner_sum, (coarse_high[...], coarse_low[...]))
    cross = dots(
        jnp.concatenate([corner_sum, old_sums[...]], axis=0),
        jnp.concatenate([solved, old_solved[...]], axis=0),
    )
    new_new = new_new + cross[:nrhs, :nrhs]
    old_new = old_new + cross[nrhs:, :nrhs] + transposed(cross[:nrhs, nrhs:])
    old_old = symmetric(small[:, nrhs : 2 * nrhs])
    energy = new_new + combine(beta, old_new + combine(old_old, beta))
    alpha = eliminate(symmetric(2.0 * energy), gram)
    image_beside = joined(even, got[:, lanes:], from_outer[...])
    whole = live * (
        image[...] - image_beside + coarse_spread(solved, coupling[0], corner_map[...], beside[...])
    )
    carried = combine(transposed(beta), alpha)
    sign = signs[...].astype(F32) * live
    first = small[:, 2 * nrhs : 3 * nrhs]
    weights = jnp.concatenate([alpha, carried + first], axis=0)
    multipliers_out[0] = sign * combine(weights, jnp.concatenate([precond[...], old_precond[...]], axis=0))
    weights = jnp.concatenate([alpha, carried], axis=0)
    change = combine(weights, jnp.concatenate([whole, old_image[...]], axis=0))
    residual_out[0] = sign * (residual[...] - change)


VMEM = pl.BlockSpec(memory_space=pltpu.VMEM)
ANY = pl.BlockSpec(memory_space=pl.ANY)


def call(body, shapes, *args, specs=None, scratch=(), flops=0):
    shapes = [jax.ShapeDtypeStruct(shape, dtype) for shape, dtype in shapes]
    moved = sum(arg.size * arg.dtype.itemsize for arg in args)
    return pl.pallas_call(
        body,
        out_shape=shapes,
        in_specs=specs or [VMEM] * len(args),
        out_specs=[VMEM] * len(shapes),
        scratch_shapes=list(scratch),
        compiler_params=pltpu.CompilerParams(vmem_limit_bytes=16 << 20),
        cost_estimate=pl.CostEstimate(flops=flops, bytes_accessed=moved, transcendentals=0),
    )(*args)


def local(count, groups, dual_rhs, dual_ops, prec_ops, corner_coupling, corner_map, signs, coarse_inverse):
    nrhs, width = dual_rhs.shape[1:]
    half = width // 2
    corners = coarse_inverse.shape[0]
    inner, outer = inner_pairs(count, groups), outer_pairs(count, groups)
    steps = rotations(count, groups)
    lanes = corners + 128 * ((3 * nrhs + 127) // 128)
    flops = 2 * nrhs * width * width

    def permute(values, pairs):
        return lax.ppermute(values, AXES, pairs)

    def region(to_inner):
        got = permute(to_inner, inner)
        values = to_inner[:, :lanes] + got[:, :lanes]
        parts = [values]
        for turns in steps:
            values = sum(parts[1:], parts[0])
            parts = [values] + [permute(values, pairs) for pairs in turns]
        return sum(parts[1:-1], parts[0]), parts[-1], got

    wide = ((nrhs, width), F32)
    face = ((nrhs, half), F32)
    pieces = 4
    product, to_inner, to_outer = call(
        functools.partial(start_kernel, count),
        [wide, face, face],
        dual_rhs, signs, prec_ops,
        specs=[VMEM, VMEM, ANY],
        scratch=[pltpu.VMEM((pieces, width // pieces, width), BF16), pltpu.SemaphoreType.DMA((pieces,))],
        flops=flops,
    )
    from_outer = permute(to_outer, outer)
    from_inner = permute(to_inner, inner)
    precond0, image0, to_inner, to_outer = call(
        functools.partial(first_kernel, count, corners),
        [wide, wide, ((nrhs, lanes + width), F32), wide],
        product, from_inner, from_outer, dual_rhs, signs, dual_ops, corner_coupling, corner_map,
        flops=flops,
    )
    square = ((corners, corners), BF16)
    coarse_parts = call(prepare_kernel, [square, square], coarse_inverse, flops=corners * corners)
    from_outer = permute(to_outer, outer)
    left, right, got = region(to_inner)
    sums0, solved0, residual1, whole0, product, small, beside, to_inner, to_outer = call(
        functools.partial(middle_kernel, count, corners),
        [
            ((nrhs, corners), F32), ((nrhs, corners), F32), wide, wide, wide, ((nrhs, 128), F32), wide, face, face,
        ],
        left, right, got, from_outer, precond0, image0, dual_rhs, signs, prec_ops, corner_coupling, corner_map,
        *coarse_parts,
        flops=flops,
    )
    from_outer = permute(to_outer, outer)
    from_inner = permute(to_inner, inner)
    (inverse,) = call(invert_kernel, [((nrhs, nrhs), F32)], small, flops=nrhs**3)
    precond1, image1, to_inner, to_outer = call(
        functools.partial(second_kernel, count, corners),
        [wide, wide, ((nrhs, lanes + half), F32), face],
        product, from_inner, from_outer, residual1, precond0, image0, dual_ops, corner_coupling, corner_map,
        flops=flops,
    )
    from_outer = permute(to_outer, outer)
    left, right, got = region(to_inner)
    whole_out = ((1, nrhs, width), F32)
    return tuple(
        call(
            functools.partial(final_kernel, count, corners),
            [whole_out, whole_out],
            left, right, got, from_outer, precond1, image1, residual1, precond0, whole0, sums0, solved0, small,
            inverse, beside, signs, corner_coupling, corner_map, *coarse_parts,
            flops=flops,
        )
    )


def solution(mesh):
    in_specs = (
        P("grp", None, "blk"),
        P("grp", "blk", None),
        P("grp", "blk", None),
        P("grp", "blk", None),
        P("grp", "blk"),
        P("grp", "blk"),
        P(),
    )
    out_specs = (P("grp", None, "blk"), P("grp", None, "blk"))
    return jax.shard_map(
        functools.partial(local, mesh.shape["blk"], mesh.shape["grp"]),
        mesh=mesh,
        in_specs=in_specs,
        out_specs=out_specs,
        check_vma=False,
    )
```

```python
import functools

import jax
import jax.numpy as jnp
from jax import lax
from jax.experimental import pallas as pl
from jax.experimental.pallas import tpu as pltpu
from jax.sharding import PartitionSpec as P

AXES = ("blk", "grp")
NN = (((1,), (0,)), ((), ()))
NT = (((1,), (1,)), ((), ()))
TN = (((0,), (0,)), ((), ()))
F32 = jnp.float32
BF16 = jnp.bfloat16


def radices(count):
    found = []
    factor = 2
    while count > 1:
        while count % factor == 0:
            found.append(factor)
            count //= factor
        factor += 1
    return found


def swap(count, groups, partner):
    pairs = []
    for blk in range(count):
        for grp in range(groups):
            other = partner(blk)
            if 0 <= other < count:
                target = other * groups + grp
            elif grp ^ 1 < groups:
                target = blk * groups + (grp ^ 1)
            else:
                target = blk * groups + grp
            pairs.append((blk * groups + grp, target))
    return pairs


def inner_pairs(count, groups):
    return swap(count, groups, lambda blk: blk ^ 1)


def outer_pairs(count, groups):
    return swap(count, groups, lambda blk: blk + 1 if blk % 2 == 1 else blk - 1)


def rotations(count, groups):
    core = 2 if count % 2 == 0 else 1
    steps = []

    def flipped(blk, turn):
        return (blk ^ 1) if (core == 2 and turn) else blk

    def add_axis(step_target, factor):
        steps.append(
            [
                [
                    (blk * groups + grp, step_target(blk, grp, turn))
                    for blk in range(count)
                    for grp in range(groups)
                ]
                for turn in range(1, factor)
            ]
        )

    stride = 1
    blk_steps = []
    for factor in radices(count // core):
        blk_steps.append((stride, factor))
        stride *= factor
    grp_steps = []
    stride = 1
    for factor in radices(groups):
        grp_steps.append((stride, factor))
        stride *= factor

    def blk_target(stride, factor):
        def target(blk, grp, turn):
            chip = blk // core
            digit = (chip // stride) % factor
            moved = chip + ((digit + turn) % factor - digit) * stride
            return flipped(moved * core + blk % core, turn) * groups + grp

        return target

    def grp_target(stride, factor):
        def target(blk, grp, turn):
            digit = (grp // stride) % factor
            moved = grp + ((digit + turn) % factor - digit) * stride
            return flipped(blk, turn) * groups + moved

        return target

    for stride, factor in blk_steps[1:]:
        add_axis(blk_target(stride, factor), factor)
    for stride, factor in grp_steps:
        add_axis(grp_target(stride, factor), factor)
    for stride, factor in blk_steps[:1]:
        add_axis(blk_target(stride, factor), factor)
    return steps


def mm(first, second, dims):
    return lax.dot_general(first, second, dims, preferred_element_type=F32)


def halves(values):
    high = values.astype(BF16)
    return high, (values - high.astype(F32)).astype(BF16)


def stacked(values):
    return jnp.concatenate(halves(values), axis=0)


def folded(rows):
    count = rows.shape[0] // 2
    return rows[:count] + rows[count:]


def dots(first, second):
    product = folded(mm(stacked(first), stacked(second), NT))
    count = second.shape[0]
    return product[:, :count] + product[:, count:]


def combine(weights, values):
    weight_high, weight_low = halves(weights)
    high, low = halves(values)
    left = jnp.concatenate([weight_high, weight_high, weight_low, weight_low], axis=0)
    right = jnp.concatenate([high, low, high, low], axis=0)
    return mm(left, right, TN)


def against(values, exact):
    return folded(mm(stacked(values), exact, NN))


def lanes_of(shape):
    return lax.broadcasted_iota(jnp.int32, shape, len(shape) - 1)


def chosen(row, corners):
    shape = (corners, row.shape[1])
    return (lax.broadcasted_iota(jnp.int32, shape, 0) == row).astype(BF16)


def live_mask(blk, count, width):
    lane = lanes_of((1, width))
    low = (blk > 0).astype(F32)
    up = (blk < count - 1).astype(F32)
    return jnp.where(lane < width // 2, low, up)


def split(even, low, up):
    return jnp.where(even, up, low), jnp.where(even, low, up)


def joined(even, from_inner, from_outer):
    low = jnp.where(even, from_outer, from_inner)
    up = jnp.where(even, from_inner, from_outer)
    return jnp.concatenate([low, up], axis=1)


def transposed(matrix):
    return matrix.T


def eliminate(matrix, target):
    count = matrix.shape[1]
    row_index = lax.broadcasted_iota(jnp.int32, (1, count, 1), 1)
    column_index = lax.broadcasted_iota(jnp.int32, (1, count, count), 2)
    diagonal = jnp.where(row_index == column_index, matrix, 0.0)
    scale = lax.rsqrt(jnp.sum(diagonal, axis=2, keepdims=True))
    matrix = matrix * lax.rsqrt(jnp.sum(diagonal, axis=1, keepdims=True))
    work = jnp.concatenate([matrix, target], axis=2) * scale
    size = 4
    for start in range(0, count, size):
        at = [start + index for index in range(size)]
        columns = [jnp.broadcast_to(work[:, :, k : k + 1], work.shape) for k in at]
        pivot = [[column[:, k : k + 1] for column in columns] for k in at]
        rows = [work[:, k : k + 1] for k in at]
        for one in range(0, size, 2):
            two = one + 1
            a, b, c, d = pivot[one][one], pivot[one][two], pivot[two][one], pivot[two][two]
            inverse = 1.0 / (a * d - b * c)
            for j in range(two + 1, size):
                p, q = pivot[one][j], pivot[two][j]
                pivot[one][j], pivot[two][j] = (d * p - b * q) * inverse, (a * q - c * p) * inverse
            p, q = rows[one], rows[two]
            rows[one], rows[two] = (d * p - b * q) * inverse, (a * q - c * p) * inverse
            for i in range(size):
                if i not in (one, two):
                    left, right = pivot[i][one], pivot[i][two]
                    for j in range(two + 1, size):
                        pivot[i][j] = pivot[i][j] - left * pivot[one][j] - right * pivot[two][j]
                    rows[i] = rows[i] - left * rows[one] - right * rows[two]
        products = [column * row for column, row in zip(columns, rows)]
        work = work - ((products[0] + products[1]) + (products[2] + products[3]))
        for k, row in zip(at, rows):
            work = jnp.where(row_index == k, row, work)
    return work[:, :, count:] * scale


def symmetric(matrix):
    return 0.5 * (matrix + transposed(matrix))


def corner_values(values, couple):
    half = values.shape[1] // 2
    both = stacked(values)
    low = folded(mm(both[:, :half], couple, NT))
    up = folded(mm(both[:, half:], couple, NT))
    return jnp.where(lanes_of(low.shape) < couple.shape[0] // 2, low, up)


TILE = 128
GROUP = 32
MOST = 32


def abreast(rows):
    half = rows.shape[0] // 2
    return [rows[:half], rows[half:]]


def tile_of(corner, middle, first, second):
    shared = jnp.concatenate(abreast(corner) + middle + abreast(first), axis=1)
    return jnp.concatenate([jnp.concatenate([shared, part], axis=1) for part in abreast(second)], axis=0)


def merged(own, got, even, lane):
    rows = lax.broadcasted_iota(jnp.int32, own.shape, 0)
    mine = (rows < own.shape[0] // 2) == even
    taken, other = jnp.where(mine, own, got), jnp.where(mine, got, own)
    return taken + jnp.where(lanes_of(own.shape) < lane, 0.0, other)


def untile(tiles, slots):
    half = tiles.shape[0] // 2
    count = 2 * half
    even, odd = tiles[:half], tiles[half:]
    both = even + odd
    start = 2 * slots
    last = start + 4 * count
    squares = [
        jnp.concatenate([both[:, at : at + count], both[:, at + count : at + 2 * count]], axis=0)
        for at in (start, start + 2 * count)
    ]
    return *squares, jnp.concatenate([even[:, last : last + count], odd[:, last : last + count]], axis=0)


def dense(tiles, maps, slots, corners):
    count = tiles.shape[0] // 8
    lane = lanes_of((1, TILE))
    low, up, index = [], [], []
    totals = [jnp.zeros((8, TILE), F32)] * 2
    for start in range(0, count, TILE // GROUP):
        parts = [jnp.zeros((8, TILE), F32), jnp.zeros((8, TILE), F32), jnp.full((1, TILE), -1.0, F32)]
        for turn, at in enumerate(range(start, min(start + TILE // GROUP, count))):
            tile, name = tiles[8 * at : 8 * at + 8], maps[8 * at : 8 * at + 1]
            totals[at % 2] = totals[at % 2] + tile
            here = (lane // GROUP == turn) & (lane % GROUP < slots)
            shift = GROUP * turn
            moved = [
                pltpu.roll(tile, shift, 1) if shift else tile,
                pltpu.roll(tile, (shift - slots) % TILE, 1),
                pltpu.roll(name, (shift - 2 * slots) % TILE, 1),
            ]
            parts = [jnp.where(here, new, old) for new, old in zip(moved, parts)]
        low.append(parts[0])
        up.append(parts[1])
        index.append(parts[2])
    values = jnp.concatenate([jnp.concatenate(low, axis=1), jnp.concatenate(up, axis=1)], axis=0)
    choice = chosen(jnp.concatenate(index, axis=1).astype(jnp.int32), corners)
    corner_sum = folded(mm(stacked(values), choice, NT))
    return jnp.concatenate([corner_sum, jnp.concatenate(totals, axis=0)], axis=1)


def dense_kernel(slots, corners, tiles, maps, out):
    out[...] = dense(tiles[...], maps[...], slots, corners)


def total_of(left, right, maps, slots, corners):
    if right.shape[1] == TILE:
        return left[...] + dense(right[...], maps[...], slots, corners)
    return left[...] + right[...]


def face_rows(rows):
    low = lax.broadcasted_iota(jnp.int32, rows.shape, 0) < rows.shape[0] // 2
    return jnp.concatenate([jnp.where(low, rows, 0.0), jnp.where(low, 0.0, rows)], axis=1)


def picked(solved, row):
    return folded(mm(stacked(solved), chosen(row.astype(jnp.int32), solved.shape[1]), NN))


def product_of(first, second):
    high, low = halves(second)
    return folded(mm(stacked(first), high, NN)) + mm(first.astype(BF16), low, NN)


def coarse_solve(corner_sum, parts):
    high, low = parts
    first = folded(mm(stacked(corner_sum), high, NN))
    return first + mm(corner_sum.astype(BF16), low, NN)


def start_kernel(
    count, rhs, signs, blocks, coupling, corner_map,
    product, to_inner, to_outer, residual_out, sign_out, couple_out, map_out, inner_extra, outer_extra, held,
    rhs_held, signs_held, coupling_held, map_held, sems,
):
    rows = held.shape[1]
    pieces = [(rhs, rhs_held), (signs, signs_held)]
    pieces += [(blocks.at[0, pl.ds(part * rows, rows)], held.at[part]) for part in range(held.shape[0])]
    pieces += [(corner_map, map_held), (coupling, coupling_held)]
    copies = [pltpu.make_async_copy(*piece, sems.at[index]) for index, piece in enumerate(pieces)]
    for copy in copies:
        copy.start()
    blk = lax.axis_index("blk")
    even = blk % 2 == 0
    nrhs, width = product.shape
    half = width // 2
    live = live_mask(blk, count, width)
    copies[0].wait()
    copies[1].wait()
    sign = signs_held[...].astype(F32) * live
    residual = sign * rhs_held[0]
    rounded = residual.astype(BF16)
    sign_out[...] = sign
    residual_out[...] = residual
    total = jnp.zeros((nrhs, width), F32)
    for part, copy in enumerate(copies[2:-2]):
        copy.wait()
        total = total + mm(rounded[:, part * rows : (part + 1) * rows], held[part], NN)
    product[...] = total
    inner, outer = split(even, total[:, :half], total[:, half:])
    to_inner[...] = inner
    to_outer[...] = outer
    copies[-2].wait()
    copies[-1].wait()
    couple = coupling_held[0]
    couple_out[...] = couple
    slots = couple.shape[0] // 2
    wide = couple.astype(F32)
    row = jnp.concatenate([map_held[...].astype(F32), jnp.zeros((1, half - 2 * slots), F32)], axis=1)
    map_out[...] = row[:, : map_out.shape[1]]
    fill = jnp.zeros((nrhs - slots - 1, half), F32)
    inner, outer = split(
        even,
        jnp.concatenate([wide[:slots], row, fill], axis=0),
        jnp.concatenate([wide[slots:], pltpu.roll(row, half - slots, 1), fill], axis=0),
    )
    inner_extra[...] = inner
    outer_extra[...] = outer


def first_kernel(
    count, product, from_inner, from_outer, residual, blocks, couple, map_row, inner_extra, outer_extra,
    precond_out, image_out, tile_out, to_inner, to_outer,
):
    blk = lax.axis_index("blk")
    even = blk % 2 == 0
    nrhs, width = product.shape
    half = width // 2
    live = live_mask(blk, count, width)
    precond = live * (product[...] - joined(even, from_inner[...], from_outer[...]))
    image = mm(precond.astype(BF16), blocks[...], NN)
    precond_out[...] = precond
    image_out[...] = image
    grams = dots(
        jnp.concatenate([residual[...], precond], axis=0), jnp.concatenate([precond, image], axis=0)
    )
    slots = couple.shape[0]
    middle = jnp.concatenate([map_row[:, :slots], jnp.zeros((1, 2 * nrhs - slots), F32)], axis=1)
    middle = jnp.broadcast_to(middle, (nrhs // 2, 2 * nrhs))
    tile = tile_of(corner_values(precond, couple[...]), [middle], grams[:nrhs, :nrhs], grams[nrhs:, nrhs:])
    tile_out[...] = tile
    inner, outer = split(even, image[:, :half], image[:, half:])
    to_inner[:, :half] = inner
    to_outer[:, :half] = outer
    to_inner[:, half:width] = inner_extra[...]
    to_outer[:, half:] = outer_extra[...]
    to_inner[:, width:] = tile


def load_kernel(blocks, after, out, sems):
    del after
    rows = out.shape[0] // sems.shape[0]
    copies = [
        pltpu.make_async_copy(
            blocks.at[0, pl.ds(part * rows, rows)], out.at[pl.ds(part * rows, rows)], sems.at[part]
        )
        for part in range(sems.shape[0])
    ]
    for copy in copies:
        copy.start()
    for copy in copies:
        copy.wait()


def prepare_kernel(coarse, high, low):
    top, rest = halves(coarse[...])
    high[...] = top
    low[...] = rest


def follow_kernel(
    count, image, got, from_outer, couple, map_row, blocks,
    part_out, product_out, spread_out, columns_out, map_out, to_inner, to_outer,
):
    blk = lax.axis_index("blk")
    even = blk % 2 == 0
    nrhs, width = image.shape
    half = width // 2
    live = live_mask(blk, count, width)
    inner_got = got[...]
    outer_got = from_outer[...]
    part = live * (image[...] - joined(even, inner_got[:, :half], outer_got[:, :half]))
    beside = joined(even, inner_got[:, half:width], outer_got[:, half:])
    wide = couple[...].astype(F32)
    slots = wide.shape[0] // 2
    other = jnp.concatenate([beside[:slots, :half], beside[:slots, half:]], axis=0)
    columns = (live * jnp.concatenate([face_rows(wide), -face_rows(other)], axis=0)).astype(BF16)
    products = mm(jnp.concatenate([stacked(part), columns], axis=0), blocks[...].reshape(width, width), NN)
    product = products[:nrhs] + products[nrhs : 2 * nrhs]
    spread = products[2 * nrhs :]
    row = jnp.concatenate(
        [
            map_row[:, : 2 * slots],
            beside[slots : slots + 1, :slots],
            beside[slots : slots + 1, half : half + slots],
            jnp.full((1, map_row.shape[1] - 4 * slots), -1.0, F32),
        ],
        axis=1,
    )
    part_out[...] = part
    product_out[...] = product
    spread_out[...] = spread
    columns_out[...] = columns
    map_out[...] = row
    count_rows = nrhs + 4 * slots
    rows = jnp.concatenate([product, spread], axis=0)
    to_inner[:count_rows, :], to_outer[:count_rows, :] = split(even, rows[:, :half], rows[:, half:])
    last = jnp.concatenate([row, jnp.zeros((1, half - row.shape[1]), F32)], axis=1)
    last = jnp.broadcast_to(last, (to_inner.shape[0] - count_rows, half))
    to_inner[count_rows:, :] = last
    to_outer[count_rows:, :] = last


def middle_kernel(
    count, corners, left, right, maps, from_inner, from_outer, part, product, spread, columns, map_row,
    precond_in, image_in, residual_in, blocks, couple, coarse_high, coarse_low,
    sums_out, solved_out, residual_out, whole_out, precond_out, image_out, small_out, tile_out, to_inner, to_outer,
):
    blk = lax.axis_index("blk")
    even = blk % 2 == 0
    nrhs, width = part.shape
    half = width // 2
    live = live_mask(blk, count, width)
    slots = couple.shape[0]
    summed = total_of(left, right, maps, slots, corners)
    corner_sum = summed[:, :corners]
    _, gram, energy = untile(summed[:, corners:], slots)
    solved = coarse_solve(corner_sum, (coarse_high[...], coarse_low[...]))
    energy = energy + dots(corner_sum, solved)
    unit = (lax.broadcasted_iota(jnp.int32, (nrhs, nrhs), 0) == lanes_of((nrhs, nrhs))).astype(F32)
    both = eliminate(jnp.stack([symmetric(2.0 * energy), symmetric(gram)]), jnp.stack([gram, unit]))
    alpha, inverse = both[0], both[1]

    rows = spread.shape[0]
    wide = map_row.shape[1]
    inner_got, outer_got = from_inner[...], from_outer[...]
    sides = [jnp.where(even, outer_got, inner_got), jnp.where(even, inner_got, outer_got)]
    index = jnp.concatenate([map_row[...]] + [side[nrhs + rows : nrhs + rows + 1, :wide] for side in sides], axis=1)
    at = picked(solved, index)
    whole = part[...] + against(at[:, :rows], columns[...])
    own = product[...] + product_of(at[:, :rows], spread[...])
    others = [
        side[:nrhs] + product_of(at[:, wide * turn : wide * turn + rows], side[nrhs : nrhs + rows])
        for turn, side in enumerate(sides, 1)
    ]
    change = live * (own - jnp.concatenate(others, axis=1))
    residual = residual_in[...] - combine(alpha, whole)
    precond = precond_in[...] - combine(alpha, change)

    image = mm(precond.astype(BF16), blocks[...], NN)
    left = jnp.concatenate([residual, precond, precond_in[...], image_in[...]], axis=0)
    grams = dots(left, jnp.concatenate([precond, image], axis=0))
    middle = abreast(grams[2 * nrhs : 3 * nrhs, nrhs:] + grams[3 * nrhs :, :nrhs])
    tile = tile_of(
        corner_values(precond, couple[...]), middle, grams[:nrhs, :nrhs], grams[nrhs : 2 * nrhs, nrhs:]
    )
    tile_out[...] = tile
    inner, outer = split(even, image[:, :half], image[:, half:])
    to_inner[:, :half] = inner
    to_inner[:, half:] = tile
    to_outer[...] = outer
    sums_out[...] = corner_sum
    solved_out[...] = solved
    residual_out[...] = residual
    whole_out[...] = whole
    precond_out[...] = precond
    image_out[...] = image
    small_out[...] = jnp.concatenate([inverse, energy, alpha, jnp.zeros((nrhs, 128 - 3 * nrhs), F32)], axis=1)


def final_kernel(
    count, corners, left, right, maps, got, from_outer, precond, image, residual, old_precond, old_image, old_sums,
    old_solved, small, columns, map_row, sign, coarse_high, coarse_low,
    multipliers_out, residual_out,
):
    blk = lax.axis_index("blk")
    even = blk % 2 == 0
    nrhs, width = precond.shape
    live = live_mask(blk, count, width)
    slots = columns.shape[0] // 2
    summed = total_of(left, right, maps, slots, corners)
    corner_sum = summed[:, :corners]
    old_new, gram, new_new = untile(summed[:, corners:], slots)
    beta = combine(small[:, :nrhs], gram)
    solved = coarse_solve(corner_sum, (coarse_high[...], coarse_low[...]))
    cross = dots(
        jnp.concatenate([corner_sum, old_sums[...]], axis=0),
        jnp.concatenate([solved, old_solved[...]], axis=0),
    )
    new_new = new_new + cross[:nrhs, :nrhs]
    old_new = old_new + cross[nrhs:, :nrhs] + transposed(cross[:nrhs, nrhs:])
    old_old = symmetric(small[:, nrhs : 2 * nrhs])
    energy = new_new + combine(beta, old_new + combine(old_old, beta))
    alpha = eliminate(symmetric(2.0 * energy)[None], gram[None])[0]
    image_beside = joined(even, got[:, : width // 2], from_outer[...])
    at = picked(solved, map_row[...])
    whole = live * (image[...] - image_beside) + against(at[:, : columns.shape[0]], columns[...])
    carried = combine(transposed(beta), alpha)
    first = small[:, 2 * nrhs : 3 * nrhs]
    weights = jnp.concatenate([alpha, carried + first], axis=0)
    multipliers_out[0] = sign[...] * combine(
        weights, jnp.concatenate([precond[...], old_precond[...]], axis=0)
    )
    weights = jnp.concatenate([alpha, carried], axis=0)
    change = combine(weights, jnp.concatenate([whole, old_image[...]], axis=0))
    residual_out[0] = sign[...] * (residual[...] - change)


VMEM = pl.BlockSpec(memory_space=pltpu.VMEM)
HBM = pl.BlockSpec(memory_space=pltpu.HBM)


def call(body, shapes, *args, specs=None, scratch=(), flops=0):
    shapes = [jax.ShapeDtypeStruct(shape, dtype) for shape, dtype in shapes]
    moved = sum(arg.size * arg.dtype.itemsize for arg in args)
    return pl.pallas_call(
        body,
        out_shape=shapes,
        in_specs=specs or [VMEM] * len(args),
        out_specs=[VMEM] * len(shapes),
        scratch_shapes=list(scratch),
        compiler_params=pltpu.CompilerParams(vmem_limit_bytes=16 << 20),
        cost_estimate=pl.CostEstimate(flops=flops, bytes_accessed=moved, transcendentals=0),
    )(*args)


def local(count, groups, dual_rhs, dual_ops, prec_ops, corner_coupling, corner_map, signs, coarse_inverse):
    nrhs, width = dual_rhs.shape[1:]
    half = width // 2
    corners = coarse_inverse.shape[0]
    inner, outer = inner_pairs(count, groups), outer_pairs(count, groups)
    steps = rotations(count, groups)
    dense_shape = ((nrhs, corners + TILE), F32)
    slots = corner_map.shape[1]
    flops = 2 * nrhs * width * width

    def permute(values, pairs):
        return lax.ppermute(values, AXES, pairs)

    def exchange(to_inner, to_outer):
        from_outer = permute(to_outer, outer)
        return permute(to_inner, inner), from_outer

    def densify(tiles, maps):
        body = functools.partial(dense_kernel, slots, corners)
        return call(body, [dense_shape], tiles, maps, flops=flops)[0]

    def region(tile, to_inner, to_outer, maps=None, follow=None):
        from_outer = permute(to_outer, outer)
        got = permute(to_inner, inner)
        even = lax.axis_index("blk") % 2 == 0
        values = merged(tile, got[:, got.shape[1] - TILE :], even, 2 * slots + 4 * nrhs)
        known = maps
        left, right = None, None
        for index, turns in enumerate(steps):
            if index > 0:
                if left.shape[1] == TILE and 8 * MOST < 2 * left.shape[0] * (1 + len(turns)):
                    known = known or (left, right)
                    left, right = densify(left, known[0]), densify(right, known[1])
                if left.shape[1] == TILE:
                    values = jnp.concatenate([left, right], axis=0)
                else:
                    values = left + right
            if follow is None and index == len(steps) - 1:
                values, from_outer = lax.optimization_barrier((values, from_outer))
                result = (got, from_outer)
            if follow is not None and index == max(len(steps) - 2, 0):
                *kept, to_inner, to_outer = follow(got, from_outer)
                values, to_inner, to_outer = lax.optimization_barrier((values, to_inner, to_outer))
                result = (*exchange(to_inner, to_outer), *kept)
            left = values
            terms = [permute(values, pairs) for pairs in turns]
            right = jnp.concatenate(terms, axis=0) if left.shape[1] == TILE else sum(terms[1:], terms[0])
        known = known or (left, right)
        if left.shape[1] == TILE:
            left = densify(left, known[0])
        return known, (left, right, known[1], *result)

    wide = ((nrhs, width), F32)
    face = ((nrhs, half), F32)
    pieces = 4
    product, to_inner, to_outer, residual0, sign, couple, map_row, *extras, held = call(
        functools.partial(start_kernel, count),
        [
            wide, face, face, wide, ((1, width), F32), (corner_coupling.shape[1:], BF16),
            ((1, 128), F32), face, face,
            ((pieces, width // pieces, width), BF16),
        ],
        *[pltpu.with_memory_space_constraint(arg, pltpu.HBM) for arg in (dual_rhs, signs, prec_ops, corner_coupling, corner_map)],
        specs=[HBM] * 5,
        scratch=[
            pltpu.VMEM(dual_rhs.shape, F32),
            pltpu.VMEM(signs.shape, jnp.int32),
            pltpu.VMEM(corner_coupling.shape, BF16),
            pltpu.VMEM(corner_map.shape, jnp.int32),
            pltpu.SemaphoreType.DMA((pieces + 4,)),
        ],
        flops=flops,
    )
    (loaded,) = call(
        load_kernel,
        [((width, width), BF16)],
        pltpu.with_memory_space_constraint(dual_ops, pltpu.HBM), sign,
        specs=[HBM, VMEM],
        scratch=[pltpu.SemaphoreType.DMA((pieces,))],
    )
    tile_shape = ((nrhs, TILE), F32)
    precond0, image0, tile, to_inner, to_outer = call(
        functools.partial(first_kernel, count),
        [wide, wide, tile_shape, ((nrhs, width + TILE), F32), wide],
        product, *exchange(to_inner, to_outer), residual0, loaded, couple, map_row, *extras,
        flops=flops,
    )
    square = ((corners, corners), BF16)
    coarse_parts = call(prepare_kernel, [square, square], coarse_inverse, flops=corners * corners)
    rows = nrhs + 2 * slots + 8

    def follow(got, from_outer):
        return call(
            functools.partial(follow_kernel, count),
            [
                wide, wide, ((2 * slots, width), F32), ((2 * slots, width), BF16), ((1, 128), F32),
                ((rows, half), F32), ((rows, half), F32),
            ],
            image0, got, from_outer, couple, map_row, held,
            flops=5 * flops,
        )

    maps, gathered = region(tile, to_inner, to_outer, follow=follow)
    columns, index = gathered[-2:]
    sums = ((nrhs, corners), F32)
    sums0, solved0, residual1, whole0, precond1, image1, small, tile, to_inner, to_outer = call(
        functools.partial(middle_kernel, count, corners),
        [sums, sums, wide, wide, wide, wide, ((nrhs, 128), F32), tile_shape, ((nrhs, half + TILE), F32), face],
        *gathered, precond0, image0, residual0, loaded, couple, *coarse_parts,
        flops=flops,
    )
    _, gathered = region(tile, to_inner, to_outer, maps=maps)
    whole_out = ((1, nrhs, width), F32)
    return tuple(
        call(
            functools.partial(final_kernel, count, corners),
            [whole_out, whole_out],
            *gathered, precond1, image1, residual1, precond0, whole0, sums0, solved0, small,
            columns, index, sign, *coarse_parts,
            flops=flops,
        )
    )


def solution(mesh):
    in_specs = (
        P("grp", None, "blk"),
        P("grp", "blk", None),
        P("grp", "blk", None),
        P("grp", "blk", None),
        P("grp", "blk"),
        P("grp", "blk"),
        P(),
    )
    out_specs = (P("grp", None, "blk"), P("grp", None, "blk"))
    return jax.shard_map(
        functools.partial(local, mesh.shape["blk"], mesh.shape["grp"]),
        mesh=mesh,
        in_specs=in_specs,
        out_specs=out_specs,
        check_vma=False,
    )
```

```python
import functools

import jax
import jax.numpy as jnp
from jax import lax
from jax.experimental import pallas as pl
from jax.experimental.pallas import tpu as pltpu
from jax.sharding import PartitionSpec as P

AXES = ("blk", "grp")
NN = (((1,), (0,)), ((), ()))
NT = (((1,), (1,)), ((), ()))
TN = (((0,), (0,)), ((), ()))
F32 = jnp.float32
BF16 = jnp.bfloat16


def radices(count):
    found = []
    factor = 2
    while count > 1:
        while count % factor == 0:
            found.append(factor)
            count //= factor
        factor += 1
    return found


def swap(count, groups, partner):
    pairs = []
    for blk in range(count):
        for grp in range(groups):
            other = partner(blk)
            if 0 <= other < count:
                target = other * groups + grp
            elif grp ^ 1 < groups:
                target = blk * groups + (grp ^ 1)
            else:
                target = blk * groups + grp
            pairs.append((blk * groups + grp, target))
    return pairs


def inner_pairs(count, groups):
    return swap(count, groups, lambda blk: blk ^ 1)


def outer_pairs(count, groups):
    return swap(count, groups, lambda blk: blk + 1 if blk % 2 == 1 else blk - 1)


def rotations(count, groups):
    core = 2 if count % 2 == 0 else 1
    steps = []

    def flipped(blk, turn):
        return (blk ^ 1) if (core == 2 and turn) else blk

    def add_axis(step_target, factor):
        steps.append(
            [
                [
                    (blk * groups + grp, step_target(blk, grp, turn))
                    for blk in range(count)
                    for grp in range(groups)
                ]
                for turn in range(1, factor)
            ]
        )

    stride = 1
    blk_steps = []
    for factor in radices(count // core):
        blk_steps.append((stride, factor))
        stride *= factor
    grp_steps = []
    stride = 1
    for factor in radices(groups):
        grp_steps.append((stride, factor))
        stride *= factor

    def blk_target(stride, factor):
        def target(blk, grp, turn):
            chip = blk // core
            digit = (chip // stride) % factor
            moved = chip + ((digit + turn) % factor - digit) * stride
            return flipped(moved * core + blk % core, turn) * groups + grp

        return target

    def grp_target(stride, factor):
        def target(blk, grp, turn):
            digit = (grp // stride) % factor
            moved = grp + ((digit + turn) % factor - digit) * stride
            return flipped(blk, turn) * groups + moved

        return target

    for stride, factor in blk_steps[1:]:
        add_axis(blk_target(stride, factor), factor)
    for stride, factor in grp_steps:
        add_axis(grp_target(stride, factor), factor)
    for stride, factor in blk_steps[:1]:
        add_axis(blk_target(stride, factor), factor)
    return steps


def mm(first, second, dims):
    return lax.dot_general(first, second, dims, preferred_element_type=F32)


def halves(values):
    high = values.astype(BF16)
    return high, (values - high.astype(F32)).astype(BF16)


def stacked(values):
    return jnp.concatenate(halves(values), axis=0)


def folded(rows):
    count = rows.shape[0] // 2
    return rows[:count] + rows[count:]


def dots(first, second):
    product = folded(mm(stacked(first), stacked(second), NT))
    count = second.shape[0]
    return product[:, :count] + product[:, count:]


def combine(weights, values):
    weight_high, weight_low = halves(weights)
    high, low = halves(values)
    left = jnp.concatenate([weight_high, weight_high, weight_low, weight_low], axis=0)
    right = jnp.concatenate([high, low, high, low], axis=0)
    return mm(left, right, TN)


def against(values, exact):
    return folded(mm(stacked(values), exact, NN))


def lanes_of(shape):
    return lax.broadcasted_iota(jnp.int32, shape, len(shape) - 1)


def chosen(row, corners):
    shape = (corners, row.shape[1])
    return (lax.broadcasted_iota(jnp.int32, shape, 0) == row).astype(BF16)


def live_mask(blk, count, width):
    lane = lanes_of((1, width))
    low = (blk > 0).astype(F32)
    up = (blk < count - 1).astype(F32)
    return jnp.where(lane < width // 2, low, up)


def split(even, low, up):
    return jnp.where(even, up, low), jnp.where(even, low, up)


def joined(even, from_inner, from_outer):
    low = jnp.where(even, from_outer, from_inner)
    up = jnp.where(even, from_inner, from_outer)
    return jnp.concatenate([low, up], axis=1)


def transposed(matrix):
    return matrix.T


def eliminate(matrix, target):
    count = matrix.shape[1]
    row_index = lax.broadcasted_iota(jnp.int32, (1, count, 1), 1)
    column_index = lax.broadcasted_iota(jnp.int32, (1, count, count), 2)
    diagonal = jnp.where(row_index == column_index, matrix, 0.0)
    scale = lax.rsqrt(jnp.sum(diagonal, axis=2, keepdims=True))
    matrix = matrix * lax.rsqrt(jnp.sum(diagonal, axis=1, keepdims=True))
    work = jnp.concatenate([matrix, target], axis=2) * scale
    size = 4
    for start in range(0, count, size):
        at = [start + index for index in range(size)]
        columns = [jnp.broadcast_to(work[:, :, k : k + 1], work.shape) for k in at]
        pivot = [[column[:, k : k + 1] for column in columns] for k in at]
        rows = [work[:, k : k + 1] for k in at]
        for one in range(0, size, 2):
            two = one + 1
            a, b, c, d = pivot[one][one], pivot[one][two], pivot[two][one], pivot[two][two]
            inverse = 1.0 / (a * d - b * c)
            for j in range(two + 1, size):
                p, q = pivot[one][j], pivot[two][j]
                pivot[one][j], pivot[two][j] = (d * p - b * q) * inverse, (a * q - c * p) * inverse
            p, q = rows[one], rows[two]
            rows[one], rows[two] = (d * p - b * q) * inverse, (a * q - c * p) * inverse
            for i in range(size):
                if i not in (one, two):
                    left, right = pivot[i][one], pivot[i][two]
                    for j in range(two + 1, size):
                        pivot[i][j] = pivot[i][j] - left * pivot[one][j] - right * pivot[two][j]
                    rows[i] = rows[i] - left * rows[one] - right * rows[two]
        products = [column * row for column, row in zip(columns, rows)]
        work = work - ((products[0] + products[1]) + (products[2] + products[3]))
        for k, row in zip(at, rows):
            work = jnp.where(row_index == k, row, work)
    return work[:, :, count:] * scale


def symmetric(matrix):
    return 0.5 * (matrix + transposed(matrix))


def corner_values(values, couple):
    half = values.shape[1] // 2
    both = stacked(values)
    low = folded(mm(both[:, :half], couple, NT))
    up = folded(mm(both[:, half:], couple, NT))
    return jnp.where(lanes_of(low.shape) < couple.shape[0] // 2, low, up)


TILE = 128
GROUP = 32
MOST = 32


def abreast(rows):
    half = rows.shape[0] // 2
    return [rows[:half], rows[half:]]


def tiles_of(even, corner, index, first, second, third):
    half = first.shape[0] // 2
    squares = abreast(first) + abreast(second) + abreast(third)
    used = sum(part.shape[1] for part in squares)
    squares = jnp.concatenate(squares + [jnp.zeros((half, TILE - used), F32)], axis=1)
    values = abreast(corner)
    gap = jnp.zeros((half, 2 * corner.shape[1]), F32)
    left, right = jnp.concatenate(values + [gap], axis=1), jnp.concatenate([gap] + values, axis=1)
    row = lax.broadcasted_iota(jnp.int32, (half, index.shape[1]), 0)
    index = jnp.where(row == jnp.where(even, 0, 1), index, 0.0)
    rest = jnp.zeros((half, TILE - left.shape[1] - index.shape[1]), F32)
    return jnp.concatenate(
        [squares, jnp.concatenate([jnp.where(even, left, right), index, rest], axis=1)], axis=0
    )


def untile(tile):
    count = 2 * tile.shape[0]
    return [
        jnp.concatenate([tile[:, at : at + count], tile[:, at + count : at + 2 * count]], axis=0)
        for at in (0, 2 * count, 4 * count)
    ]


def dense(tiles, maps, slots, corners):
    count = tiles.shape[0] // 8
    lane = lanes_of((1, TILE))
    low, up, index = [], [], []

    def moved(rows, at, to):
        shift = (to - at) % TILE
        return pltpu.roll(rows, shift, 1) if shift else rows

    for start in range(0, count, TILE // GROUP // 2):
        parts = [jnp.zeros((8, TILE), F32), jnp.zeros((8, TILE), F32), jnp.full((1, TILE), -1.0, F32)]
        for turn in range(TILE // GROUP):
            at, core = start + turn // 2, turn % 2
            if at < count:
                here = (lane // GROUP == turn) & (lane % GROUP < slots)
                tile = tiles[8 * at : 8 * at + 8]
                name = maps[8 * at + core : 8 * at + core + 1]
                new = [
                    moved(tile, 2 * slots * core, GROUP * turn),
                    moved(tile, 2 * slots * core + slots, GROUP * turn),
                    moved(name, 4 * slots, GROUP * turn),
                ]
                parts = [jnp.where(here, one, old) for one, old in zip(new, parts)]
        low.append(parts[0])
        up.append(parts[1])
        index.append(parts[2])
    values = jnp.concatenate([jnp.concatenate(low, axis=1), jnp.concatenate(up, axis=1)], axis=0)
    choice = chosen(jnp.concatenate(index, axis=1).astype(jnp.int32), corners)
    return folded(mm(stacked(values), choice, NT))


def dense_kernel(slots, corners, tiles, maps, out):
    out[:, :corners] = dense(tiles[8:], maps[8:], slots, corners)
    out[:, corners:] = jnp.concatenate([tiles[:8], jnp.zeros((out.shape[0] - 8, TILE), F32)], axis=0)


def total_of(left, right, maps, slots, corners):
    if right.shape[1] == TILE:
        return left[:, :corners] + dense(right[8:], maps[8:], slots, corners), left[:8, corners:] + right[:8]
    return left[:, :corners] + right[:, :corners], left[:8, corners:] + right[:8, corners:]


def face_rows(rows):
    low = lax.broadcasted_iota(jnp.int32, rows.shape, 0) < rows.shape[0] // 2
    return jnp.concatenate([jnp.where(low, rows, 0.0), jnp.where(low, 0.0, rows)], axis=1)


def picked(solved, row):
    return folded(mm(stacked(solved), chosen(row.astype(jnp.int32), solved.shape[1]), NN))


def product_of(first, second):
    high, low = halves(second)
    return folded(mm(stacked(first), high, NN)) + mm(first.astype(BF16), low, NN)


def coarse_solve(corner_sum, parts):
    high, low = parts
    first = folded(mm(stacked(corner_sum), high, NN))
    return first + mm(corner_sum.astype(BF16), low, NN)


def start_kernel(
    count, rhs, signs, blocks, coupling, corner_map,
    product, to_inner, to_outer, residual_out, sign_out, couple_out, map_out, inner_extra, outer_extra, held,
    rhs_held, signs_held, coupling_held, map_held, sems,
):
    rows = held.shape[1]
    pieces = [(rhs, rhs_held), (signs, signs_held)]
    pieces += [(blocks.at[0, pl.ds(part * rows, rows)], held.at[part]) for part in range(held.shape[0])]
    pieces += [(corner_map, map_held), (coupling, coupling_held)]
    copies = [pltpu.make_async_copy(*piece, sems.at[index]) for index, piece in enumerate(pieces)]
    for copy in copies:
        copy.start()
    blk = lax.axis_index("blk")
    even = blk % 2 == 0
    nrhs, width = product.shape
    half = width // 2
    live = live_mask(blk, count, width)
    copies[0].wait()
    copies[1].wait()
    sign = signs_held[...].astype(F32) * live
    residual = sign * rhs_held[0]
    rounded = residual.astype(BF16)
    sign_out[...] = sign
    residual_out[...] = residual
    total = jnp.zeros((nrhs, width), F32)
    for part, copy in enumerate(copies[2:-2]):
        copy.wait()
        total = total + mm(rounded[:, part * rows : (part + 1) * rows], held[part], NN)
    product[...] = total
    inner, outer = split(even, total[:, :half], total[:, half:])
    to_inner[...] = inner
    to_outer[...] = outer
    copies[-2].wait()
    copies[-1].wait()
    couple = coupling_held[0]
    couple_out[...] = couple
    slots = couple.shape[0] // 2
    wide = couple.astype(F32)
    row = jnp.concatenate([map_held[...].astype(F32), jnp.zeros((1, half - 2 * slots), F32)], axis=1)
    map_out[...] = row[:, : map_out.shape[1]]
    fill = jnp.zeros((nrhs - slots - 1, half), F32)
    inner, outer = split(
        even,
        jnp.concatenate([wide[:slots], row, fill], axis=0),
        jnp.concatenate([wide[slots:], pltpu.roll(row, half - slots, 1), fill], axis=0),
    )
    inner_extra[...] = inner
    outer_extra[...] = outer


def first_kernel(
    count, product, from_inner, from_outer, residual, blocks, couple, map_row, inner_extra, outer_extra,
    precond_out, image_out, tile_out, to_inner, to_outer,
):
    blk = lax.axis_index("blk")
    even = blk % 2 == 0
    nrhs, width = product.shape
    half = width // 2
    live = live_mask(blk, count, width)
    precond = live * (product[...] - joined(even, from_inner[...], from_outer[...]))
    image = mm(precond.astype(BF16), blocks[...], NN)
    precond_out[...] = precond
    image_out[...] = image
    grams = dots(
        jnp.concatenate([residual[...], precond], axis=0), jnp.concatenate([precond, image], axis=0)
    )
    slots = couple.shape[0]
    first, second = grams[:nrhs, :nrhs], grams[nrhs:, nrhs:]
    tile = tiles_of(
        even, corner_values(precond, couple[...]), map_row[:, :slots], first, second, jnp.zeros_like(first)
    )
    tile_out[...] = tile
    inner, outer = split(even, image[:, :half], image[:, half:])
    to_inner[:, :half] = inner
    to_outer[:, :half] = outer
    to_inner[:, half:width] = inner_extra[...]
    to_outer[:, half:] = outer_extra[...]
    to_inner[:, width:] = tile


def load_kernel(blocks, after, out, sems):
    del after
    rows = out.shape[0] // sems.shape[0]
    copies = [
        pltpu.make_async_copy(
            blocks.at[0, pl.ds(part * rows, rows)], out.at[pl.ds(part * rows, rows)], sems.at[part]
        )
        for part in range(sems.shape[0])
    ]
    for copy in copies:
        copy.start()
    for copy in copies:
        copy.wait()


def prepare_kernel(coarse, high, low):
    top, rest = halves(coarse[...])
    high[...] = top
    low[...] = rest


def follow_kernel(
    count, image, got, from_outer, couple, map_row, blocks,
    part_out, product_out, spread_out, columns_out, map_out, to_inner, to_outer,
):
    blk = lax.axis_index("blk")
    even = blk % 2 == 0
    nrhs, width = image.shape
    half = width // 2
    live = live_mask(blk, count, width)
    inner_got = got[...]
    outer_got = from_outer[...]
    part = live * (image[...] - joined(even, inner_got[:, :half], outer_got[:, :half]))
    beside = joined(even, inner_got[:, half:width], outer_got[:, half:])
    wide = couple[...].astype(F32)
    slots = wide.shape[0] // 2
    other = jnp.concatenate([beside[:slots, :half], beside[:slots, half:]], axis=0)
    columns = (live * jnp.concatenate([face_rows(wide), -face_rows(other)], axis=0)).astype(BF16)
    products = mm(jnp.concatenate([stacked(part), columns], axis=0), blocks[...].reshape(width, width), NN)
    product = products[:nrhs] + products[nrhs : 2 * nrhs]
    spread = products[2 * nrhs :]
    row = jnp.concatenate(
        [
            map_row[:, : 2 * slots],
            beside[slots : slots + 1, :slots],
            beside[slots : slots + 1, half : half + slots],
            jnp.full((1, map_row.shape[1] - 4 * slots), -1.0, F32),
        ],
        axis=1,
    )
    part_out[...] = part
    product_out[...] = product
    spread_out[...] = spread
    columns_out[...] = columns
    map_out[...] = row
    count_rows = nrhs + 4 * slots
    rows = jnp.concatenate([product, spread], axis=0)
    to_inner[:count_rows, :], to_outer[:count_rows, :] = split(even, rows[:, :half], rows[:, half:])
    last = jnp.concatenate([row, jnp.zeros((1, half - row.shape[1]), F32)], axis=1)
    last = jnp.broadcast_to(last, (to_inner.shape[0] - count_rows, half))
    to_inner[count_rows:, :] = last
    to_outer[count_rows:, :] = last


def middle_kernel(
    count, corners, left, right, maps, from_inner, from_outer, part, product, spread, columns, map_row,
    precond_in, image_in, residual_in, blocks, couple, coarse_high, coarse_low,
    solved_out, residual_out, whole_out, precond_out, image_out, small_out, tile_out, to_inner, to_outer,
):
    blk = lax.axis_index("blk")
    even = blk % 2 == 0
    nrhs, width = part.shape
    half = width // 2
    live = live_mask(blk, count, width)
    slots = couple.shape[0]
    corner_sum, squares = total_of(left, right, maps, slots, corners)
    gram, energy, _ = untile(squares)
    solved = coarse_solve(corner_sum, (coarse_high[...], coarse_low[...]))
    energy = energy + dots(corner_sum, solved)
    unit = (lax.broadcasted_iota(jnp.int32, (nrhs, nrhs), 0) == lanes_of((nrhs, nrhs))).astype(F32)
    both = eliminate(jnp.stack([symmetric(2.0 * energy), symmetric(gram)]), jnp.stack([gram, unit]))
    alpha, inverse = both[0], both[1]

    rows = spread.shape[0]
    wide = map_row.shape[1]
    inner_got, outer_got = from_inner[...], from_outer[...]
    sides = [jnp.where(even, outer_got, inner_got), jnp.where(even, inner_got, outer_got)]
    index = jnp.concatenate([map_row[...]] + [side[nrhs + rows : nrhs + rows + 1, :wide] for side in sides], axis=1)
    at = picked(solved, index)
    whole = part[...] + against(at[:, :rows], columns[...])
    own = product[...] + product_of(at[:, :rows], spread[...])
    others = [
        side[:nrhs] + product_of(at[:, wide * turn : wide * turn + rows], side[nrhs : nrhs + rows])
        for turn, side in enumerate(sides, 1)
    ]
    change = live * (own - jnp.concatenate(others, axis=1))
    change = combine(alpha, jnp.concatenate([whole, change], axis=1))
    residual = residual_in[...] - change[:, :width]
    precond = precond_in[...] - change[:, width:]

    image = mm(precond.astype(BF16), blocks[...], NN)
    left = jnp.concatenate([residual, precond, precond_in[...], image_in[...]], axis=0)
    grams = dots(left, jnp.concatenate([precond, image], axis=0))
    tile = tiles_of(
        even,
        corner_values(precond, couple[...]),
        jnp.zeros((1, slots), F32),
        grams[:nrhs, :nrhs],
        grams[nrhs : 2 * nrhs, nrhs:],
        grams[2 * nrhs : 3 * nrhs, nrhs:] + grams[3 * nrhs :, :nrhs],
    )
    tile_out[...] = tile
    inner, outer = split(even, image[:, :half], image[:, half:])
    to_inner[:, :half] = inner
    to_inner[:, half:] = tile
    to_outer[...] = outer
    solved_out[...] = solved
    residual_out[...] = residual
    whole_out[...] = whole
    precond_out[...] = precond
    image_out[...] = image
    small_out[...] = jnp.concatenate([inverse, energy, alpha, jnp.zeros((nrhs, 128 - 3 * nrhs), F32)], axis=1)


def final_kernel(
    count, corners, left, right, maps, got, from_outer, precond, image, residual, old_precond, old_image,
    old_solved, small, columns, map_row, sign, coarse_high, coarse_low,
    multipliers_out, residual_out,
):
    blk = lax.axis_index("blk")
    even = blk % 2 == 0
    nrhs, width = precond.shape
    live = live_mask(blk, count, width)
    slots = columns.shape[0] // 2
    corner_sum, squares = total_of(left, right, maps, slots, corners)
    gram, new_new, old_new = untile(squares)
    beta = combine(small[:, :nrhs], gram)
    solved = coarse_solve(corner_sum, (coarse_high[...], coarse_low[...]))
    old_old = symmetric(small[:, nrhs : 2 * nrhs])
    old_new = old_new + 2.0 * dots(old_solved[...], corner_sum)
    energy = new_new + combine(beta, old_new + combine(old_old, beta)) + dots(corner_sum, solved)
    alpha = eliminate(symmetric(2.0 * energy)[None], gram[None])[0]
    image_beside = joined(even, got[:, : width // 2], from_outer[...])
    at = picked(solved, map_row[...])
    whole = live * (image[...] - image_beside) + against(at[:, : columns.shape[0]], columns[...])
    first = combine(small[:, 2 * nrhs : 3 * nrhs], old_precond[...])
    carried = combine(beta, jnp.concatenate([old_precond[...], old_image[...]], axis=1))
    change = combine(alpha, jnp.concatenate([precond[...], whole], axis=1) + carried)
    multipliers_out[0] = sign[...] * (first + change[:, :width])
    residual_out[0] = sign[...] * (residual[...] - change[:, width:])


VMEM = pl.BlockSpec(memory_space=pltpu.VMEM)
HBM = pl.BlockSpec(memory_space=pltpu.HBM)


def call(body, shapes, *args, specs=None, scratch=(), flops=0):
    shapes = [jax.ShapeDtypeStruct(shape, dtype) for shape, dtype in shapes]
    moved = sum(arg.size * arg.dtype.itemsize for arg in args)
    return pl.pallas_call(
        body,
        out_shape=shapes,
        in_specs=specs or [VMEM] * len(args),
        out_specs=[VMEM] * len(shapes),
        scratch_shapes=list(scratch),
        compiler_params=pltpu.CompilerParams(vmem_limit_bytes=16 << 20),
        cost_estimate=pl.CostEstimate(flops=flops, bytes_accessed=moved, transcendentals=0),
    )(*args)


def local(count, groups, dual_rhs, dual_ops, prec_ops, corner_coupling, corner_map, signs, coarse_inverse):
    nrhs, width = dual_rhs.shape[1:]
    half = width // 2
    corners = coarse_inverse.shape[0]
    inner, outer = inner_pairs(count, groups), outer_pairs(count, groups)
    steps = rotations(count, groups)
    dense_shape = ((nrhs, corners + TILE), F32)
    slots = corner_map.shape[1]
    flops = 2 * nrhs * width * width

    def permute(values, pairs):
        return lax.ppermute(values, AXES, pairs)

    def exchange(to_inner, to_outer):
        from_outer = permute(to_outer, outer)
        return permute(to_inner, inner), from_outer

    def densify(tiles, maps):
        body = functools.partial(dense_kernel, slots, corners)
        return call(body, [dense_shape], tiles, maps, flops=flops)[0]

    def united(parts):
        if parts[0].shape[1] != TILE:
            return sum(parts[1:], parts[0])
        squares = [part[:8] for part in parts]
        return jnp.concatenate([sum(squares[1:], squares[0])] + [part[8:] for part in parts], axis=0)

    def region(tile, to_inner, to_outer, maps=None, follow=None):
        from_outer = permute(to_outer, outer)
        got = permute(to_inner, inner)
        values = tile + got[:, got.shape[1] - TILE :]
        known = maps
        left, right = None, None
        for index, turns in enumerate(steps):
            if index > 0:
                held = left.shape[0] + right.shape[0] - 16
                if left.shape[1] == TILE and 8 * MOST < 2 * held * (1 + len(turns)):
                    known = known or (left, right)
                    left, right = densify(left, known[0]), densify(right, known[1])
                values = united([left, right])
            if follow is None and index == len(steps) - 1:
                values, from_outer = lax.optimization_barrier((values, from_outer))
                result = (got, from_outer)
            if follow is not None and index == max(len(steps) - 2, 0):
                *kept, to_inner, to_outer = follow(got, from_outer)
                values, to_inner, to_outer = lax.optimization_barrier((values, to_inner, to_outer))
                result = (*exchange(to_inner, to_outer), *kept)
            left = values
            right = united([permute(values, pairs) for pairs in turns])
        known = known or (left, right)
        if left.shape[1] == TILE:
            left = densify(left, known[0])
        return known, (left, right, known[1], *result)

    wide = ((nrhs, width), F32)
    face = ((nrhs, half), F32)
    pieces = 4
    product, to_inner, to_outer, residual0, sign, couple, map_row, *extras, held = call(
        functools.partial(start_kernel, count),
        [
            wide, face, face, wide, ((1, width), F32), (corner_coupling.shape[1:], BF16),
            ((1, 128), F32), face, face,
            ((pieces, width // pieces, width), BF16),
        ],
        *[pltpu.with_memory_space_constraint(arg, pltpu.HBM) for arg in (dual_rhs, signs, prec_ops, corner_coupling, corner_map)],
        specs=[HBM] * 5,
        scratch=[
            pltpu.VMEM(dual_rhs.shape, F32),
            pltpu.VMEM(signs.shape, jnp.int32),
            pltpu.VMEM(corner_coupling.shape, BF16),
            pltpu.VMEM(corner_map.shape, jnp.int32),
            pltpu.SemaphoreType.DMA((pieces + 4,)),
        ],
        flops=flops,
    )
    (loaded,) = call(
        load_kernel,
        [((width, width), BF16)],
        pltpu.with_memory_space_constraint(dual_ops, pltpu.HBM), sign,
        specs=[HBM, VMEM],
        scratch=[pltpu.SemaphoreType.DMA((pieces,))],
    )
    tile_shape = ((nrhs, TILE), F32)
    precond0, image0, tile, to_inner, to_outer = call(
        functools.partial(first_kernel, count),
        [wide, wide, tile_shape, ((nrhs, width + TILE), F32), wide],
        product, *exchange(to_inner, to_outer), residual0, loaded, couple, map_row, *extras,
        flops=flops,
    )
    square = ((corners, corners), BF16)
    coarse_parts = call(prepare_kernel, [square, square], coarse_inverse, flops=corners * corners)
    rows = nrhs + 2 * slots + 8

    def follow(got, from_outer):
        return call(
            functools.partial(follow_kernel, count),
            [
                wide, wide, ((2 * slots, width), F32), ((2 * slots, width), BF16), ((1, 128), F32),
                ((rows, half), F32), ((rows, half), F32),
            ],
            image0, got, from_outer, couple, map_row, held,
            flops=5 * flops,
        )

    maps, gathered = region(tile, to_inner, to_outer, follow=follow)
    columns, index = gathered[-2:]
    solved0, residual1, whole0, precond1, image1, small, tile, to_inner, to_outer = call(
        functools.partial(middle_kernel, count, corners),
        [((nrhs, corners), F32), wide, wide, wide, wide, ((nrhs, 128), F32), tile_shape, ((nrhs, half + TILE), F32), face],
        *gathered, precond0, image0, residual0, loaded, couple, *coarse_parts,
        flops=flops,
    )
    _, gathered = region(tile, to_inner, to_outer, maps=maps)
    whole_out = ((1, nrhs, width), F32)
    return tuple(
        call(
            functools.partial(final_kernel, count, corners),
            [whole_out, whole_out],
            *gathered, precond1, image1, residual1, precond0, whole0, solved0, small,
            columns, index, sign, *coarse_parts,
            flops=flops,
        )
    )


def solution(mesh):
    in_specs = (
        P("grp", None, "blk"),
        P("grp", "blk", None),
        P("grp", "blk", None),
        P("grp", "blk", None),
        P("grp", "blk"),
        P("grp", "blk"),
        P(),
    )
    out_specs = (P("grp", None, "blk"), P("grp", None, "blk"))
    return jax.shard_map(
        functools.partial(local, mesh.shape["blk"], mesh.shape["grp"]),
        mesh=mesh,
        in_specs=in_specs,
        out_specs=out_specs,
        check_vma=False,
    )
```

```python
import functools

import jax
import jax.numpy as jnp
from jax import lax
from jax.experimental import pallas as pl
from jax.experimental.pallas import tpu as pltpu
from jax.sharding import PartitionSpec as P

AXES = ("blk", "grp")
NN = (((1,), (0,)), ((), ()))
NT = (((1,), (1,)), ((), ()))
F32 = jnp.float32
BF16 = jnp.bfloat16


def radices(count):
    found = []
    factor = 2
    while count > 1:
        while count % factor == 0:
            found.append(factor)
            count //= factor
        factor += 1
    return found


def swap(count, groups, partner):
    pairs = []
    for blk in range(count):
        for grp in range(groups):
            other = partner(blk)
            if 0 <= other < count:
                target = other * groups + grp
            elif grp ^ 1 < groups:
                target = blk * groups + (grp ^ 1)
            else:
                target = blk * groups + grp
            pairs.append((blk * groups + grp, target))
    return pairs


def inner_pairs(count, groups):
    return swap(count, groups, lambda blk: blk ^ 1)


def outer_pairs(count, groups):
    return swap(count, groups, lambda blk: blk + 1 if blk % 2 == 1 else blk - 1)


def rotations(count, groups):
    core = 2 if count % 2 == 0 else 1
    steps = []

    def flipped(blk, turn):
        return (blk ^ 1) if (core == 2 and turn) else blk

    def add_axis(step_target, factor):
        steps.append(
            [
                [
                    (blk * groups + grp, step_target(blk, grp, turn))
                    for blk in range(count)
                    for grp in range(groups)
                ]
                for turn in range(1, factor)
            ]
        )

    stride = 1
    blk_steps = []
    for factor in radices(count // core):
        blk_steps.append((stride, factor))
        stride *= factor
    grp_steps = []
    stride = 1
    for factor in radices(groups):
        grp_steps.append((stride, factor))
        stride *= factor

    def blk_target(stride, factor):
        def target(blk, grp, turn):
            chip = blk // core
            digit = (chip // stride) % factor
            moved = chip + ((digit + turn) % factor - digit) * stride
            return flipped(moved * core + blk % core, turn) * groups + grp

        return target

    def grp_target(stride, factor):
        def target(blk, grp, turn):
            digit = (grp // stride) % factor
            moved = grp + ((digit + turn) % factor - digit) * stride
            return flipped(blk, turn) * groups + moved

        return target

    for stride, factor in blk_steps[1:]:
        add_axis(blk_target(stride, factor), factor)
    for stride, factor in grp_steps:
        add_axis(grp_target(stride, factor), factor)
    for stride, factor in blk_steps[:1]:
        add_axis(blk_target(stride, factor), factor)
    return steps


def mm(first, second, dims):
    return lax.dot_general(first, second, dims, preferred_element_type=F32)


def halves(values):
    high = values.astype(BF16)
    return high, (values - high.astype(F32)).astype(BF16)


def stacked(values):
    return jnp.concatenate(halves(values), axis=0)


def folded(rows):
    count = rows.shape[0] // 2
    return rows[:count] + rows[count:]


def dots(first, second):
    product = folded(mm(stacked(first), stacked(second), NT))
    count = second.shape[0]
    return product[:, :count] + product[:, count:]


def against(values, exact):
    return folded(mm(stacked(values), exact, NN))


def lanes_of(shape):
    return lax.broadcasted_iota(jnp.int32, shape, len(shape) - 1)


def chosen(row, corners):
    shape = (corners, row.shape[1])
    return (lax.broadcasted_iota(jnp.int32, shape, 0) == row).astype(BF16)


def live_mask(blk, count, width):
    lane = lanes_of((1, width))
    low = (blk > 0).astype(F32)
    up = (blk < count - 1).astype(F32)
    return jnp.where(lane < width // 2, low, up)


def split(even, low, up):
    return jnp.where(even, up, low), jnp.where(even, low, up)


def joined(even, from_inner, from_outer):
    low = jnp.where(even, from_outer, from_inner)
    up = jnp.where(even, from_inner, from_outer)
    return jnp.concatenate([low, up], axis=1)


def transposed(matrix):
    return matrix.T


def eliminate(matrix, target):
    count = matrix.shape[1]
    row_index = lax.broadcasted_iota(jnp.int32, (1, count, 1), 1)
    column_index = lax.broadcasted_iota(jnp.int32, (1, count, count), 2)
    diagonal = jnp.where(row_index == column_index, matrix, 0.0)
    scale = lax.rsqrt(jnp.sum(diagonal, axis=2, keepdims=True))
    matrix = matrix * lax.rsqrt(jnp.sum(diagonal, axis=1, keepdims=True))
    work = jnp.concatenate([matrix, target], axis=2) * scale
    size = 8
    for start in range(0, count, size):
        at = [start + index for index in range(size)]
        columns = [jnp.broadcast_to(work[:, :, k : k + 1], work.shape) for k in at]
        pivot = [[column[:, k : k + 1] for column in columns] for k in at]
        rows = [work[:, k : k + 1] for k in at]
        for one in range(0, size, 2):
            two = one + 1
            a, b, c, d = pivot[one][one], pivot[one][two], pivot[two][one], pivot[two][two]
            inverse = 1.0 / (a * d - b * c)
            for j in range(two + 1, size):
                p, q = pivot[one][j], pivot[two][j]
                pivot[one][j], pivot[two][j] = (d * p - b * q) * inverse, (a * q - c * p) * inverse
            p, q = rows[one], rows[two]
            rows[one], rows[two] = (d * p - b * q) * inverse, (a * q - c * p) * inverse
            for i in range(size):
                if i not in (one, two):
                    left, right = pivot[i][one], pivot[i][two]
                    for j in range(two + 1, size):
                        pivot[i][j] = pivot[i][j] - left * pivot[one][j] - right * pivot[two][j]
                    rows[i] = rows[i] - left * rows[one] - right * rows[two]
        products = [column * row for column, row in zip(columns, rows)]
        while len(products) > 1:
            products = [one + two for one, two in zip(products[::2], products[1::2])]
        work = work - products[0]
        for k, row in zip(at, rows):
            work = jnp.where(row_index == k, row, work)
    return work[:, :, count:] * scale


def symmetric(matrix):
    return 0.5 * (matrix + transposed(matrix))


def corner_values(values, couple):
    half = values.shape[1] // 2
    both = stacked(values)
    low = folded(mm(both[:, :half], couple, NT))
    up = folded(mm(both[:, half:], couple, NT))
    return jnp.where(lanes_of(low.shape) < couple.shape[0] // 2, low, up)


TILE = 128
GROUP = 32
MOST = 32


def abreast(rows):
    half = rows.shape[0] // 2
    return [rows[:half], rows[half:]]


def tiles_of(even, corner, index, first, second, third):
    half = first.shape[0] // 2
    squares = abreast(first) + abreast(second) + abreast(third)
    used = sum(part.shape[1] for part in squares)
    squares = jnp.concatenate(squares + [jnp.zeros((half, TILE - used), F32)], axis=1)
    values = abreast(corner)
    gap = jnp.zeros((half, 2 * corner.shape[1]), F32)
    left, right = jnp.concatenate(values + [gap], axis=1), jnp.concatenate([gap] + values, axis=1)
    row = lax.broadcasted_iota(jnp.int32, (half, index.shape[1]), 0)
    index = jnp.where(row == jnp.where(even, 0, 1), index, 0.0)
    rest = jnp.zeros((half, TILE - left.shape[1] - index.shape[1]), F32)
    return jnp.concatenate(
        [squares, jnp.concatenate([jnp.where(even, left, right), index, rest], axis=1)], axis=0
    )


def untile(tile):
    count = 2 * tile.shape[0]
    return [
        jnp.concatenate([tile[:, at : at + count], tile[:, at + count : at + 2 * count]], axis=0)
        for at in (0, 2 * count, 4 * count)
    ]


def dense(tiles, maps, slots, corners):
    count = tiles.shape[0] // 8
    lane = lanes_of((1, TILE))
    low, up, index = [], [], []

    def moved(rows, at, to):
        shift = (to - at) % TILE
        return pltpu.roll(rows, shift, 1) if shift else rows

    for start in range(0, count, TILE // GROUP // 2):
        parts = [jnp.zeros((8, TILE), F32), jnp.zeros((8, TILE), F32), jnp.full((1, TILE), -1.0, F32)]
        for turn in range(TILE // GROUP):
            at, core = start + turn // 2, turn % 2
            if at < count:
                here = (lane // GROUP == turn) & (lane % GROUP < slots)
                tile = tiles[8 * at : 8 * at + 8]
                name = maps[8 * at + core : 8 * at + core + 1]
                new = [
                    moved(tile, 2 * slots * core, GROUP * turn),
                    moved(tile, 2 * slots * core + slots, GROUP * turn),
                    moved(name, 4 * slots, GROUP * turn),
                ]
                parts = [jnp.where(here, one, old) for one, old in zip(new, parts)]
        low.append(parts[0])
        up.append(parts[1])
        index.append(parts[2])
    values = jnp.concatenate([jnp.concatenate(low, axis=1), jnp.concatenate(up, axis=1)], axis=0)
    choice = chosen(jnp.concatenate(index, axis=1).astype(jnp.int32), corners)
    return folded(mm(stacked(values), choice, NT))


def dense_kernel(slots, corners, tiles, maps, out):
    out[:, :corners] = dense(tiles[8:], maps[8:], slots, corners)
    out[:, corners:] = jnp.concatenate([tiles[:8], jnp.zeros((out.shape[0] - 8, TILE), F32)], axis=0)


def total_of(left, right, maps, slots, corners):
    if right.shape[1] == TILE:
        return left[:, :corners] + dense(right[8:], maps[8:], slots, corners), left[:8, corners:] + right[:8]
    return left[:, :corners] + right[:, :corners], left[:8, corners:] + right[:8, corners:]


def face_rows(rows):
    low = lax.broadcasted_iota(jnp.int32, rows.shape, 0) < rows.shape[0] // 2
    return jnp.concatenate([jnp.where(low, rows, 0.0), jnp.where(low, 0.0, rows)], axis=1)


def both_orders(first, second):
    count = first.shape[0]
    products = dots(jnp.concatenate([first, second], axis=0), jnp.concatenate([second, first], axis=0))
    return 0.5 * (products[:count, :count] + products[count:, count:])


def picked(solved, row):
    return folded(mm(stacked(solved), chosen(row.astype(jnp.int32), solved.shape[1]), NN))


def product_of(first, second):
    high, low = halves(second)
    return folded(mm(stacked(first), high, NN)) + mm(first.astype(BF16), low, NN)


def coarse_solve(corner_sum, parts):
    high, low = parts
    first = folded(mm(stacked(corner_sum), high, NN))
    return first + mm(corner_sum.astype(BF16), low, NN)


def start_kernel(
    count, rhs, signs, blocks, product, to_inner, to_outer, residual_out, sign_out, held, rhs_held, signs_held, sems,
):
    rows = held.shape[1]
    pieces = [(rhs, rhs_held), (signs, signs_held)]
    pieces += [(blocks.at[0, pl.ds(part * rows, rows)], held.at[part]) for part in range(held.shape[0])]
    copies = [pltpu.make_async_copy(*piece, sems.at[index]) for index, piece in enumerate(pieces)]
    for copy in copies:
        copy.start()
    blk = lax.axis_index("blk")
    even = blk % 2 == 0
    nrhs, width = product.shape
    half = width // 2
    live = live_mask(blk, count, width)
    copies[0].wait()
    copies[1].wait()
    sign = signs_held[...].astype(F32) * live
    residual = sign * rhs_held[0]
    rounded = residual.astype(BF16)
    sign_out[...] = sign
    residual_out[...] = residual
    total = jnp.zeros((nrhs, width), F32)
    for part, copy in enumerate(copies[2:]):
        copy.wait()
        total = total + mm(rounded[:, part * rows : (part + 1) * rows], held[part], NN)
    product[...] = total
    inner, outer = split(even, total[:, :half], total[:, half:])
    to_inner[...] = inner
    to_outer[...] = outer


def load_kernel(
    blocks, coupling, corner_map, after, out, couple_out, map_out, inner_extra, outer_extra, coupling_held, map_held, sems
):
    del after
    parts = sems.shape[0] - 2
    rows = out.shape[0] // parts
    pieces = [(corner_map, map_held), (coupling, coupling_held)]
    pieces += [(blocks.at[0, pl.ds(part * rows, rows)], out.at[pl.ds(part * rows, rows)]) for part in range(parts)]
    copies = [pltpu.make_async_copy(*piece, sems.at[index]) for index, piece in enumerate(pieces)]
    for copy in copies:
        copy.start()
    copies[0].wait()
    copies[1].wait()
    even = lax.axis_index("blk") % 2 == 0
    nrhs, half = inner_extra.shape
    couple = coupling_held[0]
    couple_out[...] = couple
    slots = couple.shape[0] // 2
    wide = couple.astype(F32)
    row = jnp.concatenate([map_held[...].astype(F32), jnp.zeros((1, half - 2 * slots), F32)], axis=1)
    map_out[...] = row[:, : map_out.shape[1]]
    fill = jnp.zeros((nrhs - slots - 1, half), F32)
    inner, outer = split(
        even,
        jnp.concatenate([wide[:slots], row, fill], axis=0),
        jnp.concatenate([wide[slots:], pltpu.roll(row, half - slots, 1), fill], axis=0),
    )
    inner_extra[...] = inner
    outer_extra[...] = outer
    for copy in copies[2:]:
        copy.wait()


def first_kernel(
    count, product, from_inner, from_outer, residual, blocks, couple, map_row, inner_extra, outer_extra,
    precond_out, image_out, tile_out, to_inner, to_outer,
):
    blk = lax.axis_index("blk")
    even = blk % 2 == 0
    nrhs, width = product.shape
    half = width // 2
    live = live_mask(blk, count, width)
    precond = live * (product[...] - joined(even, from_inner[...], from_outer[...]))
    image = mm(precond.astype(BF16), blocks[...], NN)
    precond_out[...] = precond
    image_out[...] = image
    grams = dots(
        jnp.concatenate([residual[...], precond, image], axis=0), jnp.concatenate([precond, image], axis=0)
    )
    slots = couple.shape[0]
    first = grams[:nrhs, :nrhs]
    second = 0.5 * (grams[nrhs : 2 * nrhs, nrhs:] + grams[2 * nrhs :, :nrhs])
    tile = tiles_of(
        even, corner_values(precond, couple[...]), map_row[:, :slots], first, second, jnp.zeros_like(first)
    )
    tile_out[...] = tile
    inner, outer = split(even, image[:, :half], image[:, half:])
    to_inner[:, :half] = inner
    to_outer[:, :half] = outer
    to_inner[:, half:width] = inner_extra[...]
    to_outer[:, half:] = outer_extra[...]
    to_inner[:, width:] = tile


def prepare_kernel(coarse, high, low):
    top, rest = halves(coarse[...])
    high[...] = top
    low[...] = rest


def follow_kernel(
    count, image, got, from_outer, couple, map_row, blocks,
    part_out, product_out, spread_out, columns_out, map_out, to_inner, to_outer,
):
    blk = lax.axis_index("blk")
    even = blk % 2 == 0
    nrhs, width = image.shape
    half = width // 2
    live = live_mask(blk, count, width)
    inner_got = got[...]
    outer_got = from_outer[...]
    part = live * (image[...] - joined(even, inner_got[:, :half], outer_got[:, :half]))
    beside = joined(even, inner_got[:, half:width], outer_got[:, half:])
    wide = couple[...].astype(F32)
    slots = wide.shape[0] // 2
    other = jnp.concatenate([beside[:slots, :half], beside[:slots, half:]], axis=0)
    columns = (live * jnp.concatenate([face_rows(wide), -face_rows(other)], axis=0)).astype(BF16)
    products = mm(jnp.concatenate([stacked(part), columns], axis=0), blocks[...].reshape(width, width), NN)
    product = products[:nrhs] + products[nrhs : 2 * nrhs]
    spread = products[2 * nrhs :]
    row = jnp.concatenate(
        [
            map_row[:, : 2 * slots],
            beside[slots : slots + 1, :slots],
            beside[slots : slots + 1, half : half + slots],
            jnp.full((1, map_row.shape[1] - 4 * slots), -1.0, F32),
        ],
        axis=1,
    )
    part_out[...] = part
    product_out[...] = product
    spread_out[...] = spread
    columns_out[...] = columns
    map_out[...] = row
    count_rows = nrhs + 4 * slots
    rows = jnp.concatenate([product, spread], axis=0)
    to_inner[:count_rows, :], to_outer[:count_rows, :] = split(even, rows[:, :half], rows[:, half:])
    last = jnp.concatenate([row, jnp.zeros((1, half - row.shape[1]), F32)], axis=1)
    last = jnp.broadcast_to(last, (to_inner.shape[0] - count_rows, half))
    to_inner[count_rows:, :] = last
    to_outer[count_rows:, :] = last


def middle_kernel(
    count, corners, left, right, maps, from_inner, from_outer, part, product, spread, columns, map_row,
    precond_in, image_in, residual_in, blocks, couple, coarse_high, coarse_low,
    solved_out, residual_out, whole_out, precond_out, image_out, small_out, tile_out, to_inner, to_outer,
):
    blk = lax.axis_index("blk")
    even = blk % 2 == 0
    nrhs, width = part.shape
    half = width // 2
    live = live_mask(blk, count, width)
    slots = couple.shape[0]
    corner_sum, squares = total_of(left, right, maps, slots, corners)
    gram, energy, _ = untile(squares)
    solved = coarse_solve(corner_sum, (coarse_high[...], coarse_low[...]))
    energy = energy + both_orders(corner_sum, solved)
    unit = (lax.broadcasted_iota(jnp.int32, (nrhs, nrhs), 0) == lanes_of((nrhs, nrhs))).astype(F32)
    both = eliminate(jnp.stack([2.0 * energy, symmetric(gram)]), jnp.stack([gram, unit]))
    alpha, inverse = transposed(both[0]), both[1]

    rows = spread.shape[0]
    wide = map_row.shape[1]
    inner_got, outer_got = from_inner[...], from_outer[...]
    sides = [jnp.where(even, outer_got, inner_got), jnp.where(even, inner_got, outer_got)]
    index = jnp.concatenate([map_row[...]] + [side[nrhs + rows : nrhs + rows + 1, :wide] for side in sides], axis=1)
    at = picked(solved, index)
    whole = part[...] + against(at[:, :rows], columns[...])
    own = product[...] + product_of(at[:, :rows], spread[...])
    others = [
        side[:nrhs] + product_of(at[:, wide * turn : wide * turn + rows], side[nrhs : nrhs + rows])
        for turn, side in enumerate(sides, 1)
    ]
    change = live * (own - jnp.concatenate(others, axis=1))
    change = product_of(alpha, jnp.concatenate([whole, change], axis=1))
    residual = residual_in[...] - change[:, :width]
    precond = precond_in[...] - change[:, width:]

    image = mm(precond.astype(BF16), blocks[...], NN)
    left = jnp.concatenate([residual, precond, precond_in[...], image_in[...]], axis=0)
    grams = dots(left, jnp.concatenate([precond, image], axis=0))
    tile = tiles_of(
        even,
        corner_values(precond, couple[...]),
        jnp.zeros((1, slots), F32),
        grams[:nrhs, :nrhs],
        grams[nrhs : 2 * nrhs, nrhs:],
        grams[2 * nrhs : 3 * nrhs, nrhs:] + grams[3 * nrhs :, :nrhs],
    )
    tile_out[...] = tile
    inner, outer = split(even, image[:, :half], image[:, half:])
    to_inner[:, :half] = inner
    to_inner[:, half:] = tile
    to_outer[...] = outer
    solved_out[...] = solved
    residual_out[...] = residual
    whole_out[...] = whole
    precond_out[...] = precond
    image_out[...] = image
    small_out[...] = jnp.concatenate([inverse, energy, alpha, jnp.zeros((nrhs, 128 - 3 * nrhs), F32)], axis=1)


def assemble_kernel(count, image, got, from_outer, small, old_precond, part_out, first_out):
    blk = lax.axis_index("blk")
    nrhs, width = image.shape
    image_beside = joined(blk % 2 == 0, got[:, : width // 2], from_outer[...])
    part_out[...] = live_mask(blk, count, width) * (image[...] - image_beside)
    first_out[...] = product_of(small[:, 2 * nrhs : 3 * nrhs], old_precond[...])


def final_kernel(
    corners, left, right, maps, part, first, precond, residual, old_precond, old_image,
    old_solved, small, columns, map_row, sign, coarse_high, coarse_low,
    multipliers_out, residual_out,
):
    nrhs, width = precond.shape
    slots = columns.shape[0] // 2
    corner_sum, squares = total_of(left, right, maps, slots, corners)
    gram, new_new, old_new = untile(squares)
    inverse, old_old = small[:, :nrhs], small[:, nrhs : 2 * nrhs]
    beta = product_of(inverse, gram)
    turned = product_of(transposed(gram), inverse)
    solved = coarse_solve(corner_sum, (coarse_high[...], coarse_low[...]))
    old_new = old_new + product_of(old_old, beta) + 2.0 * dots(old_solved[...], corner_sum)
    energy = symmetric(new_new + product_of(turned, old_new)) + both_orders(corner_sum, solved)
    alpha = transposed(eliminate(2.0 * energy[None], gram[None])[0])
    at = picked(solved, map_row[...])
    whole = part[...] + against(at[:, : columns.shape[0]], columns[...])
    carried = product_of(turned, jnp.concatenate([old_precond[...], old_image[...]], axis=1))
    change = product_of(alpha, jnp.concatenate([precond[...], whole], axis=1) + carried)
    multipliers_out[0] = sign[...] * (first[...] + change[:, :width])
    residual_out[0] = sign[...] * (residual[...] - change[:, width:])


VMEM = pl.BlockSpec(memory_space=pltpu.VMEM)
HBM = pl.BlockSpec(memory_space=pltpu.HBM)


def call(body, shapes, *args, specs=None, scratch=(), flops=0):
    shapes = [jax.ShapeDtypeStruct(shape, dtype) for shape, dtype in shapes]
    moved = sum(arg.size * arg.dtype.itemsize for arg in args)
    return pl.pallas_call(
        body,
        out_shape=shapes,
        in_specs=specs or [VMEM] * len(args),
        out_specs=[VMEM] * len(shapes),
        scratch_shapes=list(scratch),
        compiler_params=pltpu.CompilerParams(vmem_limit_bytes=16 << 20),
        cost_estimate=pl.CostEstimate(flops=flops, bytes_accessed=moved, transcendentals=0),
    )(*args)


def local(count, groups, dual_rhs, dual_ops, prec_ops, corner_coupling, corner_map, signs, coarse_inverse):
    nrhs, width = dual_rhs.shape[1:]
    half = width // 2
    corners = coarse_inverse.shape[0]
    inner, outer = inner_pairs(count, groups), outer_pairs(count, groups)
    steps = rotations(count, groups)
    dense_shape = ((nrhs, corners + TILE), F32)
    slots = corner_map.shape[1]
    flops = 2 * nrhs * width * width

    def permute(values, pairs):
        return lax.ppermute(values, AXES, pairs)

    def exchange(to_inner, to_outer):
        from_outer = permute(to_outer, outer)
        return permute(to_inner, inner), from_outer

    def densify(tiles, maps):
        body = functools.partial(dense_kernel, slots, corners)
        return call(body, [dense_shape], tiles, maps, flops=flops)[0]

    def united(parts):
        if parts[0].shape[1] != TILE:
            return sum(parts[1:], parts[0])
        squares = [part[:8] for part in parts]
        return jnp.concatenate([sum(squares[1:], squares[0])] + [part[8:] for part in parts], axis=0)

    def region(tile, to_inner, to_outer, follow, maps=None):
        from_outer = permute(to_outer, outer)
        got = permute(to_inner, inner)
        values = tile + got[:, got.shape[1] - TILE :]
        known = maps
        left, right = None, None
        for index, turns in enumerate(steps):
            if index > 0:
                held = left.shape[0] + right.shape[0] - 16
                if left.shape[1] == TILE and 8 * MOST < 2 * held * (1 + len(turns)):
                    known = known or (left, right)
                    left, right = densify(left, known[0]), densify(right, known[1])
                values = united([left, right])
            if index == max(len(steps) - 2, 0):
                result, sends = follow(got, from_outer)
                values, result, sends = lax.optimization_barrier((values, result, sends))
                result = (*(exchange(*sends) if sends else ()), *result)
            left = values
            right = united([permute(values, pairs) for pairs in turns])
        known = known or (left, right)
        if left.shape[1] == TILE:
            left = densify(left, known[0])
        return known, (left, right, known[1], *result)

    wide = ((nrhs, width), F32)
    face = ((nrhs, half), F32)
    pieces = 4
    in_hbm = functools.partial(pltpu.with_memory_space_constraint, memory_space=pltpu.HBM)
    coupling_shape, map_shape = corner_coupling.shape, corner_map.shape
    product, to_inner, to_outer, residual0, sign, held = call(
        functools.partial(start_kernel, count),
        [wide, face, face, wide, ((1, width), F32), ((pieces, width // pieces, width), BF16)],
        in_hbm(dual_rhs), in_hbm(signs), in_hbm(prec_ops),
        specs=[HBM] * 3,
        scratch=[
            pltpu.VMEM(dual_rhs.shape, F32),
            pltpu.VMEM(signs.shape, jnp.int32),
            pltpu.SemaphoreType.DMA((pieces + 2,)),
        ],
        flops=flops,
    )
    loaded, couple, map_row, *extras = call(
        load_kernel,
        [((width, width), BF16), (coupling_shape[1:], BF16), ((1, 128), F32), face, face],
        in_hbm(dual_ops), in_hbm(corner_coupling), in_hbm(corner_map), sign,
        specs=[HBM] * 3 + [VMEM],
        scratch=[
            pltpu.VMEM(coupling_shape, BF16),
            pltpu.VMEM(map_shape, jnp.int32),
            pltpu.SemaphoreType.DMA((pieces + 2,)),
        ],
    )
    tile_shape = ((nrhs, TILE), F32)
    precond0, image0, tile, to_inner, to_outer = call(
        functools.partial(first_kernel, count),
        [wide, wide, tile_shape, ((nrhs, width + TILE), F32), wide],
        product, *exchange(to_inner, to_outer), residual0, loaded, couple, map_row, *extras,
        flops=flops,
    )
    square = ((corners, corners), BF16)
    coarse_parts = call(prepare_kernel, [square, square], coarse_inverse, flops=corners * corners)
    rows = nrhs + 2 * slots + 8

    def follow(got, from_outer):
        *kept, to_inner, to_outer = call(
            functools.partial(follow_kernel, count),
            [
                wide, wide, ((2 * slots, width), F32), ((2 * slots, width), BF16), ((1, 128), F32),
                ((rows, half), F32), ((rows, half), F32),
            ],
            image0, got, from_outer, couple, map_row, held,
            flops=5 * flops,
        )
        return tuple(kept), (to_inner, to_outer)

    def assemble(got, from_outer):
        body = functools.partial(assemble_kernel, count)
        return tuple(call(body, [wide, wide], image1, got, from_outer, small, precond0, flops=5 * flops)), ()

    maps, gathered = region(tile, to_inner, to_outer, follow)
    columns, index = gathered[-2:]
    solved0, residual1, whole0, precond1, image1, small, tile, to_inner, to_outer = call(
        functools.partial(middle_kernel, count, corners),
        [((nrhs, corners), F32), wide, wide, wide, wide, ((nrhs, 128), F32), tile_shape, ((nrhs, half + TILE), F32), face],
        *gathered, precond0, image0, residual0, loaded, couple, *coarse_parts,
        flops=flops,
    )
    _, gathered = region(tile, to_inner, to_outer, assemble, maps)
    whole_out = ((1, nrhs, width), F32)
    return tuple(
        call(
            functools.partial(final_kernel, corners),
            [whole_out, whole_out],
            *gathered, precond1, residual1, precond0, whole0, solved0, small,
            columns, index, sign, *coarse_parts,
            flops=flops,
        )
    )


def solution(mesh):
    in_specs = (
        P("grp", None, "blk"),
        P("grp", "blk", None),
        P("grp", "blk", None),
        P("grp", "blk", None),
        P("grp", "blk"),
        P("grp", "blk"),
        P(),
    )
    out_specs = (P("grp", None, "blk"), P("grp", None, "blk"))
    return jax.shard_map(
        functools.partial(local, mesh.shape["blk"], mesh.shape["grp"]),
        mesh=mesh,
        in_specs=in_specs,
        out_specs=out_specs,
        check_vma=False,
    )
```

```python
import functools

import jax
import jax.numpy as jnp
from jax import lax
from jax.experimental import pallas as pl
from jax.experimental.pallas import tpu as pltpu
from jax.sharding import PartitionSpec as P

AXES = ("blk", "grp")
NN = (((1,), (0,)), ((), ()))
NT = (((1,), (1,)), ((), ()))
F32 = jnp.float32
BF16 = jnp.bfloat16


def radices(count):
    found = []
    factor = 2
    while count > 1:
        while count % factor == 0:
            found.append(factor)
            count //= factor
        factor += 1
    return found


def swap(count, groups, partner):
    pairs = []
    for blk in range(count):
        for grp in range(groups):
            other = partner(blk)
            if 0 <= other < count:
                target = other * groups + grp
            elif grp ^ 1 < groups:
                target = blk * groups + (grp ^ 1)
            else:
                target = blk * groups + grp
            pairs.append((blk * groups + grp, target))
    return pairs


def inner_pairs(count, groups):
    return swap(count, groups, lambda blk: blk ^ 1)


def outer_pairs(count, groups):
    return swap(count, groups, lambda blk: blk + 1 if blk % 2 == 1 else blk - 1)


def rotations(count, groups):
    core = 2 if count % 2 == 0 else 1
    steps = []

    def flipped(blk, turn):
        return (blk ^ 1) if (core == 2 and turn) else blk

    def add_axis(step_target, factor):
        steps.append(
            [
                [
                    (blk * groups + grp, step_target(blk, grp, turn))
                    for blk in range(count)
                    for grp in range(groups)
                ]
                for turn in range(1, factor)
            ]
        )

    stride = 1
    blk_steps = []
    for factor in radices(count // core):
        blk_steps.append((stride, factor))
        stride *= factor
    grp_steps = []
    stride = 1
    for factor in radices(groups):
        grp_steps.append((stride, factor))
        stride *= factor

    def blk_target(stride, factor):
        def target(blk, grp, turn):
            chip = blk // core
            digit = (chip // stride) % factor
            moved = chip + ((digit + turn) % factor - digit) * stride
            return flipped(moved * core + blk % core, turn) * groups + grp

        return target

    def grp_target(stride, factor):
        def target(blk, grp, turn):
            digit = (grp // stride) % factor
            moved = grp + ((digit + turn) % factor - digit) * stride
            return flipped(blk, turn) * groups + moved

        return target

    for stride, factor in grp_steps:
        add_axis(grp_target(stride, factor), factor)
    for stride, factor in blk_steps:
        add_axis(blk_target(stride, factor), factor)
    return steps


def mm(first, second, dims):
    return lax.dot_general(first, second, dims, preferred_element_type=F32)


def halves(values):
    high = values.astype(BF16)
    return high, (values - high.astype(F32)).astype(BF16)


def stacked(values):
    return jnp.concatenate(halves(values), axis=0)


def folded(rows):
    count = rows.shape[0] // 2
    return rows[:count] + rows[count:]


def dots(first, second):
    product = folded(mm(stacked(first), stacked(second), NT))
    count = second.shape[0]
    return product[:, :count] + product[:, count:]


def against(values, exact):
    return folded(mm(stacked(values), exact, NN))


def lanes_of(shape):
    return lax.broadcasted_iota(jnp.int32, shape, len(shape) - 1)


def chosen(row, corners):
    shape = (corners, row.shape[1])
    return (lax.broadcasted_iota(jnp.int32, shape, 0) == row).astype(BF16)


def live_mask(blk, count, width):
    lane = lanes_of((1, width))
    low = (blk > 0).astype(F32)
    up = (blk < count - 1).astype(F32)
    return jnp.where(lane < width // 2, low, up)


def split(even, low, up):
    return jnp.where(even, up, low), jnp.where(even, low, up)


def joined(even, from_inner, from_outer):
    low = jnp.where(even, from_outer, from_inner)
    up = jnp.where(even, from_inner, from_outer)
    return jnp.concatenate([low, up], axis=1)


def transposed(matrix):
    return matrix.T


def eliminate(matrix, target, guide):
    count = matrix.shape[1]
    row_index = lax.broadcasted_iota(jnp.int32, (1, count, 1), 1)
    column_index = lax.broadcasted_iota(jnp.int32, (1, count, count), 2)
    diagonal = jnp.where(row_index == column_index, guide, 0.0)
    scale = lax.rsqrt(jnp.sum(diagonal, axis=2, keepdims=True))
    both = scale * lax.rsqrt(jnp.sum(diagonal, axis=1, keepdims=True))
    work = jnp.concatenate([matrix * both, target * scale], axis=2)
    size = 8
    for start in range(0, count, size):
        at = [start + index for index in range(size)]
        columns = [jnp.broadcast_to(work[:, :, k : k + 1], work.shape) for k in at]
        pivot = [[column[:, k : k + 1] for column in columns] for k in at]
        rows = [work[:, k : k + 1] for k in at]
        for one in range(0, size, 2):
            two = one + 1
            a, b, c, d = pivot[one][one], pivot[one][two], pivot[two][one], pivot[two][two]
            inverse = 1.0 / (a * d - b * c)
            for j in range(two + 1, size):
                p, q = pivot[one][j], pivot[two][j]
                pivot[one][j], pivot[two][j] = (d * p - b * q) * inverse, (a * q - c * p) * inverse
            p, q = rows[one], rows[two]
            rows[one], rows[two] = (d * p - b * q) * inverse, (a * q - c * p) * inverse
            for i in range(size):
                if i not in (one, two):
                    left, right = pivot[i][one], pivot[i][two]
                    for j in range(two + 1, size):
                        pivot[i][j] = pivot[i][j] - left * pivot[one][j] - right * pivot[two][j]
                    rows[i] = rows[i] - left * rows[one] - right * rows[two]
        products = [column * row for column, row in zip(columns, rows)]
        while len(products) > 1:
            products = [one + two for one, two in zip(products[::2], products[1::2])]
        work = work - products[0]
        for k, row in zip(at, rows):
            work = jnp.where(row_index == k, row, work)
    return work[:, :, count:] * scale


def symmetric(matrix):
    return 0.5 * (matrix + transposed(matrix))


def corner_values(values, couple):
    half = values.shape[1] // 2
    both = stacked(values)
    low = folded(mm(both[:, :half], couple, NT))
    up = folded(mm(both[:, half:], couple, NT))
    return jnp.where(lanes_of(low.shape) < couple.shape[0] // 2, low, up)


TILE = 128
GROUP = 32
MOST = 32


def abreast(rows):
    half = rows.shape[0] // 2
    return [rows[:half], rows[half:]]


def tiles_of(even, corner, index, first, second, third):
    half = first.shape[0] // 2
    squares = abreast(first) + abreast(second) + abreast(third)
    used = sum(part.shape[1] for part in squares)
    squares = jnp.concatenate(squares + [jnp.zeros((half, TILE - used), F32)], axis=1)
    values = abreast(corner)
    gap = jnp.zeros((half, 2 * corner.shape[1]), F32)
    left, right = jnp.concatenate(values + [gap], axis=1), jnp.concatenate([gap] + values, axis=1)
    row = lax.broadcasted_iota(jnp.int32, (half, index.shape[1]), 0)
    index = jnp.where(row == jnp.where(even, 0, 1), index, 0.0)
    rest = jnp.zeros((half, TILE - left.shape[1] - index.shape[1]), F32)
    return jnp.concatenate(
        [squares, jnp.concatenate([jnp.where(even, left, right), index, rest], axis=1)], axis=0
    )


def untile(tile):
    count = 2 * tile.shape[0]
    return [
        jnp.concatenate([tile[:, at : at + count], tile[:, at + count : at + 2 * count]], axis=0)
        for at in (0, 2 * count, 4 * count)
    ]


def dense(tiles, maps, slots, corners):
    count = tiles.shape[0] // 8
    lane = lanes_of((1, TILE))
    low, up, index = [], [], []

    def moved(rows, at, to):
        shift = (to - at) % TILE
        return pltpu.roll(rows, shift, 1) if shift else rows

    for start in range(0, count, TILE // GROUP // 2):
        parts = [jnp.zeros((8, TILE), F32), jnp.zeros((8, TILE), F32), jnp.full((1, TILE), -1.0, F32)]
        for turn in range(TILE // GROUP):
            at, core = start + turn // 2, turn % 2
            if at < count:
                here = (lane // GROUP == turn) & (lane % GROUP < slots)
                tile = tiles[8 * at : 8 * at + 8]
                name = maps[8 * at + core : 8 * at + core + 1]
                new = [
                    moved(tile, 2 * slots * core, GROUP * turn),
                    moved(tile, 2 * slots * core + slots, GROUP * turn),
                    moved(name, 4 * slots, GROUP * turn),
                ]
                parts = [jnp.where(here, one, old) for one, old in zip(new, parts)]
        low.append(parts[0])
        up.append(parts[1])
        index.append(parts[2])
    values = jnp.concatenate([jnp.concatenate(low, axis=1), jnp.concatenate(up, axis=1)], axis=0)
    choice = chosen(jnp.concatenate(index, axis=1).astype(jnp.int32), corners)
    return folded(mm(stacked(values), choice, NT))


def dense_kernel(slots, corners, tiles, maps, out):
    out[:, :corners] = dense(tiles[8:], maps[8:], slots, corners)
    out[:, corners:] = jnp.concatenate([tiles[:8], jnp.zeros((out.shape[0] - 8, TILE), F32)], axis=0)


def total_of(left, right, maps, slots, corners):
    if right.shape[1] == TILE:
        return left[:, :corners] + dense(right[8:], maps[8:], slots, corners), left[:8, corners:] + right[:8]
    return left[:, :corners] + right[:, :corners], left[:8, corners:] + right[:8, corners:]


def face_rows(rows):
    low = lax.broadcasted_iota(jnp.int32, rows.shape, 0) < rows.shape[0] // 2
    return jnp.concatenate([jnp.where(low, rows, 0.0), jnp.where(low, 0.0, rows)], axis=1)


def both_orders(first, second):
    count = first.shape[0]
    products = dots(jnp.concatenate([first, second], axis=0), jnp.concatenate([second, first], axis=0))
    return 0.5 * (products[:count, :count] + products[count:, count:])


def picked(solved, row):
    return folded(mm(stacked(solved), chosen(row.astype(jnp.int32), solved.shape[1]), NN))


def product_of(first, second):
    high, low = halves(second)
    return folded(mm(stacked(first), high, NN)) + mm(first.astype(BF16), low, NN)


def coarse_solve(corner_sum, parts):
    high, low = parts
    first = folded(mm(stacked(corner_sum), high, NN))
    return first + mm(corner_sum.astype(BF16), low, NN)


def start_kernel(
    count, rhs, signs, blocks, product, to_inner, to_outer, residual_out, sign_out, held, rhs_held, signs_held, sems,
):
    rows = held.shape[1]
    pieces = [(rhs, rhs_held), (signs, signs_held)]
    pieces += [(blocks.at[0, pl.ds(part * rows, rows)], held.at[part]) for part in range(held.shape[0])]
    copies = [pltpu.make_async_copy(*piece, sems.at[index]) for index, piece in enumerate(pieces)]
    for copy in copies:
        copy.start()
    blk = lax.axis_index("blk")
    even = blk % 2 == 0
    nrhs, width = product.shape
    half = width // 2
    live = live_mask(blk, count, width)
    copies[0].wait()
    copies[1].wait()
    sign = signs_held[...].astype(F32) * live
    residual = sign * rhs_held[0]
    rounded = residual.astype(BF16)
    sign_out[...] = sign
    residual_out[...] = residual
    total = jnp.zeros((nrhs, width), F32)
    for part, copy in enumerate(copies[2:]):
        copy.wait()
        total = total + mm(rounded[:, part * rows : (part + 1) * rows], held[part], NN)
    product[...] = total
    inner, outer = split(even, total[:, :half], total[:, half:])
    to_inner[...] = inner
    to_outer[...] = outer


def load_kernel(
    blocks, coupling, corner_map, after, out, couple_out, map_out, inner_extra, outer_extra, coupling_held, map_held, sems
):
    del after
    parts = sems.shape[0] - 2
    rows = out.shape[0] // parts
    pieces = [(corner_map, map_held), (coupling, coupling_held)]
    pieces += [(blocks.at[0, pl.ds(part * rows, rows)], out.at[pl.ds(part * rows, rows)]) for part in range(parts)]
    copies = [pltpu.make_async_copy(*piece, sems.at[index]) for index, piece in enumerate(pieces)]
    for copy in copies:
        copy.start()
    copies[0].wait()
    copies[1].wait()
    even = lax.axis_index("blk") % 2 == 0
    nrhs, half = inner_extra.shape
    couple = coupling_held[0]
    couple_out[...] = couple
    slots = couple.shape[0] // 2
    wide = couple.astype(F32)
    row = jnp.concatenate([map_held[...].astype(F32), jnp.zeros((1, half - 2 * slots), F32)], axis=1)
    map_out[...] = row[:, : map_out.shape[1]]
    fill = jnp.zeros((nrhs - slots - 1, half), F32)
    inner, outer = split(
        even,
        jnp.concatenate([wide[:slots], row, fill], axis=0),
        jnp.concatenate([wide[slots:], pltpu.roll(row, half - slots, 1), fill], axis=0),
    )
    inner_extra[...] = inner
    outer_extra[...] = outer
    for copy in copies[2:]:
        copy.wait()


def first_kernel(
    count, product, from_inner, from_outer, residual, blocks, couple, map_row, inner_extra, outer_extra,
    precond_out, image_out, tile_out, to_inner, to_outer,
):
    blk = lax.axis_index("blk")
    even = blk % 2 == 0
    nrhs, width = product.shape
    half = width // 2
    live = live_mask(blk, count, width)
    precond = live * (product[...] - joined(even, from_inner[...], from_outer[...]))
    image = mm(precond.astype(BF16), blocks[...], NN)
    precond_out[...] = precond
    image_out[...] = image
    grams = dots(
        jnp.concatenate([residual[...], precond, image], axis=0), jnp.concatenate([precond, image], axis=0)
    )
    slots = couple.shape[0]
    first = grams[:nrhs, :nrhs]
    second = 0.5 * (grams[nrhs : 2 * nrhs, nrhs:] + grams[2 * nrhs :, :nrhs])
    tile = tiles_of(
        even, corner_values(precond, couple[...]), map_row[:, :slots], first, second, jnp.zeros_like(first)
    )
    tile_out[...] = tile
    inner, outer = split(even, image[:, :half], image[:, half:])
    to_inner[:, :half] = inner
    to_outer[:, :half] = outer
    to_inner[:, half:width] = inner_extra[...]
    to_outer[:, half:] = outer_extra[...]
    to_inner[:, width:] = tile


def prepare_kernel(coarse, high, low):
    top, rest = halves(coarse[...])
    high[...] = top
    low[...] = rest


def follow_kernel(
    count, image, got, from_outer, couple, map_row, blocks,
    part_out, product_out, spread_out, columns_out, map_out, to_inner, to_outer,
):
    blk = lax.axis_index("blk")
    even = blk % 2 == 0
    nrhs, width = image.shape
    half = width // 2
    live = live_mask(blk, count, width)
    inner_got = got[...]
    outer_got = from_outer[...]
    part = live * (image[...] - joined(even, inner_got[:, :half], outer_got[:, :half]))
    beside = joined(even, inner_got[:, half:width], outer_got[:, half:])
    wide = couple[...].astype(F32)
    slots = wide.shape[0] // 2
    other = jnp.concatenate([beside[:slots, :half], beside[:slots, half:]], axis=0)
    columns = (live * jnp.concatenate([face_rows(wide), -face_rows(other)], axis=0)).astype(BF16)
    products = mm(jnp.concatenate([stacked(part), columns], axis=0), blocks[...].reshape(width, width), NN)
    product = products[:nrhs] + products[nrhs : 2 * nrhs]
    spread = products[2 * nrhs :]
    row = jnp.concatenate(
        [
            map_row[:, : 2 * slots],
            beside[slots : slots + 1, :slots],
            beside[slots : slots + 1, half : half + slots],
            jnp.full((1, map_row.shape[1] - 4 * slots), -1.0, F32),
        ],
        axis=1,
    )
    part_out[...] = part
    product_out[...] = product
    spread_out[...] = spread
    columns_out[...] = columns
    map_out[...] = row
    count_rows = nrhs + 4 * slots
    rows = jnp.concatenate([product, spread], axis=0)
    to_inner[:count_rows, :], to_outer[:count_rows, :] = split(even, rows[:, :half], rows[:, half:])
    last = jnp.concatenate([row, jnp.zeros((1, half - row.shape[1]), F32)], axis=1)
    last = jnp.broadcast_to(last, (to_inner.shape[0] - count_rows, half))
    to_inner[count_rows:, :] = last
    to_outer[count_rows:, :] = last


def middle_kernel(
    count, corners, left, right, maps, from_inner, from_outer, part, product, spread, columns, map_row,
    precond_in, image_in, residual_in, blocks, couple, coarse_high, coarse_low,
    solved_out, residual_out, whole_out, precond_out, image_out, small_out, tile_out, to_inner, to_outer,
):
    blk = lax.axis_index("blk")
    even = blk % 2 == 0
    nrhs, width = part.shape
    half = width // 2
    live = live_mask(blk, count, width)
    slots = couple.shape[0]
    corner_sum, squares = total_of(left, right, maps, slots, corners)
    gram, local_energy, _ = untile(squares)
    solved = coarse_solve(corner_sum, (coarse_high[...], coarse_low[...]))
    energy = local_energy + both_orders(corner_sum, solved)
    unit = (lax.broadcasted_iota(jnp.int32, (nrhs, nrhs), 0) == lanes_of((nrhs, nrhs))).astype(F32)
    old = symmetric(gram)
    both = eliminate(
        jnp.stack([2.0 * energy, old]), jnp.stack([gram, unit]), jnp.stack([2.0 * local_energy, old])
    )
    alpha, inverse = transposed(both[0]), both[1]

    rows = spread.shape[0]
    wide = map_row.shape[1]
    inner_got, outer_got = from_inner[...], from_outer[...]
    sides = [jnp.where(even, outer_got, inner_got), jnp.where(even, inner_got, outer_got)]
    index = jnp.concatenate([map_row[...]] + [side[nrhs + rows : nrhs + rows + 1, :wide] for side in sides], axis=1)
    at = picked(solved, index)
    whole = part[...] + against(at[:, :rows], columns[...])
    own = product[...] + product_of(at[:, :rows], spread[...])
    others = [
        side[:nrhs] + product_of(at[:, wide * turn : wide * turn + rows], side[nrhs : nrhs + rows])
        for turn, side in enumerate(sides, 1)
    ]
    change = live * (own - jnp.concatenate(others, axis=1))
    change = product_of(alpha, jnp.concatenate([whole, change], axis=1))
    residual = residual_in[...] - change[:, :width]
    precond = precond_in[...] - change[:, width:]

    image = mm(precond.astype(BF16), blocks[...], NN)
    left = jnp.concatenate([residual, precond, precond_in[...], image_in[...]], axis=0)
    grams = dots(left, jnp.concatenate([precond, image], axis=0))
    tile = tiles_of(
        even,
        corner_values(precond, couple[...]),
        jnp.zeros((1, slots), F32),
        grams[:nrhs, :nrhs],
        grams[nrhs : 2 * nrhs, nrhs:],
        grams[2 * nrhs : 3 * nrhs, nrhs:] + grams[3 * nrhs :, :nrhs],
    )
    tile_out[...] = tile
    inner, outer = split(even, image[:, :half], image[:, half:])
    to_inner[:, :half] = inner
    to_inner[:, half:] = tile
    to_outer[...] = outer
    solved_out[...] = solved
    residual_out[...] = residual
    whole_out[...] = whole
    precond_out[...] = precond
    image_out[...] = image
    small_out[...] = jnp.concatenate([inverse, energy, alpha, jnp.zeros((nrhs, 128 - 3 * nrhs), F32)], axis=1)


def assemble_kernel(count, image, got, from_outer, small, old_precond, part_out, first_out):
    blk = lax.axis_index("blk")
    nrhs, width = image.shape
    image_beside = joined(blk % 2 == 0, got[:, : width // 2], from_outer[...])
    part_out[...] = live_mask(blk, count, width) * (image[...] - image_beside)
    first_out[...] = product_of(small[:, 2 * nrhs : 3 * nrhs], old_precond[...])


def final_kernel(
    corners, left, right, maps, part, first, precond, residual, old_precond, old_image,
    old_solved, small, columns, map_row, sign, coarse_high, coarse_low,
    multipliers_out, residual_out,
):
    nrhs, width = precond.shape
    slots = columns.shape[0] // 2
    corner_sum, squares = total_of(left, right, maps, slots, corners)
    gram, new_new, old_new = untile(squares)
    inverse, old_old = small[:, :nrhs], small[:, nrhs : 2 * nrhs]
    beta = product_of(inverse, gram)
    turned = product_of(transposed(gram), inverse)
    solved = coarse_solve(corner_sum, (coarse_high[...], coarse_low[...]))
    old_new = old_new + product_of(old_old, beta) + 2.0 * dots(old_solved[...], corner_sum)
    energy = symmetric(new_new + product_of(turned, old_new)) + both_orders(corner_sum, solved)
    alpha = transposed(eliminate(2.0 * energy[None], gram[None], 2.0 * new_new[None])[0])
    at = picked(solved, map_row[...])
    whole = part[...] + against(at[:, : columns.shape[0]], columns[...])
    carried = product_of(turned, jnp.concatenate([old_precond[...], old_image[...]], axis=1))
    change = product_of(alpha, jnp.concatenate([precond[...], whole], axis=1) + carried)
    multipliers_out[0] = sign[...] * (first[...] + change[:, :width])
    residual_out[0] = sign[...] * (residual[...] - change[:, width:])


VMEM = pl.BlockSpec(memory_space=pltpu.VMEM)
HBM = pl.BlockSpec(memory_space=pltpu.HBM)


def call(body, shapes, *args, specs=None, scratch=(), flops=0):
    shapes = [jax.ShapeDtypeStruct(shape, dtype) for shape, dtype in shapes]
    moved = sum(arg.size * arg.dtype.itemsize for arg in args)
    return pl.pallas_call(
        body,
        out_shape=shapes,
        in_specs=specs or [VMEM] * len(args),
        out_specs=[VMEM] * len(shapes),
        scratch_shapes=list(scratch),
        compiler_params=pltpu.CompilerParams(vmem_limit_bytes=16 << 20),
        cost_estimate=pl.CostEstimate(flops=flops, bytes_accessed=moved, transcendentals=0),
    )(*args)


def local(count, groups, dual_rhs, dual_ops, prec_ops, corner_coupling, corner_map, signs, coarse_inverse):
    nrhs, width = dual_rhs.shape[1:]
    half = width // 2
    corners = coarse_inverse.shape[0]
    inner, outer = inner_pairs(count, groups), outer_pairs(count, groups)
    steps = rotations(count, groups)
    dense_shape = ((nrhs, corners + TILE), F32)
    slots = corner_map.shape[1]
    flops = 2 * nrhs * width * width

    def permute(values, pairs):
        return lax.ppermute(values, AXES, pairs)

    def exchange(to_inner, to_outer):
        from_outer = permute(to_outer, outer)
        return permute(to_inner, inner), from_outer

    def densify(tiles, maps):
        body = functools.partial(dense_kernel, slots, corners)
        return call(body, [dense_shape], tiles, maps, flops=flops)[0]

    def united(parts):
        if parts[0].shape[1] != TILE:
            return sum(parts[1:], parts[0])
        squares = [part[:8] for part in parts]
        return jnp.concatenate([sum(squares[1:], squares[0])] + [part[8:] for part in parts], axis=0)

    def region(tile, to_inner, to_outer, follow, maps=None):
        from_outer = permute(to_outer, outer)
        got = permute(to_inner, inner)
        values = tile + got[:, got.shape[1] - TILE :]
        known = maps
        left, right = None, None
        for index, turns in enumerate(steps):
            if index > 0:
                held = left.shape[0] + right.shape[0] - 16
                if left.shape[1] == TILE and 8 * MOST < 2 * held * (1 + len(turns)):
                    known = known or (left, right)
                    left, right = densify(left, known[0]), densify(right, known[1])
                values = united([left, right])
            if index == max(len(steps) - 2, 0):
                result, sends = follow(got, from_outer)
                values, result, sends = lax.optimization_barrier((values, result, sends))
                result = (*(exchange(*sends) if sends else ()), *result)
            left = values
            right = united([permute(values, pairs) for pairs in turns])
        known = known or (left, right)
        if left.shape[1] == TILE:
            left = densify(left, known[0])
        return known, (left, right, known[1], *result)

    wide = ((nrhs, width), F32)
    face = ((nrhs, half), F32)
    pieces = 8
    in_hbm = functools.partial(pltpu.with_memory_space_constraint, memory_space=pltpu.HBM)
    coupling_shape, map_shape = corner_coupling.shape, corner_map.shape
    product, to_inner, to_outer, residual0, sign, held = call(
        functools.partial(start_kernel, count),
        [wide, face, face, wide, ((1, width), F32), ((pieces, width // pieces, width), BF16)],
        in_hbm(dual_rhs), in_hbm(signs), in_hbm(prec_ops),
        specs=[HBM] * 3,
        scratch=[
            pltpu.VMEM(dual_rhs.shape, F32),
            pltpu.VMEM(signs.shape, jnp.int32),
            pltpu.SemaphoreType.DMA((pieces + 2,)),
        ],
        flops=flops,
    )
    loaded, couple, map_row, *extras = call(
        load_kernel,
        [((width, width), BF16), (coupling_shape[1:], BF16), ((1, 128), F32), face, face],
        in_hbm(dual_ops), in_hbm(corner_coupling), in_hbm(corner_map), sign,
        specs=[HBM] * 3 + [VMEM],
        scratch=[
            pltpu.VMEM(coupling_shape, BF16),
            pltpu.VMEM(map_shape, jnp.int32),
            pltpu.SemaphoreType.DMA((pieces + 2,)),
        ],
    )
    tile_shape = ((nrhs, TILE), F32)
    precond0, image0, tile, to_inner, to_outer = call(
        functools.partial(first_kernel, count),
        [wide, wide, tile_shape, ((nrhs, width + TILE), F32), wide],
        product, *exchange(to_inner, to_outer), residual0, loaded, couple, map_row, *extras,
        flops=flops,
    )
    square = ((corners, corners), BF16)
    coarse_parts = call(prepare_kernel, [square, square], coarse_inverse, flops=corners * corners)
    rows = nrhs + 2 * slots + 8

    def follow(got, from_outer):
        *kept, to_inner, to_outer = call(
            functools.partial(follow_kernel, count),
            [
                wide, wide, ((2 * slots, width), F32), ((2 * slots, width), BF16), ((1, 128), F32),
                ((rows, half), F32), ((rows, half), F32),
            ],
            image0, got, from_outer, couple, map_row, held,
            flops=5 * flops,
        )
        return tuple(kept), (to_inner, to_outer)

    def assemble(got, from_outer):
        body = functools.partial(assemble_kernel, count)
        return tuple(call(body, [wide, wide], image1, got, from_outer, small, precond0, flops=5 * flops)), ()

    maps, gathered = region(tile, to_inner, to_outer, follow)
    columns, index = gathered[-2:]
    solved0, residual1, whole0, precond1, image1, small, tile, to_inner, to_outer = call(
        functools.partial(middle_kernel, count, corners),
        [((nrhs, corners), F32), wide, wide, wide, wide, ((nrhs, 128), F32), tile_shape, ((nrhs, half + TILE), F32), face],
        *gathered, precond0, image0, residual0, loaded, couple, *coarse_parts,
        flops=flops,
    )
    _, gathered = region(tile, to_inner, to_outer, assemble, maps)
    whole_out = ((1, nrhs, width), F32)
    return tuple(
        call(
            functools.partial(final_kernel, corners),
            [whole_out, whole_out],
            *gathered, precond1, residual1, precond0, whole0, solved0, small,
            columns, index, sign, *coarse_parts,
            flops=flops,
        )
    )


def solution(mesh):
    in_specs = (
        P("grp", None, "blk"),
        P("grp", "blk", None),
        P("grp", "blk", None),
        P("grp", "blk", None),
        P("grp", "blk"),
        P("grp", "blk"),
        P(),
    )
    out_specs = (P("grp", None, "blk"), P("grp", None, "blk"))
    return jax.shard_map(
        functools.partial(local, mesh.shape["blk"], mesh.shape["grp"]),
        mesh=mesh,
        in_specs=in_specs,
        out_specs=out_specs,
        check_vma=False,
    )
```

```python
import functools

import jax
import jax.numpy as jnp
from jax import lax
from jax.experimental import pallas as pl
from jax.experimental.pallas import tpu as pltpu
from jax.sharding import PartitionSpec as P

AXES = ("blk", "grp")
NN = (((1,), (0,)), ((), ()))
NT = (((1,), (1,)), ((), ()))
F32 = jnp.float32
BF16 = jnp.bfloat16


def radices(count):
    found = []
    factor = 2
    while count > 1:
        while count % factor == 0:
            found.append(factor)
            count //= factor
        factor += 1
    return found


def swap(count, groups, partner):
    pairs = []
    for blk in range(count):
        for grp in range(groups):
            other = partner(blk)
            if 0 <= other < count:
                target = other * groups + grp
            elif grp ^ 1 < groups:
                target = blk * groups + (grp ^ 1)
            else:
                target = blk * groups + grp
            pairs.append((blk * groups + grp, target))
    return pairs


def inner_pairs(count, groups):
    return swap(count, groups, lambda blk: blk ^ 1)


def outer_pairs(count, groups):
    return swap(count, groups, lambda blk: blk + 1 if blk % 2 == 1 else blk - 1)


def rotations(count, groups):
    core = 2 if count % 2 == 0 else 1
    chips = count // core
    steps = []

    def pairs_of(target):
        return [
            (blk * groups + grp, target(blk // core, blk % core, grp)) for blk in range(count) for grp in range(groups)
        ]

    def place(chip, lane, grp):
        return (chip * core + lane) * groups + grp

    def turned(value, stride, factor, turn):
        digit = (value // stride) % factor
        return value + ((digit + turn) % factor - digit) * stride

    def along(axis, stride, factor):
        def pairs(turn):
            def target(chip, lane, grp):
                lane = (lane + 1) % core
                if axis == "blk":
                    return place(turned(chip, stride, factor, turn), lane, grp)
                return place(chip, lane, turned(grp, stride, factor, turn))

            return pairs_of(target)

        return [pairs(turn) for turn in range(1, factor)], False

    def both():
        def split_target(chip, lane, grp):
            return place(chip, 1, grp ^ 1) if lane == 0 else place(chip ^ 1, 0, grp)

        def across_target(chip, lane, grp):
            return place(chip ^ 1, lane ^ 1, grp ^ 1)

        return [pairs_of(split_target), pairs_of(across_target)], True

    todo = []
    for axis, size in (("grp", groups), ("blk", chips)):
        stride = 1
        for factor in radices(size):
            todo.append((axis, stride, factor))
            stride *= factor
    first = [("grp", 1, 2), ("blk", 1, 2)]
    if core == 2 and all(step in todo for step in first):
        todo = [step for step in todo if step not in first]
        steps.append(both())
    return steps + [along(*step) for step in todo]


def mm(first, second, dims):
    return lax.dot_general(first, second, dims, preferred_element_type=F32)


def halves(values):
    high = values.astype(BF16)
    return high, (values - high.astype(F32)).astype(BF16)


def stacked(values):
    return jnp.concatenate(halves(values), axis=0)


def folded(rows):
    count = rows.shape[0] // 2
    return rows[:count] + rows[count:]


def dots(first, second):
    product = folded(mm(stacked(first), stacked(second), NT))
    count = second.shape[0]
    return product[:, :count] + product[:, count:]


def against(values, exact):
    return folded(mm(stacked(values), exact, NN))


def lanes_of(shape):
    return lax.broadcasted_iota(jnp.int32, shape, len(shape) - 1)


def chosen(row, corners):
    shape = (corners, row.shape[1])
    return (lax.broadcasted_iota(jnp.int32, shape, 0) == row).astype(BF16)


def live_mask(blk, count, width):
    lane = lanes_of((1, width))
    low = (blk > 0).astype(F32)
    up = (blk < count - 1).astype(F32)
    return jnp.where(lane < width // 2, low, up)


def split(even, low, up):
    return jnp.where(even, up, low), jnp.where(even, low, up)


def joined(even, from_inner, from_outer):
    low = jnp.where(even, from_outer, from_inner)
    up = jnp.where(even, from_inner, from_outer)
    return jnp.concatenate([low, up], axis=1)


def transposed(matrix):
    return matrix.T


def eliminate(matrix, target, guide):
    count = matrix.shape[1]
    row_index = lax.broadcasted_iota(jnp.int32, (1, count, 1), 1)
    column_index = lax.broadcasted_iota(jnp.int32, (1, count, count), 2)
    diagonal = jnp.where(row_index == column_index, guide, 0.0)
    scale = lax.rsqrt(jnp.sum(diagonal, axis=2, keepdims=True))
    both = scale * lax.rsqrt(jnp.sum(diagonal, axis=1, keepdims=True))
    work = jnp.concatenate([matrix * both, target * scale], axis=2)
    size = 8
    for start in range(0, count, size):
        at = [start + index for index in range(size)]
        columns = [jnp.broadcast_to(work[:, :, k : k + 1], work.shape) for k in at]
        pivot = [[column[:, k : k + 1] for column in columns] for k in at]
        rows = [work[:, k : k + 1] for k in at]
        for one in range(0, size, 2):
            two = one + 1
            a, b, c, d = pivot[one][one], pivot[one][two], pivot[two][one], pivot[two][two]
            inverse = 1.0 / (a * d - b * c)
            for j in range(two + 1, size):
                p, q = pivot[one][j], pivot[two][j]
                pivot[one][j], pivot[two][j] = (d * p - b * q) * inverse, (a * q - c * p) * inverse
            p, q = rows[one], rows[two]
            rows[one], rows[two] = (d * p - b * q) * inverse, (a * q - c * p) * inverse
            for i in range(size):
                if i not in (one, two):
                    left, right = pivot[i][one], pivot[i][two]
                    for j in range(two + 1, size):
                        pivot[i][j] = pivot[i][j] - left * pivot[one][j] - right * pivot[two][j]
                    rows[i] = rows[i] - left * rows[one] - right * rows[two]
        products = [column * row for column, row in zip(columns, rows)]
        while len(products) > 1:
            products = [one + two for one, two in zip(products[::2], products[1::2])]
        work = work - products[0]
        for k, row in zip(at, rows):
            work = jnp.where(row_index == k, row, work)
    return work[:, :, count:] * scale


def symmetric(matrix):
    return 0.5 * (matrix + transposed(matrix))


def corner_values(values, couple):
    half = values.shape[1] // 2
    both = stacked(values)
    low = folded(mm(both[:, :half], couple, NT))
    up = folded(mm(both[:, half:], couple, NT))
    return jnp.where(lanes_of(low.shape) < couple.shape[0] // 2, low, up)


TILE = 128
GROUP = 32
MOST = 32


def abreast(rows):
    half = rows.shape[0] // 2
    return [rows[:half], rows[half:]]


def tiles_of(even, corner, index, first, second, third):
    half = first.shape[0] // 2
    squares = abreast(first) + abreast(second) + abreast(third)
    used = sum(part.shape[1] for part in squares)
    squares = jnp.concatenate(squares + [jnp.zeros((half, TILE - used), F32)], axis=1)
    values = abreast(corner)
    gap = jnp.zeros((half, 2 * corner.shape[1]), F32)
    left, right = jnp.concatenate(values + [gap], axis=1), jnp.concatenate([gap] + values, axis=1)
    row = lax.broadcasted_iota(jnp.int32, (half, index.shape[1]), 0)
    index = jnp.where(row == jnp.where(even, 0, 1), index, 0.0)
    rest = jnp.zeros((half, TILE - left.shape[1] - index.shape[1]), F32)
    return jnp.concatenate(
        [squares, jnp.concatenate([jnp.where(even, left, right), index, rest], axis=1)], axis=0
    )


def untile(tile):
    count = 2 * tile.shape[0]
    return [
        jnp.concatenate([tile[:, at : at + count], tile[:, at + count : at + 2 * count]], axis=0)
        for at in (0, 2 * count, 4 * count)
    ]


def dense(tiles, maps, slots, corners):
    count = tiles.shape[0] // 8
    lane = lanes_of((1, TILE))
    low, up, index = [], [], []

    def moved(rows, at, to):
        shift = (to - at) % TILE
        return pltpu.roll(rows, shift, 1) if shift else rows

    for start in range(0, count, TILE // GROUP // 2):
        parts = [jnp.zeros((8, TILE), F32), jnp.zeros((8, TILE), F32), jnp.full((1, TILE), -1.0, F32)]
        for turn in range(TILE // GROUP):
            at, core = start + turn // 2, turn % 2
            if at < count:
                here = (lane // GROUP == turn) & (lane % GROUP < slots)
                tile = tiles[8 * at : 8 * at + 8]
                name = maps[8 * at + core : 8 * at + core + 1]
                new = [
                    moved(tile, 2 * slots * core, GROUP * turn),
                    moved(tile, 2 * slots * core + slots, GROUP * turn),
                    moved(name, 4 * slots, GROUP * turn),
                ]
                parts = [jnp.where(here, one, old) for one, old in zip(new, parts)]
        low.append(parts[0])
        up.append(parts[1])
        index.append(parts[2])
    values = jnp.concatenate([jnp.concatenate(low, axis=1), jnp.concatenate(up, axis=1)], axis=0)
    choice = chosen(jnp.concatenate(index, axis=1).astype(jnp.int32), corners)
    return folded(mm(stacked(values), choice, NT))


def dense_kernel(slots, corners, tiles, maps, out):
    out[:, :corners] = dense(tiles[8:], maps[8:], slots, corners)
    out[:, corners:] = jnp.concatenate([tiles[:8], jnp.zeros((out.shape[0] - 8, TILE), F32)], axis=0)


def total_of(left, right, maps, slots, corners):
    if right.shape[1] == TILE:
        return left[:, :corners] + dense(right[8:], maps[8:], slots, corners), left[:8, corners:] + right[:8]
    return left[:, :corners] + right[:, :corners], left[:8, corners:] + right[:8, corners:]


def face_rows(rows):
    low = lax.broadcasted_iota(jnp.int32, rows.shape, 0) < rows.shape[0] // 2
    return jnp.concatenate([jnp.where(low, rows, 0.0), jnp.where(low, 0.0, rows)], axis=1)


def both_orders(first, second):
    count = first.shape[0]
    products = dots(jnp.concatenate([first, second], axis=0), jnp.concatenate([second, first], axis=0))
    return 0.5 * (products[:count, :count] + products[count:, count:])


def picked(solved, row):
    return folded(mm(stacked(solved), chosen(row.astype(jnp.int32), solved.shape[1]), NN))


def product_of(first, second):
    high, low = halves(second)
    return folded(mm(stacked(first), high, NN)) + mm(first.astype(BF16), low, NN)


def coarse_solve(corner_sum, parts):
    high, low = parts
    first = folded(mm(stacked(corner_sum), high, NN))
    return first + mm(corner_sum.astype(BF16), low, NN)


def start_kernel(
    count, rhs, signs, blocks, product, to_inner, to_outer, residual_out, sign_out, held, rhs_held, signs_held, sems,
):
    rows = held.shape[1]
    pieces = [(rhs, rhs_held), (signs, signs_held)]
    pieces += [(blocks.at[0, pl.ds(part * rows, rows)], held.at[part]) for part in range(held.shape[0])]
    copies = [pltpu.make_async_copy(*piece, sems.at[index]) for index, piece in enumerate(pieces)]
    for copy in copies:
        copy.start()
    blk = lax.axis_index("blk")
    even = blk % 2 == 0
    nrhs, width = product.shape
    half = width // 2
    live = live_mask(blk, count, width)
    copies[0].wait()
    copies[1].wait()
    sign = signs_held[...].astype(F32) * live
    residual = sign * rhs_held[0]
    rounded = residual.astype(BF16)
    sign_out[...] = sign
    residual_out[...] = residual
    total = jnp.zeros((nrhs, width), F32)
    for part, copy in enumerate(copies[2:]):
        copy.wait()
        total = total + mm(rounded[:, part * rows : (part + 1) * rows], held[part], NN)
    product[...] = total
    inner, outer = split(even, total[:, :half], total[:, half:])
    to_inner[...] = inner
    to_outer[...] = outer


def load_kernel(
    blocks, coupling, corner_map, after, out, couple_out, map_out, inner_extra, outer_extra, coupling_held, map_held, sems
):
    del after
    parts = sems.shape[0] - 2
    rows = out.shape[0] // parts
    pieces = [(corner_map, map_held), (coupling, coupling_held)]
    pieces += [(blocks.at[0, pl.ds(part * rows, rows)], out.at[pl.ds(part * rows, rows)]) for part in range(parts)]
    copies = [pltpu.make_async_copy(*piece, sems.at[index]) for index, piece in enumerate(pieces)]
    for copy in copies:
        copy.start()
    copies[0].wait()
    copies[1].wait()
    even = lax.axis_index("blk") % 2 == 0
    nrhs, half = inner_extra.shape
    couple = coupling_held[0]
    couple_out[...] = couple
    slots = couple.shape[0] // 2
    wide = couple.astype(F32)
    row = jnp.concatenate([map_held[...].astype(F32), jnp.zeros((1, half - 2 * slots), F32)], axis=1)
    map_out[...] = row[:, : map_out.shape[1]]
    fill = jnp.zeros((nrhs - slots - 1, half), F32)
    inner, outer = split(
        even,
        jnp.concatenate([wide[:slots], row, fill], axis=0),
        jnp.concatenate([wide[slots:], pltpu.roll(row, half - slots, 1), fill], axis=0),
    )
    inner_extra[...] = inner
    outer_extra[...] = outer
    for copy in copies[2:]:
        copy.wait()


def first_kernel(
    count, product, from_inner, from_outer, residual, blocks, couple, map_row, inner_extra, outer_extra,
    precond_out, image_out, tile_out, to_inner, to_outer,
):
    blk = lax.axis_index("blk")
    even = blk % 2 == 0
    nrhs, width = product.shape
    half = width // 2
    live = live_mask(blk, count, width)
    precond = live * (product[...] - joined(even, from_inner[...], from_outer[...]))
    image = mm(precond.astype(BF16), blocks[...], NN)
    precond_out[...] = precond
    image_out[...] = image
    grams = dots(
        jnp.concatenate([residual[...], precond], axis=0), jnp.concatenate([precond, image], axis=0)
    )
    slots = couple.shape[0]
    first, second = grams[:nrhs, :nrhs], grams[nrhs:, nrhs:]
    tile = tiles_of(
        even, corner_values(precond, couple[...]), map_row[:, :slots], first, second, jnp.zeros_like(first)
    )
    tile_out[...] = tile
    inner, outer = split(even, image[:, :half], image[:, half:])
    to_inner[:, :half] = inner
    to_outer[:, :half] = outer
    to_inner[:, half:width] = inner_extra[...]
    to_outer[:, half:] = outer_extra[...]
    to_inner[:, width:] = tile


def prepare_kernel(coarse, high, low):
    top, rest = halves(coarse[...])
    high[...] = top
    low[...] = rest


def follow_kernel(
    count, image, got, from_outer, couple, map_row, blocks,
    part_out, product_out, spread_out, columns_out, map_out, to_inner, to_outer,
):
    blk = lax.axis_index("blk")
    even = blk % 2 == 0
    nrhs, width = image.shape
    half = width // 2
    live = live_mask(blk, count, width)
    inner_got = got[...]
    outer_got = from_outer[...]
    part = live * (image[...] - joined(even, inner_got[:, :half], outer_got[:, :half]))
    beside = joined(even, inner_got[:, half:width], outer_got[:, half:])
    wide = couple[...].astype(F32)
    slots = wide.shape[0] // 2
    other = jnp.concatenate([beside[:slots, :half], beside[:slots, half:]], axis=0)
    columns = (live * jnp.concatenate([face_rows(wide), -face_rows(other)], axis=0)).astype(BF16)
    products = mm(jnp.concatenate([stacked(part), columns], axis=0), blocks[...].reshape(width, width), NN)
    product = products[:nrhs] + products[nrhs : 2 * nrhs]
    spread = products[2 * nrhs :]
    row = jnp.concatenate(
        [
            map_row[:, : 2 * slots],
            beside[slots : slots + 1, :slots],
            beside[slots : slots + 1, half : half + slots],
            jnp.full((1, map_row.shape[1] - 4 * slots), -1.0, F32),
        ],
        axis=1,
    )
    part_out[...] = part
    product_out[...] = product
    spread_out[...] = spread
    columns_out[...] = columns
    map_out[...] = row
    count_rows = nrhs + 4 * slots
    rows = jnp.concatenate([product, spread], axis=0)
    to_inner[:count_rows, :], to_outer[:count_rows, :] = split(even, rows[:, :half], rows[:, half:])
    last = jnp.concatenate([row, jnp.zeros((1, half - row.shape[1]), F32)], axis=1)
    last = jnp.broadcast_to(last, (to_inner.shape[0] - count_rows, half))
    to_inner[count_rows:, :] = last
    to_outer[count_rows:, :] = last


def middle_kernel(
    count, corners, left, right, maps, from_inner, from_outer, part, product, spread, columns, map_row,
    precond_in, image_in, residual_in, blocks, couple, coarse_high, coarse_low,
    solved_out, residual_out, whole_out, precond_out, image_out, small_out, tile_out, to_inner, to_outer,
):
    blk = lax.axis_index("blk")
    even = blk % 2 == 0
    nrhs, width = part.shape
    half = width // 2
    live = live_mask(blk, count, width)
    slots = couple.shape[0]
    corner_sum, squares = total_of(left, right, maps, slots, corners)
    gram, local_energy, _ = untile(squares)
    local_energy = symmetric(local_energy)
    solved = coarse_solve(corner_sum, (coarse_high[...], coarse_low[...]))
    energy = local_energy + both_orders(corner_sum, solved)
    unit = (lax.broadcasted_iota(jnp.int32, (nrhs, nrhs), 0) == lanes_of((nrhs, nrhs))).astype(F32)
    old = symmetric(gram)
    both = eliminate(
        jnp.stack([2.0 * energy, old]), jnp.stack([gram, unit]), jnp.stack([2.0 * local_energy, old])
    )
    alpha, inverse = transposed(both[0]), both[1]

    rows = spread.shape[0]
    wide = map_row.shape[1]
    inner_got, outer_got = from_inner[...], from_outer[...]
    sides = [jnp.where(even, outer_got, inner_got), jnp.where(even, inner_got, outer_got)]
    index = jnp.concatenate([map_row[...]] + [side[nrhs + rows : nrhs + rows + 1, :wide] for side in sides], axis=1)
    at = picked(solved, index)
    whole = part[...] + against(at[:, :rows], columns[...])
    own = product[...] + product_of(at[:, :rows], spread[...])
    others = [
        side[:nrhs] + product_of(at[:, wide * turn : wide * turn + rows], side[nrhs : nrhs + rows])
        for turn, side in enumerate(sides, 1)
    ]
    change = live * (own - jnp.concatenate(others, axis=1))
    change = product_of(alpha, jnp.concatenate([whole, change], axis=1))
    residual = residual_in[...] - change[:, :width]
    precond = precond_in[...] - change[:, width:]

    image = mm(precond.astype(BF16), blocks[...], NN)
    early = dots(jnp.concatenate([residual, image_in[...]], axis=0), precond)
    late = dots(jnp.concatenate([precond, precond_in[...]], axis=0), image)
    tile = tiles_of(
        even,
        corner_values(precond, couple[...]),
        jnp.zeros((1, slots), F32),
        early[:nrhs],
        late[:nrhs],
        late[nrhs:] + early[nrhs:],
    )
    tile_out[...] = tile
    inner, outer = split(even, image[:, :half], image[:, half:])
    to_inner[:, :half] = inner
    to_inner[:, half:] = tile
    to_outer[...] = outer
    solved_out[...] = solved
    residual_out[...] = residual
    whole_out[...] = whole
    precond_out[...] = precond
    image_out[...] = image
    small_out[...] = jnp.concatenate([inverse, energy, alpha, jnp.zeros((nrhs, 128 - 3 * nrhs), F32)], axis=1)


def assemble_kernel(count, image, got, from_outer, small, old_precond, part_out, first_out):
    blk = lax.axis_index("blk")
    nrhs, width = image.shape
    image_beside = joined(blk % 2 == 0, got[:, : width // 2], from_outer[...])
    part_out[...] = live_mask(blk, count, width) * (image[...] - image_beside)
    first_out[...] = product_of(small[:, 2 * nrhs : 3 * nrhs], old_precond[...])


def final_kernel(
    corners, left, right, maps, part, first, precond, residual, old_precond, old_image,
    old_solved, small, columns, map_row, sign, coarse_high, coarse_low,
    multipliers_out, residual_out,
):
    nrhs, width = precond.shape
    slots = columns.shape[0] // 2
    corner_sum, squares = total_of(left, right, maps, slots, corners)
    gram, new_new, old_new = untile(squares)
    inverse, old_old = small[:, :nrhs], small[:, nrhs : 2 * nrhs]
    beta = product_of(inverse, gram)
    turned = product_of(transposed(gram), inverse)
    solved = coarse_solve(corner_sum, (coarse_high[...], coarse_low[...]))
    old_new = old_new + product_of(old_old, beta) + 2.0 * dots(old_solved[...], corner_sum)
    energy = symmetric(new_new + product_of(turned, old_new)) + both_orders(corner_sum, solved)
    alpha = transposed(eliminate(2.0 * energy[None], gram[None], 2.0 * new_new[None])[0])
    at = picked(solved, map_row[...])
    whole = part[...] + against(at[:, : columns.shape[0]], columns[...])
    carried = product_of(turned, jnp.concatenate([old_precond[...], old_image[...]], axis=1))
    change = product_of(alpha, jnp.concatenate([precond[...], whole], axis=1) + carried)
    multipliers_out[0] = sign[...] * (first[...] + change[:, :width])
    residual_out[0] = sign[...] * (residual[...] - change[:, width:])


VMEM = pl.BlockSpec(memory_space=pltpu.VMEM)
HBM = pl.BlockSpec(memory_space=pltpu.HBM)


def call(body, shapes, *args, specs=None, scratch=(), flops=0):
    shapes = [jax.ShapeDtypeStruct(shape, dtype) for shape, dtype in shapes]
    moved = sum(arg.size * arg.dtype.itemsize for arg in args)
    return pl.pallas_call(
        body,
        out_shape=shapes,
        in_specs=specs or [VMEM] * len(args),
        out_specs=[VMEM] * len(shapes),
        scratch_shapes=list(scratch),
        compiler_params=pltpu.CompilerParams(vmem_limit_bytes=16 << 20),
        cost_estimate=pl.CostEstimate(flops=flops, bytes_accessed=moved, transcendentals=0),
    )(*args)


def local(count, groups, dual_rhs, dual_ops, prec_ops, corner_coupling, corner_map, signs, coarse_inverse):
    nrhs, width = dual_rhs.shape[1:]
    half = width // 2
    corners = coarse_inverse.shape[0]
    inner, outer = inner_pairs(count, groups), outer_pairs(count, groups)
    steps = rotations(count, groups)
    dense_shape = ((nrhs, corners + TILE), F32)
    slots = corner_map.shape[1]
    flops = 2 * nrhs * width * width

    def permute(values, pairs):
        return lax.ppermute(values, AXES, pairs)

    def exchange(to_inner, to_outer):
        from_outer = permute(to_outer, outer)
        return permute(to_inner, inner), from_outer

    def densify(tiles, maps):
        body = functools.partial(dense_kernel, slots, corners)
        return call(body, [dense_shape], tiles, maps, flops=flops)[0]

    def united(parts):
        if parts[0].shape[1] != TILE:
            return sum(parts[1:], parts[0])
        squares = [part[:8] for part in parts]
        return jnp.concatenate([sum(squares[1:], squares[0])] + [part[8:] for part in parts], axis=0)

    def region(tile, to_inner, to_outer, follow, maps=None):
        from_outer = permute(to_outer, outer)
        got = permute(to_inner, inner)
        values = tile + got[:, got.shape[1] - TILE :]
        known = maps
        left, right = None, None
        for index, (turns, relayed) in enumerate(steps):
            if index > 0:
                held = left.shape[0] + right.shape[0] - 16
                if left.shape[1] == TILE and 8 * MOST < 2 * held * (1 + len(turns) + relayed):
                    known = known or (left, right)
                    left, right = densify(left, known[0]), densify(right, known[1])
                values = united([left, right])
            if index == max(len(steps) - (1 if maps else 2), 0):
                result, sends = follow(got, from_outer)
                values, result, sends = lax.optimization_barrier((values, result, sends))
                result = (*(exchange(*sends) if sends else ()), *result)
            left = values
            terms = [permute(values, pairs) for pairs in turns]
            right = united(terms + [permute(terms[0], inner)] * relayed)
        known = known or (left, right)
        if left.shape[1] == TILE:
            left = densify(left, known[0])
        return known, (left, right, known[1], *result)

    wide = ((nrhs, width), F32)
    face = ((nrhs, half), F32)
    pieces = 8
    in_hbm = functools.partial(pltpu.with_memory_space_constraint, memory_space=pltpu.HBM)
    coupling_shape, map_shape = corner_coupling.shape, corner_map.shape
    product, to_inner, to_outer, residual0, sign, held = call(
        functools.partial(start_kernel, count),
        [wide, face, face, wide, ((1, width), F32), ((pieces, width // pieces, width), BF16)],
        in_hbm(dual_rhs), in_hbm(signs), in_hbm(prec_ops),
        specs=[HBM] * 3,
        scratch=[
            pltpu.VMEM(dual_rhs.shape, F32),
            pltpu.VMEM(signs.shape, jnp.int32),
            pltpu.SemaphoreType.DMA((pieces + 2,)),
        ],
        flops=flops,
    )
    loaded, couple, map_row, *extras = call(
        load_kernel,
        [((width, width), BF16), (coupling_shape[1:], BF16), ((1, 128), F32), face, face],
        in_hbm(dual_ops), in_hbm(corner_coupling), in_hbm(corner_map), sign,
        specs=[HBM] * 3 + [VMEM],
        scratch=[
            pltpu.VMEM(coupling_shape, BF16),
            pltpu.VMEM(map_shape, jnp.int32),
            pltpu.SemaphoreType.DMA((pieces + 2,)),
        ],
    )
    tile_shape = ((nrhs, TILE), F32)
    precond0, image0, tile, to_inner, to_outer = call(
        functools.partial(first_kernel, count),
        [wide, wide, tile_shape, ((nrhs, width + TILE), F32), wide],
        product, *exchange(to_inner, to_outer), residual0, loaded, couple, map_row, *extras,
        flops=flops,
    )
    square = ((corners, corners), BF16)
    coarse_parts = call(prepare_kernel, [square, square], coarse_inverse, flops=corners * corners)
    rows = nrhs + 2 * slots + 8

    def follow(got, from_outer):
        *kept, to_inner, to_outer = call(
            functools.partial(follow_kernel, count),
            [
                wide, wide, ((2 * slots, width), F32), ((2 * slots, width), BF16), ((1, 128), F32),
                ((rows, half), F32), ((rows, half), F32),
            ],
            image0, got, from_outer, couple, map_row, held,
            flops=5 * flops,
        )
        return tuple(kept), (to_inner, to_outer)

    def assemble(got, from_outer):
        body = functools.partial(assemble_kernel, count)
        return tuple(call(body, [wide, wide], image1, got, from_outer, small, precond0, flops=5 * flops)), ()

    maps, gathered = region(tile, to_inner, to_outer, follow)
    columns, index = gathered[-2:]
    solved0, residual1, whole0, precond1, image1, small, tile, to_inner, to_outer = call(
        functools.partial(middle_kernel, count, corners),
        [((nrhs, corners), F32), wide, wide, wide, wide, ((nrhs, 128), F32), tile_shape, ((nrhs, half + TILE), F32), face],
        *gathered, precond0, image0, residual0, loaded, couple, *coarse_parts,
        flops=flops,
    )
    _, gathered = region(tile, to_inner, to_outer, assemble, maps)
    whole_out = ((1, nrhs, width), F32)
    return tuple(
        call(
            functools.partial(final_kernel, corners),
            [whole_out, whole_out],
            *gathered, precond1, residual1, precond0, whole0, solved0, small,
            columns, index, sign, *coarse_parts,
            flops=flops,
        )
    )


def solution(mesh):
    in_specs = (
        P("grp", None, "blk"),
        P("grp", "blk", None),
        P("grp", "blk", None),
        P("grp", "blk", None),
        P("grp", "blk"),
        P("grp", "blk"),
        P(),
    )
    out_specs = (P("grp", None, "blk"), P("grp", None, "blk"))
    return jax.shard_map(
        functools.partial(local, mesh.shape["blk"], mesh.shape["grp"]),
        mesh=mesh,
        in_specs=in_specs,
        out_specs=out_specs,
        check_vma=False,
    )
```

```python
import functools

import jax
import jax.numpy as jnp
from jax import lax
from jax.experimental import pallas as pl
from jax.experimental.pallas import tpu as pltpu
from jax.sharding import PartitionSpec as P

AXES = ("blk", "grp")
NN = (((1,), (0,)), ((), ()))
NT = (((1,), (1,)), ((), ()))
F32 = jnp.float32
BF16 = jnp.bfloat16


def radices(count):
    found = []
    factor = 2
    while count > 1:
        while count % factor == 0:
            found.append(factor)
            count //= factor
        factor += 1
    return found


def swap(count, groups, partner):
    pairs = []
    for blk in range(count):
        for grp in range(groups):
            other = partner(blk)
            if 0 <= other < count:
                target = other * groups + grp
            elif grp ^ 1 < groups:
                target = blk * groups + (grp ^ 1)
            else:
                target = blk * groups + grp
            pairs.append((blk * groups + grp, target))
    return pairs


def inner_pairs(count, groups):
    return swap(count, groups, lambda blk: blk ^ 1)


def outer_pairs(count, groups):
    return swap(count, groups, lambda blk: blk + 1 if blk % 2 == 1 else blk - 1)


def rotations(count, groups):
    core = 2 if count % 2 == 0 else 1
    chips = count // core
    steps = []

    def pairs_of(target):
        return [
            (blk * groups + grp, target(blk // core, blk % core, grp)) for blk in range(count) for grp in range(groups)
        ]

    def place(chip, lane, grp):
        return (chip * core + lane) * groups + grp

    def turned(value, stride, factor, turn):
        digit = (value // stride) % factor
        return value + ((digit + turn) % factor - digit) * stride

    def along(axis, stride, factor):
        def pairs(turn):
            def target(chip, lane, grp):
                lane = (lane + 1) % core
                if axis == "blk":
                    return place(turned(chip, stride, factor, turn), lane, grp)
                return place(chip, lane, turned(grp, stride, factor, turn))

            return pairs_of(target)

        return [pairs(turn) for turn in range(1, factor)], False

    def both():
        def split_target(chip, lane, grp):
            return place(chip, 1, grp ^ 1) if lane == 0 else place(chip ^ 1, 0, grp)

        def across_target(chip, lane, grp):
            return place(chip ^ 1, lane ^ 1, grp ^ 1)

        return [pairs_of(split_target), pairs_of(across_target)], True

    todo = []
    for axis, size in (("grp", groups), ("blk", chips)):
        stride = 1
        for factor in radices(size):
            todo.append((axis, stride, factor))
            stride *= factor
    first = [("grp", 1, 2), ("blk", 1, 2)]
    if core == 2 and all(step in todo for step in first):
        todo = [step for step in todo if step not in first]
        steps.append(both())
    return steps + [along(*step) for step in todo]


def mm(first, second, dims):
    return lax.dot_general(first, second, dims, preferred_element_type=F32)


def halves(values):
    high = values.astype(BF16)
    return high, (values - high.astype(F32)).astype(BF16)


def stacked(values):
    return jnp.concatenate(halves(values), axis=0)


def folded(rows):
    count = rows.shape[0] // 2
    return rows[:count] + rows[count:]


def dots(first, second):
    first_high, first_low = halves(first)
    high, low = halves(second)
    left = jnp.concatenate([first_high, first_low, first_high], axis=1)
    return mm(left, jnp.concatenate([high, high, low], axis=1), NT)


def against(values, exact):
    return folded(mm(stacked(values), exact, NN))


def lanes_of(shape):
    return lax.broadcasted_iota(jnp.int32, shape, len(shape) - 1)


def chosen(row, corners):
    shape = (corners, row.shape[1])
    return (lax.broadcasted_iota(jnp.int32, shape, 0) == row).astype(BF16)


def live_mask(blk, count, width):
    lane = lanes_of((1, width))
    low = (blk > 0).astype(F32)
    up = (blk < count - 1).astype(F32)
    return jnp.where(lane < width // 2, low, up)


def split(even, low, up):
    return jnp.where(even, up, low), jnp.where(even, low, up)


def joined(even, from_inner, from_outer):
    low = jnp.where(even, from_outer, from_inner)
    up = jnp.where(even, from_inner, from_outer)
    return jnp.concatenate([low, up], axis=1)


def transposed(matrix):
    return matrix.T


def weighted(weights, values):
    top = weights.astype(BF16).astype(F32)
    left = transposed(jnp.concatenate([top, weights - top, top], axis=0)).astype(BF16)
    high, low = halves(values)
    return mm(left, jnp.concatenate([high, high, low], axis=0), NN)


def eliminate(matrix, target, guide):
    count = matrix.shape[1]
    row_index = lax.broadcasted_iota(jnp.int32, (1, count, 1), 1)
    column_index = lax.broadcasted_iota(jnp.int32, (1, count, count), 2)
    diagonal = jnp.where(row_index == column_index, guide, 0.0)
    scale = lax.rsqrt(jnp.sum(diagonal, axis=2, keepdims=True))
    both = scale * lax.rsqrt(jnp.sum(diagonal, axis=1, keepdims=True))
    work = jnp.concatenate([matrix * both, target * scale], axis=2)
    size = 8
    for start in range(0, count, size):
        at = [start + index for index in range(size)]
        columns = [jnp.broadcast_to(work[:, :, k : k + 1], work.shape) for k in at]
        pivot = [[column[:, k : k + 1] for column in columns] for k in at]
        rows = [work[:, k : k + 1] for k in at]
        for one in range(0, size, 2):
            two = one + 1
            a, b, c, d = pivot[one][one], pivot[one][two], pivot[two][one], pivot[two][two]
            inverse = 1.0 / (a * d - b * c)
            for j in range(two + 1, size):
                p, q = pivot[one][j], pivot[two][j]
                pivot[one][j], pivot[two][j] = (d * p - b * q) * inverse, (a * q - c * p) * inverse
            p, q = rows[one], rows[two]
            rows[one], rows[two] = (d * p - b * q) * inverse, (a * q - c * p) * inverse
            for i in range(size):
                if i not in (one, two):
                    left, right = pivot[i][one], pivot[i][two]
                    for j in range(two + 1, size):
                        pivot[i][j] = pivot[i][j] - left * pivot[one][j] - right * pivot[two][j]
                    rows[i] = rows[i] - left * rows[one] - right * rows[two]
        products = [column * row for column, row in zip(columns, rows)]
        while len(products) > 1:
            products = [one + two for one, two in zip(products[::2], products[1::2])]
        work = work - products[0]
        for k, row in zip(at, rows):
            work = jnp.where(row_index == k, row, work)
    return work[:, :, count:] * scale


def symmetric(matrix):
    return 0.5 * (matrix + transposed(matrix))


def corner_values(values, couple):
    half = values.shape[1] // 2
    both = stacked(values)
    low = folded(mm(both[:, :half], couple, NT))
    up = folded(mm(both[:, half:], couple, NT))
    return jnp.where(lanes_of(low.shape) < couple.shape[0] // 2, low, up)


TILE = 128
GROUP = 32
MOST = 32


def abreast(rows):
    half = rows.shape[0] // 2
    return [rows[:half], rows[half:]]


def tiles_of(even, corner, index, first, second, third):
    half = first.shape[0] // 2
    squares = abreast(first) + abreast(second) + abreast(third)
    used = sum(part.shape[1] for part in squares)
    squares = jnp.concatenate(squares + [jnp.zeros((half, TILE - used), F32)], axis=1)
    values = abreast(corner)
    gap = jnp.zeros((half, 2 * corner.shape[1]), F32)
    left, right = jnp.concatenate(values + [gap], axis=1), jnp.concatenate([gap] + values, axis=1)
    row = lax.broadcasted_iota(jnp.int32, (half, index.shape[1]), 0)
    index = jnp.where(row == jnp.where(even, 0, 1), index, 0.0)
    rest = jnp.zeros((half, TILE - left.shape[1] - index.shape[1]), F32)
    return jnp.concatenate(
        [squares, jnp.concatenate([jnp.where(even, left, right), index, rest], axis=1)], axis=0
    )


def untile(tile):
    count = 2 * tile.shape[0]
    return [
        jnp.concatenate([tile[:, at : at + count], tile[:, at + count : at + 2 * count]], axis=0)
        for at in (0, 2 * count, 4 * count)
    ]


def dense(tiles, maps, slots, corners):
    count = tiles.shape[0] // 8
    lane = lanes_of((1, TILE))
    low, up, index = [], [], []

    def moved(rows, at, to):
        shift = (to - at) % TILE
        return pltpu.roll(rows, shift, 1) if shift else rows

    for start in range(0, count, TILE // GROUP // 2):
        parts = [jnp.zeros((8, TILE), F32), jnp.zeros((8, TILE), F32), jnp.full((1, TILE), -1.0, F32)]
        for turn in range(TILE // GROUP):
            at, core = start + turn // 2, turn % 2
            if at < count:
                here = (lane // GROUP == turn) & (lane % GROUP < slots)
                tile = tiles[8 * at : 8 * at + 8]
                name = maps[8 * at + core : 8 * at + core + 1]
                new = [
                    moved(tile, 2 * slots * core, GROUP * turn),
                    moved(tile, 2 * slots * core + slots, GROUP * turn),
                    moved(name, 4 * slots, GROUP * turn),
                ]
                parts = [jnp.where(here, one, old) for one, old in zip(new, parts)]
        low.append(parts[0])
        up.append(parts[1])
        index.append(parts[2])
    values = jnp.concatenate([jnp.concatenate(low, axis=1), jnp.concatenate(up, axis=1)], axis=0)
    choice = chosen(jnp.concatenate(index, axis=1).astype(jnp.int32), corners)
    return folded(mm(stacked(values), choice, NT))


def dense_kernel(slots, corners, tiles, maps, out):
    out[:, :corners] = dense(tiles[8:], maps[8:], slots, corners)
    out[:, corners:] = jnp.concatenate([tiles[:8], jnp.zeros((out.shape[0] - 8, TILE), F32)], axis=0)


def total_of(left, right, maps, slots, corners):
    if right.shape[1] == TILE:
        return left[:, :corners] + dense(right[8:], maps[8:], slots, corners), left[:8, corners:] + right[:8]
    return left[:, :corners] + right[:, :corners], left[:8, corners:] + right[:8, corners:]


def face_rows(rows):
    low = lax.broadcasted_iota(jnp.int32, rows.shape, 0) < rows.shape[0] // 2
    return jnp.concatenate([jnp.where(low, rows, 0.0), jnp.where(low, 0.0, rows)], axis=1)


def both_orders(first, second):
    count = first.shape[0]
    products = dots(jnp.concatenate([first, second], axis=0), jnp.concatenate([second, first], axis=0))
    return 0.5 * (products[:count, :count] + products[count:, count:])


def picked(solved, row):
    return folded(mm(stacked(solved), chosen(row.astype(jnp.int32), solved.shape[1]), NN))


def product_of(first, second):
    high, low = halves(second)
    return folded(mm(stacked(first), high, NN)) + mm(first.astype(BF16), low, NN)


def coarse_solve(corner_sum, parts):
    high, low = parts
    first = folded(mm(stacked(corner_sum), high, NN))
    return first + mm(corner_sum.astype(BF16), low, NN)


def start_kernel(
    count, rhs, signs, blocks, product, to_inner, to_outer, residual_out, sign_out, held, rhs_held, signs_held, sems,
):
    rows = held.shape[1]
    pieces = [(rhs, rhs_held), (signs, signs_held)]
    pieces += [(blocks.at[0, pl.ds(part * rows, rows)], held.at[part]) for part in range(held.shape[0])]
    copies = [pltpu.make_async_copy(*piece, sems.at[index]) for index, piece in enumerate(pieces)]
    for copy in copies:
        copy.start()
    blk = lax.axis_index("blk")
    even = blk % 2 == 0
    nrhs, width = product.shape
    half = width // 2
    live = live_mask(blk, count, width)
    copies[0].wait()
    copies[1].wait()
    sign = signs_held[...].astype(F32) * live
    residual = sign * rhs_held[0]
    rounded = residual.astype(BF16)
    sign_out[...] = sign
    residual_out[...] = residual
    total = jnp.zeros((nrhs, width), F32)
    for part, copy in enumerate(copies[2:]):
        copy.wait()
        total = total + mm(rounded[:, part * rows : (part + 1) * rows], held[part], NN)
    product[...] = total
    inner, outer = split(even, total[:, :half], total[:, half:])
    to_inner[...] = inner
    to_outer[...] = outer


def load_kernel(
    blocks, coupling, corner_map, after, out, couple_out, map_out, inner_extra, outer_extra, coupling_held, map_held, sems
):
    del after
    parts = sems.shape[0] - 2
    rows = out.shape[0] // parts
    pieces = [(corner_map, map_held), (coupling, coupling_held)]
    pieces += [(blocks.at[0, pl.ds(part * rows, rows)], out.at[pl.ds(part * rows, rows)]) for part in range(parts)]
    copies = [pltpu.make_async_copy(*piece, sems.at[index]) for index, piece in enumerate(pieces)]
    for copy in copies:
        copy.start()
    copies[0].wait()
    copies[1].wait()
    even = lax.axis_index("blk") % 2 == 0
    nrhs, half = inner_extra.shape
    couple = coupling_held[0]
    couple_out[...] = couple
    slots = couple.shape[0] // 2
    wide = couple.astype(F32)
    row = jnp.concatenate([map_held[...].astype(F32), jnp.zeros((1, half - 2 * slots), F32)], axis=1)
    map_out[...] = row[:, : map_out.shape[1]]
    fill = jnp.zeros((nrhs - slots - 1, half), F32)
    inner, outer = split(
        even,
        jnp.concatenate([wide[:slots], row, fill], axis=0),
        jnp.concatenate([wide[slots:], pltpu.roll(row, half - slots, 1), fill], axis=0),
    )
    inner_extra[...] = inner
    outer_extra[...] = outer
    for copy in copies[2:]:
        copy.wait()


def first_kernel(
    count, product, from_inner, from_outer, residual, blocks, couple, map_row, inner_extra, outer_extra,
    precond_out, image_out, tile_out, to_inner, to_outer,
):
    blk = lax.axis_index("blk")
    even = blk % 2 == 0
    nrhs, width = product.shape
    half = width // 2
    live = live_mask(blk, count, width)
    precond = live * (product[...] - joined(even, from_inner[...], from_outer[...]))
    image = mm(precond.astype(BF16), blocks[...], NN)
    precond_out[...] = precond
    image_out[...] = image
    first, second = dots(residual[...], precond), dots(precond, image)
    slots = couple.shape[0]
    tile = tiles_of(
        even, corner_values(precond, couple[...]), map_row[:, :slots], first, second, jnp.zeros_like(first)
    )
    tile_out[...] = tile
    inner, outer = split(even, image[:, :half], image[:, half:])
    to_inner[:, :half] = inner
    to_outer[:, :half] = outer
    to_inner[:, half:width] = inner_extra[...]
    to_outer[:, half:] = outer_extra[...]
    to_inner[:, width:] = tile


def prepare_kernel(coarse, high, low):
    top, rest = halves(coarse[...])
    high[...] = top
    low[...] = rest


def follow_kernel(
    count, image, got, from_outer, couple, map_row, blocks,
    part_out, product_out, spread_out, columns_out, map_out, to_inner, to_outer,
):
    blk = lax.axis_index("blk")
    even = blk % 2 == 0
    nrhs, width = image.shape
    half = width // 2
    live = live_mask(blk, count, width)
    inner_got = got[...]
    outer_got = from_outer[...]
    part = live * (image[...] - joined(even, inner_got[:, :half], outer_got[:, :half]))
    beside = joined(even, inner_got[:, half:width], outer_got[:, half:])
    wide = couple[...].astype(F32)
    slots = wide.shape[0] // 2
    other = jnp.concatenate([beside[:slots, :half], beside[:slots, half:]], axis=0)
    columns = (live * jnp.concatenate([face_rows(wide), -face_rows(other)], axis=0)).astype(BF16)
    products = mm(jnp.concatenate([stacked(part), columns], axis=0), blocks[...].reshape(width, width), NN)
    product = products[:nrhs] + products[nrhs : 2 * nrhs]
    spread = products[2 * nrhs :]
    row = jnp.concatenate(
        [
            map_row[:, : 2 * slots],
            beside[slots : slots + 1, :slots],
            beside[slots : slots + 1, half : half + slots],
            jnp.full((1, map_row.shape[1] - 4 * slots), -1.0, F32),
        ],
        axis=1,
    )
    part_out[...] = part
    product_out[...] = product
    spread_out[...] = spread
    columns_out[...] = columns
    map_out[...] = row
    count_rows = nrhs + 4 * slots
    rows = jnp.concatenate([product, spread], axis=0)
    to_inner[:count_rows, :], to_outer[:count_rows, :] = split(even, rows[:, :half], rows[:, half:])
    last = jnp.concatenate([row, jnp.zeros((1, half - row.shape[1]), F32)], axis=1)
    last = jnp.broadcast_to(last, (to_inner.shape[0] - count_rows, half))
    to_inner[count_rows:, :] = last
    to_outer[count_rows:, :] = last


def middle_kernel(
    count, corners, left, right, maps, from_inner, from_outer, part, product, spread, columns, map_row,
    precond_in, image_in, residual_in, blocks, couple, coarse_high, coarse_low,
    solved_out, residual_out, whole_out, precond_out, image_out, small_out, tile_out, to_inner, to_outer,
):
    blk = lax.axis_index("blk")
    even = blk % 2 == 0
    nrhs, width = part.shape
    half = width // 2
    live = live_mask(blk, count, width)
    slots = couple.shape[0]
    corner_sum, squares = total_of(left, right, maps, slots, corners)
    gram, local_energy, _ = untile(squares)
    local_energy = symmetric(local_energy)
    solved = coarse_solve(corner_sum, (coarse_high[...], coarse_low[...]))
    energy = local_energy + both_orders(corner_sum, solved)
    unit = (lax.broadcasted_iota(jnp.int32, (nrhs, nrhs), 0) == lanes_of((nrhs, nrhs))).astype(F32)
    old = symmetric(gram)
    both = eliminate(
        jnp.stack([2.0 * energy, old]), jnp.stack([gram, unit]), jnp.stack([2.0 * local_energy, old])
    )
    alpha, inverse = both[0], both[1]

    rows = spread.shape[0]
    wide = map_row.shape[1]
    inner_got, outer_got = from_inner[...], from_outer[...]
    sides = [jnp.where(even, outer_got, inner_got), jnp.where(even, inner_got, outer_got)]
    index = jnp.concatenate([map_row[...]] + [side[nrhs + rows : nrhs + rows + 1, :wide] for side in sides], axis=1)
    at = picked(solved, index)
    whole = part[...] + against(at[:, :rows], columns[...])
    own = product[...] + product_of(at[:, :rows], spread[...])
    others = [
        side[:nrhs] + product_of(at[:, wide * turn : wide * turn + rows], side[nrhs : nrhs + rows])
        for turn, side in enumerate(sides, 1)
    ]
    change = live * (own - jnp.concatenate(others, axis=1))
    change = weighted(alpha, jnp.concatenate([whole, change], axis=1))
    residual = residual_in[...] - change[:, :width]
    precond = precond_in[...] - change[:, width:]

    image = mm(precond.astype(BF16), blocks[...], NN)
    early = dots(jnp.concatenate([residual, image_in[...]], axis=0), precond)
    late = dots(jnp.concatenate([precond, precond_in[...]], axis=0), image)
    tile = tiles_of(
        even,
        corner_values(precond, couple[...]),
        jnp.zeros((1, slots), F32),
        early[:nrhs],
        late[:nrhs],
        late[nrhs:] + early[nrhs:],
    )
    tile_out[...] = tile
    inner, outer = split(even, image[:, :half], image[:, half:])
    to_inner[:, :half] = inner
    to_inner[:, half:] = tile
    to_outer[...] = outer
    solved_out[...] = solved
    residual_out[...] = residual
    whole_out[...] = whole
    precond_out[...] = precond
    image_out[...] = image
    small_out[...] = jnp.concatenate([inverse, energy, transposed(alpha), jnp.zeros((nrhs, 128 - 3 * nrhs), F32)], axis=1)


def assemble_kernel(count, image, got, from_outer, small, old_precond, part_out, first_out):
    blk = lax.axis_index("blk")
    nrhs, width = image.shape
    image_beside = joined(blk % 2 == 0, got[:, : width // 2], from_outer[...])
    part_out[...] = live_mask(blk, count, width) * (image[...] - image_beside)
    first_out[...] = product_of(small[:, 2 * nrhs : 3 * nrhs], old_precond[...])


def final_kernel(
    corners, left, right, maps, part, first, precond, residual, old_precond, old_image,
    old_solved, small, columns, map_row, sign, coarse_high, coarse_low,
    multipliers_out, residual_out,
):
    nrhs, width = precond.shape
    slots = columns.shape[0] // 2
    corner_sum, squares = total_of(left, right, maps, slots, corners)
    gram, new_new, old_new = untile(squares)
    inverse, old_old = small[:, :nrhs], small[:, nrhs : 2 * nrhs]
    beta = product_of(inverse, gram)
    turned = product_of(transposed(gram), inverse)
    solved = coarse_solve(corner_sum, (coarse_high[...], coarse_low[...]))
    old_new = old_new + product_of(old_old, beta) + 2.0 * dots(old_solved[...], corner_sum)
    energy = symmetric(new_new + product_of(turned, old_new)) + both_orders(corner_sum, solved)
    alpha = eliminate(2.0 * energy[None], gram[None], 2.0 * new_new[None])[0]
    at = picked(solved, map_row[...])
    whole = part[...] + against(at[:, : columns.shape[0]], columns[...])
    carried = product_of(turned, jnp.concatenate([old_precond[...], old_image[...]], axis=1))
    change = weighted(alpha, jnp.concatenate([precond[...], whole], axis=1) + carried)
    multipliers_out[0] = sign[...] * (first[...] + change[:, :width])
    residual_out[0] = sign[...] * (residual[...] - change[:, width:])


VMEM = pl.BlockSpec(memory_space=pltpu.VMEM)
HBM = pl.BlockSpec(memory_space=pltpu.HBM)


def call(body, shapes, *args, specs=None, scratch=(), flops=0):
    shapes = [jax.ShapeDtypeStruct(shape, dtype) for shape, dtype in shapes]
    moved = sum(arg.size * arg.dtype.itemsize for arg in args)
    return pl.pallas_call(
        body,
        out_shape=shapes,
        in_specs=specs or [VMEM] * len(args),
        out_specs=[VMEM] * len(shapes),
        scratch_shapes=list(scratch),
        compiler_params=pltpu.CompilerParams(vmem_limit_bytes=16 << 20),
        cost_estimate=pl.CostEstimate(flops=flops, bytes_accessed=moved, transcendentals=0),
    )(*args)


def local(count, groups, dual_rhs, dual_ops, prec_ops, corner_coupling, corner_map, signs, coarse_inverse):
    nrhs, width = dual_rhs.shape[1:]
    half = width // 2
    corners = coarse_inverse.shape[0]
    inner, outer = inner_pairs(count, groups), outer_pairs(count, groups)
    steps = rotations(count, groups)
    dense_shape = ((nrhs, corners + TILE), F32)
    slots = corner_map.shape[1]
    flops = 2 * nrhs * width * width

    def permute(values, pairs):
        return lax.ppermute(values, AXES, pairs)

    def exchange(to_inner, to_outer):
        from_outer = permute(to_outer, outer)
        return permute(to_inner, inner), from_outer

    def densify(tiles, maps):
        body = functools.partial(dense_kernel, slots, corners)
        return call(body, [dense_shape], tiles, maps, flops=flops)[0]

    def united(parts):
        if parts[0].shape[1] != TILE:
            return sum(parts[1:], parts[0])
        squares = [part[:8] for part in parts]
        return jnp.concatenate([sum(squares[1:], squares[0])] + [part[8:] for part in parts], axis=0)

    def region(tile, to_inner, to_outer, follow, maps=None):
        from_outer = permute(to_outer, outer)
        got = permute(to_inner, inner)
        values = tile + got[:, got.shape[1] - TILE :]
        known = maps
        left, right = None, None
        for index, (turns, relayed) in enumerate(steps):
            if index > 0:
                held = left.shape[0] + right.shape[0] - 16
                if left.shape[1] == TILE and 8 * MOST < 2 * held * (1 + len(turns) + relayed):
                    known = known or (left, right)
                    left, right = densify(left, known[0]), densify(right, known[1])
                values = united([left, right])
            if index == max(len(steps) - (1 if maps else 2), 0):
                result, sends = follow(got, from_outer)
                values, result, sends = lax.optimization_barrier((values, result, sends))
                result = (*(exchange(*sends) if sends else ()), *result)
            left = values
            terms = [permute(values, pairs) for pairs in turns]
            right = united(terms + [permute(terms[0], inner)] * relayed)
        known = known or (left, right)
        if left.shape[1] == TILE:
            left = densify(left, known[0])
        return known, (left, right, known[1], *result)

    wide = ((nrhs, width), F32)
    face = ((nrhs, half), F32)
    pieces = 8
    in_hbm = functools.partial(pltpu.with_memory_space_constraint, memory_space=pltpu.HBM)
    coupling_shape, map_shape = corner_coupling.shape, corner_map.shape
    product, to_inner, to_outer, residual0, sign, held = call(
        functools.partial(start_kernel, count),
        [wide, face, face, wide, ((1, width), F32), ((pieces, width // pieces, width), BF16)],
        in_hbm(dual_rhs), in_hbm(signs), in_hbm(prec_ops),
        specs=[HBM] * 3,
        scratch=[
            pltpu.VMEM(dual_rhs.shape, F32),
            pltpu.VMEM(signs.shape, jnp.int32),
            pltpu.SemaphoreType.DMA((pieces + 2,)),
        ],
        flops=flops,
    )
    loaded, couple, map_row, *extras = call(
        load_kernel,
        [((width, width), BF16), (coupling_shape[1:], BF16), ((1, 128), F32), face, face],
        in_hbm(dual_ops), in_hbm(corner_coupling), in_hbm(corner_map), sign,
        specs=[HBM] * 3 + [VMEM],
        scratch=[
            pltpu.VMEM(coupling_shape, BF16),
            pltpu.VMEM(map_shape, jnp.int32),
            pltpu.SemaphoreType.DMA((pieces + 2,)),
        ],
    )
    tile_shape = ((nrhs, TILE), F32)
    precond0, image0, tile, to_inner, to_outer = call(
        functools.partial(first_kernel, count),
        [wide, wide, tile_shape, ((nrhs, width + TILE), F32), wide],
        product, *exchange(to_inner, to_outer), residual0, loaded, couple, map_row, *extras,
        flops=flops,
    )
    square = ((corners, corners), BF16)
    coarse_parts = call(prepare_kernel, [square, square], coarse_inverse, flops=corners * corners)
    rows = nrhs + 2 * slots + 8

    def follow(got, from_outer):
        *kept, to_inner, to_outer = call(
            functools.partial(follow_kernel, count),
            [
                wide, wide, ((2 * slots, width), F32), ((2 * slots, width), BF16), ((1, 128), F32),
                ((rows, half), F32), ((rows, half), F32),
            ],
            image0, got, from_outer, couple, map_row, held,
            flops=5 * flops,
        )
        return tuple(kept), (to_inner, to_outer)

    def assemble(got, from_outer):
        body = functools.partial(assemble_kernel, count)
        return tuple(call(body, [wide, wide], image1, got, from_outer, small, precond0, flops=5 * flops)), ()

    maps, gathered = region(tile, to_inner, to_outer, follow)
    columns, index = gathered[-2:]
    solved0, residual1, whole0, precond1, image1, small, tile, to_inner, to_outer = call(
        functools.partial(middle_kernel, count, corners),
        [((nrhs, corners), F32), wide, wide, wide, wide, ((nrhs, 128), F32), tile_shape, ((nrhs, half + TILE), F32), face],
        *gathered, precond0, image0, residual0, loaded, couple, *coarse_parts,
        flops=flops,
    )
    _, gathered = region(tile, to_inner, to_outer, assemble, maps)
    whole_out = ((1, nrhs, width), F32)
    return tuple(
        call(
            functools.partial(final_kernel, corners),
            [whole_out, whole_out],
            *gathered, precond1, residual1, precond0, whole0, solved0, small,
            columns, index, sign, *coarse_parts,
            flops=flops,
        )
    )


def solution(mesh):
    in_specs = (
        P("grp", None, "blk"),
        P("grp", "blk", None),
        P("grp", "blk", None),
        P("grp", "blk", None),
        P("grp", "blk"),
        P("grp", "blk"),
        P(),
    )
    out_specs = (P("grp", None, "blk"), P("grp", None, "blk"))
    return jax.shard_map(
        functools.partial(local, mesh.shape["blk"], mesh.shape["grp"]),
        mesh=mesh,
        in_specs=in_specs,
        out_specs=out_specs,
        check_vma=False,
    )
```

```python
import functools

import jax
import jax.numpy as jnp
from jax import lax
from jax.experimental import pallas as pl
from jax.experimental.pallas import tpu as pltpu
from jax.sharding import PartitionSpec as P

AXES = ("blk", "grp")
NN = (((1,), (0,)), ((), ()))
NT = (((1,), (1,)), ((), ()))
F32 = jnp.float32
BF16 = jnp.bfloat16


def radices(count):
    found = []
    factor = 2
    while count > 1:
        while count % factor == 0:
            found.append(factor)
            count //= factor
        factor += 1
    return found


def swap(count, groups, partner):
    pairs = []
    for blk in range(count):
        for grp in range(groups):
            other = partner(blk)
            if 0 <= other < count:
                target = other * groups + grp
            elif grp ^ 1 < groups:
                target = blk * groups + (grp ^ 1)
            else:
                target = blk * groups + grp
            pairs.append((blk * groups + grp, target))
    return pairs


def inner_pairs(count, groups):
    return swap(count, groups, lambda blk: blk ^ 1)


def outer_pairs(count, groups):
    return swap(count, groups, lambda blk: blk + 1 if blk % 2 == 1 else blk - 1)


def rotations(count, groups):
    core = 2 if count % 2 == 0 else 1
    chips = count // core
    steps = []

    def pairs_of(target):
        return [
            (blk * groups + grp, target(blk // core, blk % core, grp)) for blk in range(count) for grp in range(groups)
        ]

    def place(chip, lane, grp):
        return (chip * core + lane) * groups + grp

    def turned(value, stride, factor, turn):
        digit = (value // stride) % factor
        return value + ((digit + turn) % factor - digit) * stride

    def along(axis, stride, factor):
        def pairs(turn):
            def target(chip, lane, grp):
                lane = (lane + 1) % core
                if axis == "blk":
                    return place(turned(chip, stride, factor, turn), lane, grp)
                return place(chip, lane, turned(grp, stride, factor, turn))

            return pairs_of(target)

        return [pairs(turn) for turn in range(1, factor)], False

    def both():
        def split_target(chip, lane, grp):
            return place(chip, 1, grp ^ 1) if lane == 0 else place(chip ^ 1, 0, grp)

        def across_target(chip, lane, grp):
            return place(chip ^ 1, lane ^ 1, grp ^ 1)

        return [pairs_of(across_target), pairs_of(split_target)], True

    todo = []
    for axis, size in (("grp", groups), ("blk", chips)):
        stride = 1
        for factor in radices(size):
            todo.append((axis, stride, factor))
            stride *= factor
    first = [("grp", 1, 2), ("blk", 1, 2)]
    if core == 2 and all(step in todo for step in first):
        todo = [step for step in todo if step not in first]
        steps.append(both())
    return steps + [along(*step) for step in todo]


def mm(first, second, dims):
    return lax.dot_general(first, second, dims, preferred_element_type=F32)


def halves(values):
    high = values.astype(BF16)
    return high, (values - high.astype(F32)).astype(BF16)


def stacked(values):
    return jnp.concatenate(halves(values), axis=0)


def folded(rows):
    count = rows.shape[0] // 2
    return rows[:count] + rows[count:]


def dots(first, second):
    first_high, first_low = halves(first)
    high, low = halves(second)
    left = jnp.concatenate([first_high, first_low, first_high], axis=1)
    return mm(left, jnp.concatenate([high, high, low], axis=1), NT)


def against(values, exact):
    return folded(mm(stacked(values), exact, NN))


def lanes_of(shape):
    return lax.broadcasted_iota(jnp.int32, shape, len(shape) - 1)


def chosen(row, corners):
    shape = (corners, row.shape[1])
    return (lax.broadcasted_iota(jnp.int32, shape, 0) == row).astype(BF16)


def live_mask(blk, count, width):
    lane = lanes_of((1, width))
    low = (blk > 0).astype(F32)
    up = (blk < count - 1).astype(F32)
    return jnp.where(lane < width // 2, low, up)


def split(even, low, up):
    return jnp.where(even, up, low), jnp.where(even, low, up)


def joined(even, from_inner, from_outer):
    low = jnp.where(even, from_outer, from_inner)
    up = jnp.where(even, from_inner, from_outer)
    return jnp.concatenate([low, up], axis=1)


def transposed(matrix):
    return matrix.T


def weighted(weights, values):
    top = weights.astype(BF16).astype(F32)
    left = transposed(jnp.concatenate([top, weights - top, top], axis=0)).astype(BF16)
    high, low = halves(values)
    return mm(left, jnp.concatenate([high, high, low], axis=0), NN)


def eliminate(matrix, target, guide):
    count = matrix.shape[1]
    row_index = lax.broadcasted_iota(jnp.int32, (1, count, 1), 1)
    column_index = lax.broadcasted_iota(jnp.int32, (1, count, count), 2)
    diagonal = jnp.where(row_index == column_index, guide, 0.0)
    scale = lax.rsqrt(jnp.sum(diagonal, axis=2, keepdims=True))
    both = scale * lax.rsqrt(jnp.sum(diagonal, axis=1, keepdims=True))
    work = jnp.concatenate([matrix * both, target * scale], axis=2)
    size = 8
    for start in range(0, count, size):
        at = [start + index for index in range(size)]
        columns = [jnp.broadcast_to(work[:, :, k : k + 1], work.shape) for k in at]
        pivot = [[column[:, k : k + 1] for column in columns] for k in at]
        rows = [work[:, k : k + 1] for k in at]
        for one in range(0, size, 2):
            two = one + 1
            a, b, c, d = pivot[one][one], pivot[one][two], pivot[two][one], pivot[two][two]
            inverse = 1.0 / (a * d - b * c)
            for j in range(two + 1, size):
                p, q = pivot[one][j], pivot[two][j]
                pivot[one][j], pivot[two][j] = (d * p - b * q) * inverse, (a * q - c * p) * inverse
            p, q = rows[one], rows[two]
            rows[one], rows[two] = (d * p - b * q) * inverse, (a * q - c * p) * inverse
            for i in range(size):
                if i not in (one, two):
                    left, right = pivot[i][one], pivot[i][two]
                    for j in range(two + 1, size):
                        pivot[i][j] = pivot[i][j] - left * pivot[one][j] - right * pivot[two][j]
                    rows[i] = rows[i] - left * rows[one] - right * rows[two]
        products = [column * row for column, row in zip(columns, rows)]
        while len(products) > 1:
            products = [one + two for one, two in zip(products[::2], products[1::2])]
        work = work - products[0]
        for k, row in zip(at, rows):
            work = jnp.where(row_index == k, row, work)
    return work[:, :, count:] * scale


def symmetric(matrix):
    return 0.5 * (matrix + transposed(matrix))


def corner_values(values, couple):
    half = values.shape[1] // 2
    both = stacked(values)
    low = folded(mm(both[:, :half], couple, NT))
    up = folded(mm(both[:, half:], couple, NT))
    return jnp.where(lanes_of(low.shape) < couple.shape[0] // 2, low, up)


TILE = 128
GROUP = 32
MOST = 32


def abreast(rows):
    half = rows.shape[0] // 2
    return [rows[:half], rows[half:]]


def tiles_of(even, corner, index, first, second, third):
    half = first.shape[0] // 2
    squares = abreast(first) + abreast(second) + abreast(third)
    used = sum(part.shape[1] for part in squares)
    squares = jnp.concatenate(squares + [jnp.zeros((half, TILE - used), F32)], axis=1)
    values = abreast(corner)
    gap = jnp.zeros((half, 2 * corner.shape[1]), F32)
    left, right = jnp.concatenate(values + [gap], axis=1), jnp.concatenate([gap] + values, axis=1)
    row = lax.broadcasted_iota(jnp.int32, (half, index.shape[1]), 0)
    index = jnp.where(row == jnp.where(even, 0, 1), index, 0.0)
    rest = jnp.zeros((half, TILE - left.shape[1] - index.shape[1]), F32)
    return jnp.concatenate(
        [squares, jnp.concatenate([jnp.where(even, left, right), index, rest], axis=1)], axis=0
    )


def untile(tile):
    count = 2 * tile.shape[0]
    return [
        jnp.concatenate([tile[:, at : at + count], tile[:, at + count : at + 2 * count]], axis=0)
        for at in (0, 2 * count, 4 * count)
    ]


def dense(tiles, maps, slots, corners):
    count = tiles.shape[0] // 8
    lane = lanes_of((1, TILE))
    low, up, index = [], [], []

    def moved(rows, at, to):
        shift = (to - at) % TILE
        return pltpu.roll(rows, shift, 1) if shift else rows

    for start in range(0, count, TILE // GROUP // 2):
        parts = [jnp.zeros((8, TILE), F32), jnp.zeros((8, TILE), F32), jnp.full((1, TILE), -1.0, F32)]
        for turn in range(TILE // GROUP):
            at, core = start + turn // 2, turn % 2
            if at < count:
                here = (lane // GROUP == turn) & (lane % GROUP < slots)
                tile = tiles[8 * at : 8 * at + 8]
                name = maps[8 * at + core : 8 * at + core + 1]
                new = [
                    moved(tile, 2 * slots * core, GROUP * turn),
                    moved(tile, 2 * slots * core + slots, GROUP * turn),
                    moved(name, 4 * slots, GROUP * turn),
                ]
                parts = [jnp.where(here, one, old) for one, old in zip(new, parts)]
        low.append(parts[0])
        up.append(parts[1])
        index.append(parts[2])
    values = jnp.concatenate([jnp.concatenate(low, axis=1), jnp.concatenate(up, axis=1)], axis=0)
    choice = chosen(jnp.concatenate(index, axis=1).astype(jnp.int32), corners)
    return folded(mm(stacked(values), choice, NT))


def dense_kernel(slots, corners, tiles, maps, out):
    out[:, :corners] = dense(tiles[8:], maps[8:], slots, corners)
    out[:, corners:] = jnp.concatenate([tiles[:8], jnp.zeros((out.shape[0] - 8, TILE), F32)], axis=0)


def total_of(left, right, maps, slots, corners):
    if right.shape[1] == TILE:
        return left[:, :corners] + dense(right[8:], maps[8:], slots, corners), left[:8, corners:] + right[:8]
    return left[:, :corners] + right[:, :corners], left[:8, corners:] + right[:8, corners:]


def face_rows(rows):
    low = lax.broadcasted_iota(jnp.int32, rows.shape, 0) < rows.shape[0] // 2
    return jnp.concatenate([jnp.where(low, rows, 0.0), jnp.where(low, 0.0, rows)], axis=1)


def both_orders(first, second):
    count = first.shape[0]
    products = dots(jnp.concatenate([first, second], axis=0), jnp.concatenate([second, first], axis=0))
    return 0.5 * (products[:count, :count] + products[count:, count:])


def picked(solved, row):
    return folded(mm(stacked(solved), chosen(row.astype(jnp.int32), solved.shape[1]), NN))


def product_of(first, second):
    high, low = halves(second)
    return folded(mm(stacked(first), high, NN)) + mm(first.astype(BF16), low, NN)


def coarse_solve(corner_sum, parts):
    high, low = parts
    first = folded(mm(stacked(corner_sum), high, NN))
    return first + mm(corner_sum.astype(BF16), low, NN)


def start_kernel(
    count, rhs, signs, blocks, product, to_inner, to_outer, residual_out, sign_out, held, rhs_held, signs_held, sems,
):
    rows = held.shape[1]
    pieces = [(rhs, rhs_held), (signs, signs_held)]
    pieces += [(blocks.at[0, pl.ds(part * rows, rows)], held.at[part]) for part in range(held.shape[0])]
    copies = [pltpu.make_async_copy(*piece, sems.at[index]) for index, piece in enumerate(pieces)]
    for copy in copies:
        copy.start()
    blk = lax.axis_index("blk")
    even = blk % 2 == 0
    nrhs, width = product.shape
    half = width // 2
    live = live_mask(blk, count, width)
    copies[0].wait()
    copies[1].wait()
    sign = signs_held[...].astype(F32) * live
    residual = sign * rhs_held[0]
    rounded = residual.astype(BF16)
    sign_out[...] = sign
    residual_out[...] = residual
    total = jnp.zeros((nrhs, width), F32)
    for part, copy in enumerate(copies[2:]):
        copy.wait()
        total = total + mm(rounded[:, part * rows : (part + 1) * rows], held[part], NN)
    product[...] = total
    inner, outer = split(even, total[:, :half], total[:, half:])
    to_inner[...] = inner
    to_outer[...] = outer


def load_kernel(
    blocks, coupling, corner_map, after, out, couple_out, map_out, inner_extra, outer_extra, coupling_held, map_held, sems
):
    del after
    parts = sems.shape[0] - 2
    rows = out.shape[0] // parts
    pieces = [(corner_map, map_held), (coupling, coupling_held)]
    pieces += [(blocks.at[0, pl.ds(part * rows, rows)], out.at[pl.ds(part * rows, rows)]) for part in range(parts)]
    copies = [pltpu.make_async_copy(*piece, sems.at[index]) for index, piece in enumerate(pieces)]
    for copy in copies:
        copy.start()
    copies[0].wait()
    copies[1].wait()
    even = lax.axis_index("blk") % 2 == 0
    nrhs, half = inner_extra.shape
    couple = coupling_held[0]
    couple_out[...] = couple
    slots = couple.shape[0] // 2
    wide = couple.astype(F32)
    row = jnp.concatenate([map_held[...].astype(F32), jnp.zeros((1, half - 2 * slots), F32)], axis=1)
    map_out[...] = row[:, : map_out.shape[1]]
    fill = jnp.zeros((nrhs - slots - 1, half), F32)
    inner, outer = split(
        even,
        jnp.concatenate([wide[:slots], row, fill], axis=0),
        jnp.concatenate([wide[slots:], pltpu.roll(row, half - slots, 1), fill], axis=0),
    )
    inner_extra[...] = inner
    outer_extra[...] = outer
    for copy in copies[2:]:
        copy.wait()


def first_kernel(
    count, product, from_inner, from_outer, residual, blocks, couple, map_row, inner_extra, outer_extra,
    precond_out, image_out, tile_out, to_inner, to_outer,
):
    blk = lax.axis_index("blk")
    even = blk % 2 == 0
    nrhs, width = product.shape
    half = width // 2
    live = live_mask(blk, count, width)
    precond = live * (product[...] - joined(even, from_inner[...], from_outer[...]))
    image = mm(precond.astype(BF16), blocks[...], NN)
    precond_out[...] = precond
    image_out[...] = image
    first, second = dots(residual[...], precond), dots(precond, image)
    slots = couple.shape[0]
    tile = tiles_of(
        even, corner_values(precond, couple[...]), map_row[:, :slots], first, second, jnp.zeros_like(first)
    )
    tile_out[...] = tile
    inner, outer = split(even, image[:, :half], image[:, half:])
    to_inner[:, :half] = inner
    to_outer[:, :half] = outer
    to_inner[:, half:width] = inner_extra[...]
    to_outer[:, half:] = outer_extra[...]
    to_inner[:, width:] = tile


def prepare_kernel(coarse, high, low):
    top, rest = halves(coarse[...])
    high[...] = top
    low[...] = rest


def follow_kernel(
    count, image, got, from_outer, couple, map_row, blocks,
    part_out, product_out, spread_out, columns_out, map_out, to_inner, to_outer,
):
    blk = lax.axis_index("blk")
    even = blk % 2 == 0
    nrhs, width = image.shape
    half = width // 2
    live = live_mask(blk, count, width)
    inner_got = got[...]
    outer_got = from_outer[...]
    part = live * (image[...] - joined(even, inner_got[:, :half], outer_got[:, :half]))
    beside = joined(even, inner_got[:, half:width], outer_got[:, half:])
    wide = couple[...].astype(F32)
    slots = wide.shape[0] // 2
    other = jnp.concatenate([beside[:slots, :half], beside[:slots, half:]], axis=0)
    columns = (live * jnp.concatenate([face_rows(wide), -face_rows(other)], axis=0)).astype(BF16)
    products = mm(jnp.concatenate([stacked(part), columns], axis=0), blocks[...].reshape(width, width), NN)
    product = products[:nrhs] + products[nrhs : 2 * nrhs]
    spread = products[2 * nrhs :]
    row = jnp.concatenate(
        [
            map_row[:, : 2 * slots],
            beside[slots : slots + 1, :slots],
            beside[slots : slots + 1, half : half + slots],
            jnp.full((1, map_row.shape[1] - 4 * slots), -1.0, F32),
        ],
        axis=1,
    )
    part_out[...] = part
    product_out[...] = product
    spread_out[...] = spread
    columns_out[...] = columns
    map_out[...] = row
    count_rows = nrhs + 4 * slots
    rows = jnp.concatenate([product, spread], axis=0)
    to_inner[:count_rows, :], to_outer[:count_rows, :] = split(even, rows[:, :half], rows[:, half:])
    last = jnp.concatenate([row, jnp.zeros((1, half - row.shape[1]), F32)], axis=1)
    last = jnp.broadcast_to(last, (to_inner.shape[0] - count_rows, half))
    to_inner[count_rows:, :] = last
    to_outer[count_rows:, :] = last


def middle_kernel(
    count, corners, left, right, maps, from_inner, from_outer, part, product, spread, columns, map_row,
    precond_in, image_in, residual_in, blocks, couple, coarse_high, coarse_low,
    solved_out, residual_out, whole_out, precond_out, image_out, small_out, tile_out, to_inner, to_outer,
):
    blk = lax.axis_index("blk")
    even = blk % 2 == 0
    nrhs, width = part.shape
    half = width // 2
    live = live_mask(blk, count, width)
    slots = couple.shape[0]
    corner_sum, squares = total_of(left, right, maps, slots, corners)
    gram, local_energy, _ = untile(squares)
    local_energy = symmetric(local_energy)
    solved = coarse_solve(corner_sum, (coarse_high[...], coarse_low[...]))
    energy = local_energy + both_orders(corner_sum, solved)
    unit = (lax.broadcasted_iota(jnp.int32, (nrhs, nrhs), 0) == lanes_of((nrhs, nrhs))).astype(F32)
    old = symmetric(gram)
    both = eliminate(
        jnp.stack([2.0 * energy, old]), jnp.stack([gram, unit]), jnp.stack([2.0 * local_energy, old])
    )
    alpha, inverse = both[0], both[1]

    rows = spread.shape[0]
    wide = map_row.shape[1]
    inner_got, outer_got = from_inner[...], from_outer[...]
    sides = [jnp.where(even, outer_got, inner_got), jnp.where(even, inner_got, outer_got)]
    index = jnp.concatenate([map_row[...]] + [side[nrhs + rows : nrhs + rows + 1, :wide] for side in sides], axis=1)
    at = picked(solved, index)
    whole = part[...] + against(at[:, :rows], columns[...])
    own = product[...] + product_of(at[:, :rows], spread[...])
    others = [
        side[:nrhs] + product_of(at[:, wide * turn : wide * turn + rows], side[nrhs : nrhs + rows])
        for turn, side in enumerate(sides, 1)
    ]
    change = live * (own - jnp.concatenate(others, axis=1))
    change = weighted(alpha, jnp.concatenate([whole, change], axis=1))
    residual = residual_in[...] - change[:, :width]
    precond = precond_in[...] - change[:, width:]

    image = mm(precond.astype(BF16), blocks[...], NN)
    early = dots(jnp.concatenate([residual, image_in[...]], axis=0), precond)
    late = dots(jnp.concatenate([precond, precond_in[...]], axis=0), image)
    tile = tiles_of(
        even,
        corner_values(precond, couple[...]),
        jnp.zeros((1, slots), F32),
        early[:nrhs],
        late[:nrhs],
        late[nrhs:] + early[nrhs:],
    )
    tile_out[...] = tile
    inner, outer = split(even, image[:, :half], image[:, half:])
    to_inner[:, :half] = inner
    to_inner[:, half:] = tile
    to_outer[...] = outer
    solved_out[...] = solved
    residual_out[...] = residual
    whole_out[...] = whole
    precond_out[...] = precond
    image_out[...] = image
    small_out[...] = jnp.concatenate([inverse, energy, transposed(alpha), jnp.zeros((nrhs, 128 - 3 * nrhs), F32)], axis=1)


def assemble_kernel(count, image, got, from_outer, small, old_precond, part_out, first_out):
    blk = lax.axis_index("blk")
    nrhs, width = image.shape
    image_beside = joined(blk % 2 == 0, got[:, : width // 2], from_outer[...])
    part_out[...] = live_mask(blk, count, width) * (image[...] - image_beside)
    first_out[...] = product_of(small[:, 2 * nrhs : 3 * nrhs], old_precond[...])


def final_kernel(
    corners, left, right, maps, part, first, precond, residual, old_precond, old_image,
    old_solved, small, columns, map_row, sign, coarse_high, coarse_low,
    multipliers_out, residual_out,
):
    nrhs, width = precond.shape
    slots = columns.shape[0] // 2
    corner_sum, squares = total_of(left, right, maps, slots, corners)
    gram, new_new, old_new = untile(squares)
    inverse, old_old = small[:, :nrhs], small[:, nrhs : 2 * nrhs]
    beta = product_of(inverse, gram)
    turned = product_of(transposed(gram), inverse)
    solved = coarse_solve(corner_sum, (coarse_high[...], coarse_low[...]))
    old_new = old_new + product_of(old_old, beta) + 2.0 * dots(old_solved[...], corner_sum)
    energy = symmetric(new_new + product_of(turned, old_new)) + both_orders(corner_sum, solved)
    alpha = eliminate(2.0 * energy[None], gram[None], 2.0 * new_new[None])[0]
    at = picked(solved, map_row[...])
    whole = part[...] + against(at[:, : columns.shape[0]], columns[...])
    carried = product_of(turned, jnp.concatenate([old_precond[...], old_image[...]], axis=1))
    change = weighted(alpha, jnp.concatenate([precond[...], whole], axis=1) + carried)
    multipliers_out[0] = sign[...] * (first[...] + change[:, :width])
    residual_out[0] = sign[...] * (residual[...] - change[:, width:])


VMEM = pl.BlockSpec(memory_space=pltpu.VMEM)
HBM = pl.BlockSpec(memory_space=pltpu.HBM)


def call(body, shapes, *args, specs=None, scratch=(), flops=0):
    shapes = [jax.ShapeDtypeStruct(shape, dtype) for shape, dtype in shapes]
    moved = sum(arg.size * arg.dtype.itemsize for arg in args)
    return pl.pallas_call(
        body,
        out_shape=shapes,
        in_specs=specs or [VMEM] * len(args),
        out_specs=[VMEM] * len(shapes),
        scratch_shapes=list(scratch),
        compiler_params=pltpu.CompilerParams(vmem_limit_bytes=16 << 20),
        cost_estimate=pl.CostEstimate(flops=flops, bytes_accessed=moved, transcendentals=0),
    )(*args)


def local(count, groups, dual_rhs, dual_ops, prec_ops, corner_coupling, corner_map, signs, coarse_inverse):
    nrhs, width = dual_rhs.shape[1:]
    half = width // 2
    corners = coarse_inverse.shape[0]
    inner, outer = inner_pairs(count, groups), outer_pairs(count, groups)
    steps = rotations(count, groups)
    dense_shape = ((nrhs, corners + TILE), F32)
    slots = corner_map.shape[1]
    flops = 2 * nrhs * width * width

    def permute(values, pairs):
        return lax.ppermute(values, AXES, pairs)

    def exchange(to_inner, to_outer):
        from_outer = permute(to_outer, outer)
        return permute(to_inner, inner), from_outer

    def densify(tiles, maps):
        body = functools.partial(dense_kernel, slots, corners)
        return call(body, [dense_shape], tiles, maps, flops=flops)[0]

    def united(parts):
        if parts[0].shape[1] != TILE:
            return sum(parts[1:], parts[0])
        squares = [part[:8] for part in parts]
        return jnp.concatenate([sum(squares[1:], squares[0])] + [part[8:] for part in parts], axis=0)

    def region(tile, to_inner, to_outer, follow, maps=None):
        from_outer = permute(to_outer, outer)
        got = permute(to_inner, inner)
        values = tile + got[:, got.shape[1] - TILE :]
        known = maps
        left, right = None, None
        for index, (turns, relayed) in enumerate(steps):
            if index > 0:
                held = left.shape[0] + right.shape[0] - 16
                if left.shape[1] == TILE and 8 * MOST < 2 * held * (1 + len(turns) + relayed):
                    known = known or (left, right)
                    left, right = densify(left, known[0]), densify(right, known[1])
                values = united([left, right])
            if index == max(len(steps) - (1 if maps else 2), 0):
                result, sends = follow(got, from_outer)
                values, result, sends = lax.optimization_barrier((values, result, sends))
                result = (*(exchange(*sends) if sends else ()), *result)
            left = values
            terms = [permute(values, pairs) for pairs in turns]
            right = united(terms + [permute(terms[-1], inner)] * relayed)
        known = known or (left, right)
        if left.shape[1] == TILE:
            left = densify(left, known[0])
        return known, (left, right, known[1], *result)

    wide = ((nrhs, width), F32)
    face = ((nrhs, half), F32)
    pieces = 8
    in_hbm = functools.partial(pltpu.with_memory_space_constraint, memory_space=pltpu.HBM)
    coupling_shape, map_shape = corner_coupling.shape, corner_map.shape
    product, to_inner, to_outer, residual0, sign, held = call(
        functools.partial(start_kernel, count),
        [wide, face, face, wide, ((1, width), F32), ((pieces, width // pieces, width), BF16)],
        in_hbm(dual_rhs), in_hbm(signs), in_hbm(prec_ops),
        specs=[HBM] * 3,
        scratch=[
            pltpu.VMEM(dual_rhs.shape, F32),
            pltpu.VMEM(signs.shape, jnp.int32),
            pltpu.SemaphoreType.DMA((pieces + 2,)),
        ],
        flops=flops,
    )
    loaded, couple, map_row, *extras = call(
        load_kernel,
        [((width, width), BF16), (coupling_shape[1:], BF16), ((1, 128), F32), face, face],
        in_hbm(dual_ops), in_hbm(corner_coupling), in_hbm(corner_map), sign,
        specs=[HBM] * 3 + [VMEM],
        scratch=[
            pltpu.VMEM(coupling_shape, BF16),
            pltpu.VMEM(map_shape, jnp.int32),
            pltpu.SemaphoreType.DMA((pieces + 2,)),
        ],
    )
    tile_shape = ((nrhs, TILE), F32)
    precond0, image0, tile, to_inner, to_outer = call(
        functools.partial(first_kernel, count),
        [wide, wide, tile_shape, ((nrhs, width + TILE), F32), wide],
        product, *exchange(to_inner, to_outer), residual0, loaded, couple, map_row, *extras,
        flops=flops,
    )
    square = ((corners, corners), BF16)
    coarse_parts = call(prepare_kernel, [square, square], coarse_inverse, flops=corners * corners)
    rows = nrhs + 2 * slots + 8

    def follow(got, from_outer):
        *kept, to_inner, to_outer = call(
            functools.partial(follow_kernel, count),
            [
                wide, wide, ((2 * slots, width), F32), ((2 * slots, width), BF16), ((1, 128), F32),
                ((rows, half), F32), ((rows, half), F32),
            ],
            image0, got, from_outer, couple, map_row, held,
            flops=5 * flops,
        )
        return tuple(kept), (to_inner, to_outer)

    def assemble(got, from_outer):
        body = functools.partial(assemble_kernel, count)
        return tuple(call(body, [wide, wide], image1, got, from_outer, small, precond0, flops=5 * flops)), ()

    maps, gathered = region(tile, to_inner, to_outer, follow)
    columns, index = gathered[-2:]
    solved0, residual1, whole0, precond1, image1, small, tile, to_inner, to_outer = call(
        functools.partial(middle_kernel, count, corners),
        [((nrhs, corners), F32), wide, wide, wide, wide, ((nrhs, 128), F32), tile_shape, ((nrhs, half + TILE), F32), face],
        *gathered, precond0, image0, residual0, loaded, couple, *coarse_parts,
        flops=flops,
    )
    _, gathered = region(tile, to_inner, to_outer, assemble, maps)
    whole_out = ((1, nrhs, width), F32)
    return tuple(
        call(
            functools.partial(final_kernel, corners),
            [whole_out, whole_out],
            *gathered, precond1, residual1, precond0, whole0, solved0, small,
            columns, index, sign, *coarse_parts,
            flops=flops,
        )
    )


def solution(mesh):
    in_specs = (
        P("grp", None, "blk"),
        P("grp", "blk", None),
        P("grp", "blk", None),
        P("grp", "blk", None),
        P("grp", "blk"),
        P("grp", "blk"),
        P(),
    )
    out_specs = (P("grp", None, "blk"), P("grp", None, "blk"))
    return jax.shard_map(
        functools.partial(local, mesh.shape["blk"], mesh.shape["grp"]),
        mesh=mesh,
        in_specs=in_specs,
        out_specs=out_specs,
        check_vma=False,
    )
```
